32 devices in a mesh: dp: 8 (over z, y), tensor: 4 (over x, core).
Axes of the slice: x: 2, y: 2, z: 4, core: 2. Of those that a mesh axis runs over, the one named last changes fastest.
Arguments:
- frames: bfloat16 [31744, 324], P(('dp', 'tensor')), may hold values from -6 to 6
- cotangent: bfloat16 [31744, 324], P(('dp', 'tensor')), may hold values from -6 to 6
- lengths: int32 [64], P('dp'), may hold values from 62 to 496, as said below
- rate_kind: int32 [64], P('dp'), may hold values from 0 to 2
- attn_w: float32 [4, 324, 324], P(None, None, 'tensor')
- attn_m: float32 [4, 324, 324], P(None, None, 'tensor')
- attn_v: float32 [4, 324, 324], P(None, None, 'tensor'), as said below
- ffin_w: float32 [2, 324, 1296], P(None, None, 'tensor')
- ffin_m: float32 [2, 324, 1296], P(None, None, 'tensor')
- ffin_v: float32 [2, 324, 1296], P(None, None, 'tensor'), as said below
- ffout_w: float32 [2, 1296, 324], P(None, 'tensor')
- ffout_m: float32 [2, 1296, 324], P(None, 'tensor')
- ffout_v: float32 [2, 1296, 324], P(None, 'tensor'), as said below
- convin_w: float32 [2, 324, 324], P(None, None, 'tensor')
- convin_m: float32 [2, 324, 324], P(None, None, 'tensor')
- convin_v: float32 [2, 324, 324], P(None, None, 'tensor'), as said below
- convout_w: float32 [324, 324], P('tensor')
- convout_m: float32 [324, 324], P('tensor')
- convout_v: float32 [324, 324], P('tensor'), as said below
- depth_w: float32 [31, 324], replicated
- depth_m: float32 [31, 324], replicated
- depth_v: float32 [31, 324], replicated, as said below
- norm_w: float32 [8, 324], replicated, as said below
- norm_m: float32 [8, 324], replicated
- norm_v: float32 [8, 324], replicated, as said below
- bn_w: float32 [2, 324], replicated, as said below
- bn_m: float32 [2, 324], replicated
- bn_v: float32 [2, 324], replicated, as said below
- table_w: float32 [3, 324], replicated, may hold values from -3 to 3
- table_m: float32 [3, 324], replicated
- table_v: float32 [3, 324], replicated, as said below
Outputs:
- out: bfloat16 [31744, 324], P(('dp', 'tensor'))
- in_grad: float32 [31744, 324], P(('dp', 'tensor'))
- attn_w_new: float32 [4, 324, 324], P(None, None, 'tensor')
- attn_m_new: float32 [4, 324, 324], P(None, None, 'tensor')
- attn_v_new: float32 [3, 324, 324], P(None, None, 'tensor')
- attn_out_v_new: float32 [324, 324], P(None, 'tensor')
- ffin_w_new: float32 [2, 324, 1296], P(None, None, 'tensor')
- ffin_m_new: float32 [2, 324, 1296], P(None, None, 'tensor')
- ffin_v_new: float32 [2, 324, 1296], P(None, None, 'tensor')
- ffout_w_new: float32 [2, 1296, 324], P(None, 'tensor')
- ffout_m_new: float32 [2, 1296, 324], P(None, 'tensor')
- ffout_v_new: float32 [2, 1296, 324], P(None, 'tensor')
- convin_w_new: float32 [2, 324, 324], P(None, None, 'tensor')
- convin_m_new: float32 [2, 324, 324], P(None, None, 'tensor')
- convin_v_new: float32 [2, 324, 324], P(None, None, 'tensor')
- convout_w_new: float32 [324, 324], P('tensor')
- convout_m_new: float32 [324, 324], P('tensor')
- convout_v_new: float32 [324, 324], P('tensor')
- depth_w_new: float32 [31, 324], replicated
- depth_m_new: float32 [31, 324], replicated
- depth_v_new: float32 [31, 324], replicated
- norm_w_new: float32 [8, 324], replicated
- norm_m_new: float32 [8, 324], replicated
- norm_v_new: float32 [8, 324], replicated
- bn_w_new: float32 [2, 324], replicated
- bn_m_new: float32 [2, 324], replicated
- bn_v_new: float32 [2, 324], replicated
- table_w_new: float32 [3, 324], replicated
- table_m_new: float32 [3, 324], replicated
- table_v_new: float32 [3, 324], replicated
- weight_norms: float32 [12], replicated
- update_norms: float32 [12], replicated
The draws below stay inside these ranges and needn't reach their ends.
Inputs may be any that keep to these rules, and one draw needn't show every extreme that they name: `lengths`: valid frames of each utterance, counted from its start. `attn_v`: positive entries. `ffin_v`: positive entries. `ffout_v`: positive entries. `convin_v`: positive entries. `convout_v`: positive entries. `depth_v`: positive entries. `norm_v`: positive entries. `bn_v`: positive entries. `table_v`: positive entries. `norm_w`: gains (rows 0 to 3) are positive. `bn_w`: the gain (row 0) is positive.
All inputs are finite; a program needn't handle non-finite values.
Results may differ from the reference program's by a relative error of at most 0.03.
The reference program's roundings to bfloat16 on the way (of `attn_low`, `queries`, `prob_low`, `mixed_low`, `hidden_low` and `act_low`) count: a program that leaves them out, or rounds other values in their place, can miss the bound.
Values may be sent and summed in bfloat16 or wider, within the bound.
No kernel may reach another device: no remote copies, remote signals or barrier semaphores. Data moves between devices by JAX's collectives and lax.ppermute only.
A program may use at most 192 MiB of HBM per device.

```python
import math
import jax
import jax.numpy as jnp
from jax import lax

D = 324
HEADS = 4
FF = 1296
KERNEL = 31
RATES = 3
STEP = 10
SLOT = 496
HD = 81
UTTS = 64
FRAMES = 31744


def rising(array_shape, grow_dim, rise_ratio):
    extent = array_shape[grow_dim]
    position = jnp.arange(extent, dtype=jnp.float32) / max(extent - 1, 1)
    view_shape = [1] * len(array_shape)
    view_shape[grow_dim] = extent
    return (1.0 + (rise_ratio - 1.0) * position).reshape(view_shape)


def mixed_noise(sub_key, array_shape):
    gauss_key = jax.random.fold_in(sub_key, 0)
    gaussian = jax.random.normal(gauss_key, array_shape, jnp.float32)
    return gaussian


def master_draw(sub_key, array_shape, grow_dim, spread_scale, rise_ratio):
    return mixed_noise(sub_key, array_shape) * spread_scale * jnp.sqrt(rising(array_shape, grow_dim, rise_ratio))


def moment_draw(sub_key, array_shape, grad_size):
    return mixed_noise(sub_key, array_shape) * (0.11 * grad_size)


def square_draw(sub_key, array_shape, grow_dim, grad_size, rise_ratio):
    spread_key, level_key = jax.random.split(sub_key)
    spread_part = jax.random.uniform(spread_key, array_shape, jnp.float32, 0.5, 2.0)
    if grow_dim >= 0:
        level_part = rising(array_shape, grow_dim, rise_ratio)
    else:
        level_part = jax.random.uniform(level_key, array_shape, jnp.float32, 1.0, 4.0)
    return 0.001001 * grad_size * grad_size * level_part * spread_part


def out_boost():
    return math.sqrt(SLOT / 5.0)


def matrix_size():
    return 0.6 * math.sqrt(0.5 * FRAMES)


def vector_size():
    return math.sqrt(0.5 * FRAMES)


def attn_size():
    return jnp.array([1.0, 1.0, 1.0, 1.0 / out_boost()], jnp.float32).reshape(4, 1, 1) * matrix_size()


def draw_lengths(key, part):
    key = jax.random.fold_in(key, 1)
    draw_key, high_key, low_key = jax.random.split(key, 3)
    position = jnp.arange(UTTS, dtype=jnp.int32)
    floor_len = SLOT // 8 + SLOT // 2 * position // UTTS
    ceiling = jnp.minimum(floor_len + SLOT // 3 + 1, SLOT + 1)
    drawn = jax.random.randint(draw_key, (UTTS,), floor_len, ceiling)
    pick_high = jax.random.randint(high_key, (), UTTS // 2, UTTS)
    pick_low = jax.random.randint(low_key, (), 0, max(1, UTTS // 4))
    drawn = jnp.where(position == pick_low, SLOT // 8, drawn)
    drawn = jnp.where(position == pick_high, SLOT, drawn)
    return drawn.astype(jnp.int32)


def draw_attn_w(key, part):
    key = jax.random.fold_in(key, 11)
    boost = jnp.array([1.0, 1.0, 1.0, out_boost()], jnp.float32).reshape(4, 1, 1)
    return master_draw(key, (4, D, D), 2, D ** (-0.5), 3.0) * boost


def draw_attn_m(key, part):
    key = jax.random.fold_in(key, 12)
    return moment_draw(key, (4, D, D), attn_size())


def draw_attn_v(key, part):
    key = jax.random.fold_in(key, 13)
    return square_draw(key, (4, D, D), 2, attn_size(), 4.0)


def draw_ffin_w(key, part):
    key = jax.random.fold_in(key, 21)
    return master_draw(key, (2, D, FF), 2, D ** (-0.5), 3.0)


def draw_ffin_m(key, part):
    key = jax.random.fold_in(key, 22)
    return moment_draw(key, (2, D, FF), matrix_size())


def draw_ffin_v(key, part):
    key = jax.random.fold_in(key, 23)
    return square_draw(key, (2, D, FF), 2, matrix_size(), 4.0)


def draw_ffout_w(key, part):
    key = jax.random.fold_in(key, 31)
    return master_draw(key, (2, FF, D), 1, FF ** (-0.5), 3.0)


def draw_ffout_m(key, part):
    key = jax.random.fold_in(key, 32)
    return moment_draw(key, (2, FF, D), matrix_size())


def draw_ffout_v(key, part):
    key = jax.random.fold_in(key, 33)
    return square_draw(key, (2, FF, D), 1, matrix_size(), 4.0)


def draw_convin_w(key, part):
    key = jax.random.fold_in(key, 41)
    return master_draw(key, (2, D, D), 2, D ** (-0.5), 3.0)


def draw_convin_m(key, part):
    key = jax.random.fold_in(key, 42)
    return moment_draw(key, (2, D, D), matrix_size())


def draw_convin_v(key, part):
    key = jax.random.fold_in(key, 43)
    return square_draw(key, (2, D, D), 2, matrix_size(), 4.0)


def draw_convout_w(key, part):
    key = jax.random.fold_in(key, 51)
    return master_draw(key, (D, D), 0, D ** (-0.5), 3.0)


def draw_convout_m(key, part):
    key = jax.random.fold_in(key, 52)
    return moment_draw(key, (D, D), matrix_size())


def draw_convout_v(key, part):
    key = jax.random.fold_in(key, 53)
    return square_draw(key, (D, D), 0, matrix_size(), 4.0)


def draw_depth_w(key, part):
    key = jax.random.fold_in(key, 61)
    return master_draw(key, (KERNEL, D), 1, KERNEL ** (-0.5), 3.0)


def draw_depth_m(key, part):
    key = jax.random.fold_in(key, 62)
    return moment_draw(key, (KERNEL, D), matrix_size())


def draw_depth_v(key, part):
    key = jax.random.fold_in(key, 63)
    return square_draw(key, (KERNEL, D), 1, matrix_size(), 4.0)


def draw_norm_w(key, part):
    key = jax.random.fold_in(key, 71)
    gain_key, shift_key = jax.random.split(key)
    gains = jax.random.uniform(gain_key, (4, D), jnp.float32, 0.6, 1.4)
    shifts = mixed_noise(shift_key, (4, D)) * 0.3
    return jnp.concatenate([gains, shifts], axis=0)


def draw_norm_m(key, part):
    key = jax.random.fold_in(key, 72)
    return moment_draw(key, (8, D), vector_size())


def draw_norm_v(key, part):
    key = jax.random.fold_in(key, 73)
    return square_draw(key, (8, D), -1, vector_size(), 1.0)


def draw_bn_w(key, part):
    key = jax.random.fold_in(key, 81)
    gain_key, shift_key = jax.random.split(key)
    gains = jax.random.uniform(gain_key, (1, D), jnp.float32, 0.6, 1.4)
    shifts = mixed_noise(shift_key, (1, D)) * 0.3
    return jnp.concatenate([gains, shifts], axis=0)


def draw_bn_m(key, part):
    key = jax.random.fold_in(key, 82)
    return moment_draw(key, (2, D), vector_size())


def draw_bn_v(key, part):
    key = jax.random.fold_in(key, 83)
    return square_draw(key, (2, D), -1, vector_size(), 1.0)


def draw_table_m(key, part):
    key = jax.random.fold_in(key, 92)
    return moment_draw(key, (RATES, D), vector_size() / math.sqrt(RATES))


def draw_table_v(key, part):
    key = jax.random.fold_in(key, 93)
    return square_draw(key, (RATES, D), -1, vector_size() / math.sqrt(RATES), 1.0)


def place_ends(entries, rng, least, largest):
    spot = [jax.random.randint(jax.random.fold_in(rng, axis), (), 0, length) for axis, length in enumerate(entries.shape)]
    main_axis = entries.shape.index(max(entries.shape))
    neighbour = spot[:main_axis] + [(spot[main_axis] + 1) % entries.shape[main_axis]] + spot[main_axis + 1:]
    return entries.at[tuple(spot)].set(least).at[tuple(neighbour)].set(largest)


def block_scale(key, dims, cuts, low, high):
    def one(axis_at, blocks):
        heights = jax.random.uniform(jax.random.fold_in(jax.random.fold_in(key, 6), axis_at), (blocks,), jnp.float32, low / len(cuts), high / len(cuts))
        return jnp.repeat(jnp.exp(heights), dims[axis_at] // blocks).reshape((-1,) + (1,) * (len(dims) - axis_at - 1))

    level = one(*cuts[0])
    for cut in cuts[1:]:
        level = level * one(*cut)
    return level


def centred(stream_key, shape, scale, most, cuts=(), kind=jnp.bfloat16):
    gain = block_scale(stream_key, shape, cuts, -0.22, 0.18) if cuts else 1.0
    values = jax.random.normal(stream_key, shape, jnp.float32) * scale * gain
    return jnp.minimum(jnp.maximum(values, -most), most).astype(kind)


def setup_inputs(seed: int = 0) -> dict:
    key_of = jax.random.split(jax.random.key(seed), 32)
    return {
        "frames": centred(key_of[0], (FRAMES, D), 1.0, 6.0, ((0, 32),)),
        "cotangent": centred(key_of[1], (FRAMES, D), 1.0, 6.0, ((0, 32),)),
        "lengths": draw_lengths(jax.random.fold_in(key_of[31], 71), 0),
        "rate_kind": place_ends(jax.random.randint(key_of[3], (UTTS,), 0, RATES), jax.random.fold_in(key_of[3], 1), 0, RATES - 1).astype(jnp.int32),
        "attn_w": draw_attn_w(jax.random.fold_in(key_of[31], 71), 0),
        "attn_m": draw_attn_m(jax.random.fold_in(key_of[31], 71), 0),
        "attn_v": draw_attn_v(jax.random.fold_in(key_of[31], 71), 0),
        "ffin_w": draw_ffin_w(jax.random.fold_in(key_of[31], 71), 0),
        "ffin_m": draw_ffin_m(jax.random.fold_in(key_of[31], 71), 0),
        "ffin_v": draw_ffin_v(jax.random.fold_in(key_of[31], 71), 0),
        "ffout_w": draw_ffout_w(jax.random.fold_in(key_of[31], 71), 0),
        "ffout_m": draw_ffout_m(jax.random.fold_in(key_of[31], 71), 0),
        "ffout_v": draw_ffout_v(jax.random.fold_in(key_of[31], 71), 0),
        "convin_w": draw_convin_w(jax.random.fold_in(key_of[31], 71), 0),
        "convin_m": draw_convin_m(jax.random.fold_in(key_of[31], 71), 0),
        "convin_v": draw_convin_v(jax.random.fold_in(key_of[31], 71), 0),
        "convout_w": draw_convout_w(jax.random.fold_in(key_of[31], 71), 0),
        "convout_m": draw_convout_m(jax.random.fold_in(key_of[31], 71), 0),
        "convout_v": draw_convout_v(jax.random.fold_in(key_of[31], 71), 0),
        "depth_w": draw_depth_w(jax.random.fold_in(key_of[31], 71), 0),
        "depth_m": draw_depth_m(jax.random.fold_in(key_of[31], 71), 0),
        "depth_v": draw_depth_v(jax.random.fold_in(key_of[31], 71), 0),
        "norm_w": draw_norm_w(jax.random.fold_in(key_of[31], 71), 0),
        "norm_m": draw_norm_m(jax.random.fold_in(key_of[31], 71), 0),
        "norm_v": draw_norm_v(jax.random.fold_in(key_of[31], 71), 0),
        "bn_w": draw_bn_w(jax.random.fold_in(key_of[31], 71), 0),
        "bn_m": draw_bn_m(jax.random.fold_in(key_of[31], 71), 0),
        "bn_v": draw_bn_v(jax.random.fold_in(key_of[31], 71), 0),
        "table_w": centred(key_of[28], (RATES, D), 0.5, 3.0, (), jnp.float32),
        "table_m": draw_table_m(jax.random.fold_in(key_of[31], 71), 0),
        "table_v": draw_table_v(jax.random.fold_in(key_of[31], 71), 0),
    }


PRECISE = lax.Precision.HIGHEST
EPS_NORM = 1e-05
BETA_ONE = 0.9
BETA_TWO = 0.999
ADAM_EPS = 1e-06
WEIGHT_DECAY = 0.01
RATE_MATRIX = 0.3
RATE_VECTOR = 0.5
MASK_FILL = -1e+30

@jax.custom_vjp
def low(v):
    return lax.optimization_barrier(v.astype(jnp.bfloat16)).astype(jnp.float32)

@jax.custom_vjp
def low_back(v):
    return v

def low_keep(v):
    return (low(v), None)

def low_pass(kept, grad):
    return (grad,)

def back_keep(v):
    return (v, None)

def back_low(kept, grad):
    return (low(grad),)
low.defvjp(low_keep, low_pass)
low_back.defvjp(back_keep, back_low)

def exact_dot(left_side, right_side):
    return jnp.dot(left_side, right_side, precision=PRECISE)

def layer_norm(resid, gain_row, shift_row):
    center = resid - lax.optimization_barrier(jnp.mean(resid, axis=-1, keepdims=True))
    spread = lax.optimization_barrier(jnp.mean(center * center, axis=-1, keepdims=True))
    return center * lax.rsqrt(spread + EPS_NORM) * gain_row + shift_row

def depthwise(signal, kernel):
    half_width = KERNEL // 2
    padded = jnp.pad(signal, ((0, 0), (half_width, half_width), (0, 0)))
    total = jnp.zeros(signal.shape, jnp.float32)
    for offset in range(KERNEL):
        total = total + padded[:, offset:offset + SLOT, :] * kernel[offset]
    return total

def feed_forward(inputs, weight_in, weight_out):
    hidden_pre = low_back(exact_dot(low(inputs), weight_in))
    hidden_low = low(jax.nn.silu(hidden_pre))
    return low_back(exact_dot(hidden_low, weight_out))

def attend_group(queries, key_rows, value_rows, group_lengths):
    batch_size = queries.shape[0]
    query_heads = queries.reshape(batch_size, SLOT, HEADS, HD)
    key_heads = key_rows.reshape(batch_size, SLOT, HEADS, HD)
    value_heads = value_rows.reshape(batch_size, SLOT, HEADS, HD)
    raw_scores = jnp.einsum('bqhe,bkhe->bhqk', query_heads, key_heads, precision=PRECISE) * (1.0 / math.sqrt(HD))
    scores = low_back(raw_scores)
    key_valid = jnp.arange(SLOT)[None, :] < group_lengths[:, None]
    scores = jnp.where(key_valid[:, None, None, :], scores, MASK_FILL)
    score_top = lax.optimization_barrier(jnp.max(scores, axis=-1, keepdims=True))
    exponent = jnp.exp(scores - score_top)
    prob_low = low(exponent / lax.optimization_barrier(jnp.sum(exponent, axis=-1, keepdims=True)))
    mixed = jnp.einsum('bhqk,bkhe->bqhe', prob_low, value_heads, precision=PRECISE)
    return low_back(low(mixed.reshape(batch_size, SLOT, D)))

def layer_forward(inputs, params, lengths, onehot, frame_mask):
    attn_w, ffin_w, ffout_w, convin_w, convout_w, depth_w, norm_w, bn_w, table_w = params
    attn_low = low(attn_w)
    ffin_low = low(ffin_w)
    ffout_low = low(ffout_w)
    convin_low = low(convin_w)
    convout_low = low(convout_w)
    base_rows = (inputs.reshape(UTTS, SLOT, D) + exact_dot(onehot, table_w)[:, None, :]).reshape(FRAMES, D)
    base_low = low(base_rows)
    queries = low_back(low(exact_dot(base_low, attn_low[0])))
    key_rows = low_back(low(exact_dot(base_low, attn_low[1])))
    value_rows = low_back(low(exact_dot(base_low, attn_low[2])))
    group_size = math.gcd(UTTS, max(1, 4096 // SLOT))
    block_count = UTTS // group_size

    def one_block(pieces):
        return jax.checkpoint(attend_group)(*pieces)
    mixed_low = lax.map(one_block, (queries.reshape(block_count, group_size, SLOT, D), key_rows.reshape(block_count, group_size, SLOT, D), value_rows.reshape(block_count, group_size, SLOT, D), lengths.reshape(block_count, group_size)))
    attn_out = low_back(exact_dot(mixed_low.reshape(FRAMES, D), attn_low[3]))
    first_out = layer_norm(base_rows + attn_out, norm_w[0], norm_w[4])
    second = layer_norm(first_out + feed_forward(first_out, ffin_low[0], ffout_low[0]), norm_w[1], norm_w[5])
    second_low = low(second)
    value_pre = low_back(exact_dot(second_low, convin_low[0]))
    gate_pre = low_back(exact_dot(second_low, convin_low[1]))
    weight_col = frame_mask.reshape(FRAMES, 1)
    glu_out = value_pre * jax.nn.sigmoid(gate_pre) * weight_col
    conv_out = depthwise(glu_out.reshape(UTTS, SLOT, D), depth_w).reshape(FRAMES, D)
    valid_count = jnp.sum(frame_mask)
    bn_mean = lax.optimization_barrier(jnp.sum(conv_out * weight_col, axis=0)) / valid_count
    center = conv_out - bn_mean
    bn_var = lax.optimization_barrier(jnp.sum(center * center * weight_col, axis=0)) / valid_count
    bn_out = center * lax.rsqrt(bn_var + EPS_NORM) * bn_w[0] + bn_w[1]
    act_low = low(jax.nn.silu(bn_out))
    conv_branch = low_back(exact_dot(act_low, convout_low))
    third_out = layer_norm(second + conv_branch, norm_w[2], norm_w[6])
    return layer_norm(third_out + feed_forward(third_out, ffin_low[1], ffout_low[1]), norm_w[3], norm_w[7])

def adam_step(weight, first, second, grad):
    first_new = BETA_ONE * first + (1.0 - BETA_ONE) * grad
    second_new = BETA_TWO * second + (1.0 - BETA_TWO) * grad * grad
    direction = first_new / (1.0 - BETA_ONE ** STEP) / (jnp.sqrt(second_new / (1.0 - BETA_TWO ** STEP)) + ADAM_EPS)
    return (first_new, second_new, direction)

def lamb_matrix(weight, first, second, grad):
    first_new, second_new, direction = adam_step(weight, first, second, grad)
    direction = direction + WEIGHT_DECAY * weight
    weight_norm = jnp.sqrt(jnp.sum(weight * weight))
    update_norm = jnp.sqrt(jnp.sum(direction * direction))
    return (weight - RATE_MATRIX * (weight_norm / update_norm) * direction, first_new, second_new, weight_norm, update_norm)

def lamb_stack(weight, first, second, grad):
    return jax.vmap(lamb_matrix)(weight, first, second, grad)

def adam_vector(weight, first, second, grad):
    first_new, second_new, direction = adam_step(weight, first, second, grad)
    return (weight - RATE_VECTOR * direction, first_new, second_new)

def reference(frames, cotangent, lengths, rate_kind, attn_w, attn_m, attn_v, ffin_w, ffin_m, ffin_v, ffout_w, ffout_m, ffout_v, convin_w, convin_m, convin_v, convout_w, convout_m, convout_v, depth_w, depth_m, depth_v, norm_w, norm_m, norm_v, bn_w, bn_m, bn_v, table_w, table_m, table_v):
    frame_mask = (jnp.arange(SLOT)[None, :] < lengths[:, None]).astype(jnp.float32)
    onehot = (rate_kind[:, None] == jnp.arange(RATES)[None, :]).astype(jnp.float32)
    params = (attn_w, ffin_w, ffout_w, convin_w, convout_w, depth_w, norm_w, bn_w, table_w)

    def closed(inputs, weights):
        return layer_forward(inputs, weights, lengths, onehot, frame_mask)
    fourth, pull = jax.vjp(closed, frames.astype(jnp.float32), params)
    seed_grad = cotangent.astype(jnp.float32) * frame_mask.reshape(FRAMES, 1)
    in_grad, grads = pull(seed_grad)
    attn_g, ffin_g, ffout_g, convin_g, convout_g, depth_g, norm_g, bn_g, table_g = grads
    attn_new = lamb_stack(attn_w, attn_m, attn_v, attn_g)
    ffin_new = lamb_stack(ffin_w, ffin_m, ffin_v, ffin_g)
    ffout_new = lamb_stack(ffout_w, ffout_m, ffout_v, ffout_g)
    convin_new = lamb_stack(convin_w, convin_m, convin_v, convin_g)
    convout_new = lamb_matrix(convout_w, convout_m, convout_v, convout_g)
    depth_new = lamb_matrix(depth_w, depth_m, depth_v, depth_g)
    norm_new = adam_vector(norm_w, norm_m, norm_v, norm_g)
    bn_new = adam_vector(bn_w, bn_m, bn_v, bn_g)
    table_new = adam_vector(table_w, table_m, table_v, table_g)
    weight_norms = jnp.concatenate([attn_new[3], ffin_new[3], ffout_new[3], convin_new[3], convout_new[3][None], depth_new[3][None]])
    update_norms = jnp.concatenate([attn_new[4], ffin_new[4], ffout_new[4], convin_new[4], convout_new[4][None], depth_new[4][None]])
    return (fourth.astype(jnp.bfloat16), in_grad, attn_new[0], attn_new[1], attn_new[2][:3], attn_new[2][3], ffin_new[0], ffin_new[1], ffin_new[2], ffout_new[0], ffout_new[1], ffout_new[2], convin_new[0], convin_new[1], convin_new[2], convout_new[0], convout_new[1], convout_new[2], depth_new[0], depth_new[1], depth_new[2], norm_new[0], norm_new[1], norm_new[2], bn_new[0], bn_new[1], bn_new[2], table_new[0], table_new[1], table_new[2], weight_norms, update_norms)
```

```python
import functools
import math

import jax
import jax.numpy as jnp
import numpy as np
from jax import lax
from jax.experimental import pallas as pl
from jax.experimental.pallas import tpu as pltpu
from jax.sharding import PartitionSpec as P

D = 324
HEADS = 4
KERNEL = 31
HALF = KERNEL // 2
RATES = 3
STEP = 10
SLOT = 496
HD = 81
PAD = 96
WIDE = HEADS * PAD

EPS_NORM = 1e-05
BETA_ONE = 0.9
BETA_TWO = 0.999
ADAM_EPS = 1e-06
WEIGHT_DECAY = 0.01
RATE_MATRIX = 0.3
RATE_VECTOR = 0.5
MASK_FILL = -1e30
SCALE = 1.0 / math.sqrt(HD)
PRECISE = lax.Precision.HIGHEST

F32 = jnp.float32
BF16 = jnp.bfloat16
VMEM_LIMIT = 56 * 1024 * 1024
LEAD = 16
SPAN = 544


def dot_nn(left, right):
    return lax.dot_general(left, right, (((1,), (0,)), ((), ())), preferred_element_type=F32)


def dot_nt(left, right):
    return lax.dot_general(left, right, (((1,), (1,)), ((), ())), preferred_element_type=F32)


def dot_tn(left, right):
    return lax.dot_general(left, right, (((0,), (0,)), ((), ())), preferred_element_type=F32)


def sigmoid(value):
    return 0.5 * jnp.tanh(0.5 * value) + 0.5


def ln_forward(resid):
    center = resid - jnp.mean(resid, axis=-1, keepdims=True)
    inv = lax.rsqrt(jnp.mean(center * center, axis=-1, keepdims=True) + EPS_NORM)
    return center * inv, inv


def ln_backward(upstream, normal, inv, gain):
    scaled = upstream * gain
    grad = inv * (
        scaled
        - jnp.mean(scaled, axis=-1, keepdims=True)
        - normal * jnp.mean(scaled * normal, axis=-1, keepdims=True)
    )
    gain_sum = jnp.sum(upstream * normal, axis=0, keepdims=True)
    shift_sum = jnp.sum(upstream, axis=0, keepdims=True)
    return grad, gain_sum, shift_sum


def put_sums(ref, first, gain_sum, shift_sum):
    @pl.when(first)
    def _():
        ref[...] = jnp.zeros_like(ref)

    ref[0:1, :] += gain_sum
    ref[1:2, :] += shift_sum


def attn_fwd_kernel(
    rank_ref, len_ref, kind_ref, frames, table, weights, pick, norm,
    qkv_out, mixed_out, lse_out, n1_out, s1_out, wout_out,
):
    utt = pl.program_id(0)
    rank = rank_ref[0]

    @pl.when(utt == 0)
    def _():
        turned = jnp.concatenate([weights[t ^ rank, 3] for t in range(HEADS)], axis=0)
        spaced = dot_nt(pick[...], turned).astype(BF16)
        wout_out[...] = dot_nn(spaced, pick[...]).astype(BF16)

    base = frames[...].astype(F32) + table[pl.ds(kind_ref[utt], 1), :]
    base_low = base.astype(BF16)
    valid = lax.broadcasted_iota(jnp.int32, (SLOT, 1), 0) < len_ref[utt]
    for head in range(HEADS):
        w_head = weights[head ^ rank, 0:3].reshape(3 * PAD, D)
        qkv = dot_nt(w_head, base_low).astype(BF16)
        qkv_out[head] = qkv
        queries, keys, values = qkv[:PAD], qkv[PAD : 2 * PAD], qkv[2 * PAD :]
        scores = jnp.where(valid, dot_tn(keys, queries) * SCALE, MASK_FILL)
        top = jnp.max(scores, axis=0, keepdims=True)
        expo = jnp.exp(scores - top)
        total = jnp.sum(expo, axis=0, keepdims=True)
        probs = (expo * (1.0 / total)).astype(BF16)
        lse_out[head] = top + jnp.log(total)
        mixed_out[head * PAD : (head + 1) * PAD, :] = dot_nn(values, probs).astype(BF16)
    attn_out = dot_tn(mixed_out[...], wout_out[...])
    normal, inv = ln_forward(base + attn_out)
    n1_out[...] = normal
    s1_out[...] = inv


def ffn_fwd_kernel(
    last_layer, n_in, norm_in, norm_out, w_in, w_out, *rest,
):
    if last_layer:
        cot, weight, hid_out, slope_out, out_ref, grad_ref, sums_ref, acc, z_low = rest
    else:
        hid_out, slope_out, n_ref, s_ref, acc, z_low = rest
    step = pl.program_id(0)

    @pl.when(step == 0)
    def _():
        z = n_in[...] * norm_in[0:1, :] + norm_in[1:2, :]
        acc[...] = z
        z_low[...] = z.astype(BF16)

    pre = dot_nn(z_low[...], w_in[0])
    sig = sigmoid(pre)
    hidden = pre * sig
    hid_low = hidden.astype(BF16)
    hid_out[0] = hid_low
    slope_out[0] = (sig + hidden * (1.0 - sig)).astype(BF16)
    acc[...] += dot_nn(hid_low, w_out[0])

    @pl.when(step == pl.num_programs(0) - 1)
    def _():
        normal, inv = ln_forward(acc[...])
        if last_layer:
            gain = norm_out[0:1, :]
            out_ref[...] = (normal * gain + norm_out[1:2, :]).astype(BF16)
            upstream = cot[...].astype(F32) * weight[...]
            grad, gain_sum, shift_sum = ln_backward(upstream, normal, inv, gain)
            grad_ref[...] = grad
            sums_ref[...] = jnp.zeros_like(sums_ref)
            sums_ref[0:1, :] = gain_sum
            sums_ref[1:2, :] = shift_sum
        else:
            n_ref[...] = normal
            s_ref[...] = inv


def ffn_bwd_kernel(
    up, n_in, s_in, norm_in, w_in, w_out, hid, slope,
    win_out, wout_out, grad_ref, sums_ref, acc, up_low, up_turn, z_turn,
):
    step = pl.program_id(0)

    @pl.when(step == 0)
    def _():
        upstream = up[...]
        acc[...] = upstream
        low = upstream.astype(BF16)
        up_low[...] = low
        up_turn[...] = low.T
        z = n_in[...] * norm_in[0:1, :] + norm_in[1:2, :]
        z_turn[...] = z.astype(BF16).T

    pre_grad = (dot_nt(up_low[...], w_out[0]) * slope[0].astype(F32)).astype(BF16)
    wout_out[0] = dot_nn(up_turn[...], hid[0]).astype(BF16)
    win_out[0] = dot_nn(z_turn[...], pre_grad).astype(BF16)
    acc[...] += dot_nt(pre_grad, w_in[0])

    @pl.when(step == pl.num_programs(0) - 1)
    def _():
        grad, gain_sum, shift_sum = ln_backward(acc[...], n_in[...], s_in[...], norm_in[0:1, :])
        grad_ref[...] = grad
        sums_ref[...] = jnp.zeros_like(sums_ref)
        sums_ref[0:1, :] = gain_sum
        sums_ref[1:2, :] = shift_sum


def shifted(scratch):
    for shift in range(1, 8):
        scratch[shift, 0 : SPAN - 8, :] = scratch[0, pl.ds(shift, SPAN - 8), :]


def load_padded(scratch, signal):
    scratch[0, 0:LEAD, :] = jnp.zeros((LEAD, WIDE), F32)
    scratch[0, pl.ds(LEAD + SLOT, SPAN - LEAD - SLOT), :] = jnp.zeros((SPAN - LEAD - SLOT, WIDE), F32)
    scratch[0, pl.ds(LEAD, SLOT), :] = signal
    shifted(scratch)


ROWS_AT_ONCE = SLOT // 2
LANES = 128


def depth_loop(body_fn):
    for half in range(SLOT // ROWS_AT_ONCE):
        for tile in range(WIDE // LANES):
            body_fn(half * ROWS_AT_ONCE, slice(tile * LANES, (tile + 1) * LANES))


def conv_fwd_kernel(
    rank_ref, len_ref, n_in, norm_in, weights, taps,
    value_out, sig_out, conv_out, stat_out, padded,
):
    utt = pl.program_id(0)
    rank = rank_ref[0]
    z_low = (n_in[...] * norm_in[0:1, :] + norm_in[1:2, :]).astype(BF16)
    w_value = jnp.concatenate([weights[t ^ rank, 0] for t in range(HEADS)], axis=0)
    w_gate = jnp.concatenate([weights[t ^ rank, 1] for t in range(HEADS)], axis=0)
    value = dot_nt(z_low, w_value)
    sig = sigmoid(dot_nt(z_low, w_gate))
    value_out[...] = value
    sig_out[...] = sig
    count = len_ref[utt]
    valid = (lax.broadcasted_iota(jnp.int32, (SLOT, 1), 0) < count).astype(F32)
    load_padded(padded, value * sig * valid)

    def block(row, lanes):
        total = jnp.zeros((ROWS_AT_ONCE, LANES), F32)
        for tap in range(KERNEL):
            place = tap + 1
            rows = pl.ds(row + place // 8 * 8, ROWS_AT_ONCE)
            total = total + padded[place % 8, rows, lanes] * taps[tap : tap + 1, lanes]
        conv_out[pl.ds(row, ROWS_AT_ONCE), lanes] = total

    depth_loop(block)
    conv = conv_out[...]
    number = count.astype(F32)
    mean = jnp.sum(conv * valid, axis=0, keepdims=True) / number
    center = (conv - mean) * valid
    stat_out[...] = jnp.zeros_like(stat_out)
    stat_out[0:1, :] = mean
    stat_out[1:2, :] = jnp.sum(center * center, axis=0, keepdims=True)
    stat_out[2:3, :] = jnp.zeros_like(mean) + number


def mid_fwd_kernel(conv, stats, bn, n_in, norm_in, weights, act_out, n_ref, s_ref):
    normal = (conv[...] - stats[0:1, :]) * stats[1:2, :]
    out = normal * bn[0:1, :] + bn[1:2, :]
    act = (out * sigmoid(out)).astype(BF16)
    act_out[...] = act
    second = n_in[...] * norm_in[0:1, :] + norm_in[1:2, :]
    normal, inv = ln_forward(second + dot_nn(act, weights[...]))
    n_ref[...] = normal
    s_ref[...] = inv


def mid_bwd_kernel(rank_ref, conv, stats, bn, act, grad, weights, b_out, wgrad_out, sums_ref, acc):
    utt = pl.program_id(0)
    grad_low = grad[...].astype(BF16)
    normal = (conv[...] - stats[0:1, :]) * stats[1:2, :]
    out = normal * bn[0:1, :] + bn[1:2, :]
    sig = sigmoid(out)
    b_grad = dot_nt(grad_low, weights[...]) * (sig * (1.0 + out * (1.0 - sig)))
    b_out[...] = b_grad
    put_sums(
        sums_ref,
        utt == 0,
        jnp.sum(b_grad * normal, axis=0, keepdims=True),
        jnp.sum(b_grad, axis=0, keepdims=True),
    )
    part = dot_tn(act[...], grad_low)

    @pl.when(utt == 0)
    def _():
        acc[...] = part

    @pl.when(utt > 0)
    def _():
        acc[...] += part

    @pl.when(utt == pl.num_programs(0) - 1)
    def _():
        rank = rank_ref[0]
        for t in range(HEADS):
            wgrad_out[t ^ rank] = acc[t * PAD : (t + 1) * PAD, :].astype(BF16)


def conv_bwd_kernel(
    rank_ref, len_ref, b_in, conv, value_in, sig_in, stats, bn, bsums, taps, weights,
    n_in, s_in, norm_in, up, grad_ref, wgrad_out, tap_out, sums_ref, glu_pad, cg_pad, cg_ref,
    gg_ref, acc,
):
    utt = pl.program_id(0)
    rank = rank_ref[0]
    valid = (lax.broadcasted_iota(jnp.int32, (SLOT, 1), 0) < len_ref[utt]).astype(F32)
    value, sig = value_in[...], sig_in[...]
    load_padded(glu_pad, value * sig * valid)
    gain, inv = bn[0:1, :], stats[1:2, :]
    normal = (conv[...] - stats[0:1, :]) * inv
    conv_grad = (valid * inv) * (
        b_in[...] * gain - gain * bsums[1:2, :] - normal * (gain * bsums[0:1, :])
    )
    cg_ref[...] = conv_grad
    load_padded(cg_pad, conv_grad)

    @pl.when(utt == 0)
    def _():
        tap_out[...] = jnp.zeros_like(tap_out)

    def block(row, lanes):
        own = cg_ref[pl.ds(row, ROWS_AT_ONCE), lanes]
        for tap in range(KERNEL):
            place = tap + 1
            rows = pl.ds(row + place // 8 * 8, ROWS_AT_ONCE)
            part = glu_pad[place % 8, rows, lanes] * own
            tap_out[tap, :, lanes] += jnp.sum(part.reshape(ROWS_AT_ONCE // 8, 8, LANES), axis=0)

    depth_loop(block)

    def back_block(row, lanes):
        total = jnp.zeros((ROWS_AT_ONCE, LANES), F32)
        for tap in range(KERNEL):
            place = KERNEL - tap
            rows = pl.ds(row + place // 8 * 8, ROWS_AT_ONCE)
            total = total + cg_pad[place % 8, rows, lanes] * taps[tap : tap + 1, lanes]
        gg_ref[pl.ds(row, ROWS_AT_ONCE), lanes] = total

    depth_loop(back_block)
    glu_grad = gg_ref[...] * valid
    value_grad = (glu_grad * sig).astype(BF16)
    gate_grad = (glu_grad * value * sig * (1.0 - sig)).astype(BF16)
    w_value = jnp.concatenate([weights[t ^ rank, 0] for t in range(HEADS)], axis=0)
    w_gate = jnp.concatenate([weights[t ^ rank, 1] for t in range(HEADS)], axis=0)
    z_low = (n_in[...] * norm_in[0:1, :] + norm_in[1:2, :]).astype(BF16)
    value_part = dot_tn(value_grad, z_low)
    gate_part = dot_tn(gate_grad, z_low)

    @pl.when(utt == 0)
    def _():
        acc[0] = value_part
        acc[1] = gate_part

    @pl.when(utt > 0)
    def _():
        acc[0] += value_part
        acc[1] += gate_part

    @pl.when(utt == pl.num_programs(0) - 1)
    def _():
        for t in range(HEADS):
            wgrad_out[t ^ rank, 0] = acc[0, t * PAD : (t + 1) * PAD, :].astype(BF16)
            wgrad_out[t ^ rank, 1] = acc[1, t * PAD : (t + 1) * PAD, :].astype(BF16)

    upstream = up[...] + dot_nn(value_grad, w_value) + dot_nn(gate_grad, w_gate)
    grad, gain_sum, shift_sum = ln_backward(upstream, n_in[...], s_in[...], norm_in[0:1, :])
    grad_ref[...] = grad
    put_sums(sums_ref, utt == 0, gain_sum, shift_sum)


def attn_bwd_kernel(
    rank_ref, len_ref, kind_ref, frames, table, weights, wout, pick, qkv_in, mixed, lse, grad,
    grad_out, wgrad_out, table_out, acc, acc_out,
):
    utt = pl.program_id(0)
    rank = rank_ref[0]
    kind = kind_ref[utt]

    @pl.when(utt == 0)
    def _():
        acc[...] = jnp.zeros_like(acc)
        acc_out[...] = jnp.zeros_like(acc_out)
        table_out[...] = jnp.zeros_like(table_out)

    base_low = (frames[...].astype(F32) + table[pl.ds(kind, 1), :]).astype(BF16)
    valid = lax.broadcasted_iota(jnp.int32, (SLOT, 1), 0) < len_ref[utt]
    upstream = grad[...]
    up_low = upstream.astype(BF16)
    acc_out[...] += dot_nn(mixed[...], up_low)
    mixed_grad = dot_nt(wout[...], up_low).astype(BF16)
    total = upstream
    for head in range(HEADS):
        queries = qkv_in[head, 0:PAD, :]
        keys = qkv_in[head, PAD : 2 * PAD, :]
        values = qkv_in[head, 2 * PAD :, :]
        up_head = mixed_grad[head * PAD : (head + 1) * PAD, :]
        scores = jnp.where(valid, dot_tn(keys, queries) * SCALE, MASK_FILL)
        probs = jnp.exp(scores - lse[head])
        prob_grad = dot_tn(values, up_head)
        delta = jnp.sum(prob_grad * probs, axis=0, keepdims=True)
        score_grad = (probs * (prob_grad - delta)).astype(BF16)
        query_grad = (dot_nn(keys, score_grad) * SCALE).astype(BF16)
        key_grad = (dot_nt(queries, score_grad) * SCALE).astype(BF16)
        value_grad = dot_nt(up_head, probs.astype(BF16)).astype(BF16)
        grads = jnp.concatenate([query_grad, key_grad, value_grad], axis=0)
        acc[head] += dot_nn(grads, base_low)
        total = total + dot_tn(grads, weights[head ^ rank, 0:3].reshape(3 * PAD, D))
    grad_out[...] = total
    column = jnp.sum(total, axis=0, keepdims=True)
    place = lax.broadcasted_iota(jnp.int32, table_out.shape, 0)
    table_out[...] += jnp.where(place == kind, column, 0.0)

    @pl.when(utt == pl.num_programs(0) - 1)
    def _():
        turned = dot_nt(pick[...], acc_out[...].astype(BF16)).astype(BF16)
        turned = dot_nn(turned, pick[...]).astype(BF16)
        for t in range(HEADS):
            wgrad_out[t ^ rank, 0:3] = acc[t].astype(BF16).reshape(3, PAD, D)
            wgrad_out[t ^ rank, 3] = turned[t * PAD : (t + 1) * PAD, :]


def adam_step(first, second, grad_full):
    first_new = BETA_ONE * first + (1.0 - BETA_ONE) * grad_full
    second_new = BETA_TWO * second + (1.0 - BETA_TWO) * grad_full * grad_full
    direction = (first_new * (1.0 / (1.0 - BETA_ONE**STEP))) / (
        jnp.sqrt(second_new * (1.0 / (1.0 - BETA_TWO**STEP))) + ADAM_EPS
    )
    return (first_new, second_new, direction)


def lamb_kernel(turn, weight, first, second, grad, m_out, v_out, u_out, sums_out):
    full = grad[0].astype(F32)
    if turn:
        full = full.T
    rows, columns = weight.shape[1:]
    full = full[:rows, :columns]
    own = weight[0]
    first_new, second_new, direction = adam_step(first[0], second[0], full)
    direction = direction + WEIGHT_DECAY * own
    m_out[0] = first_new
    v_out[0] = second_new
    u_out[0] = direction
    place = lax.broadcasted_iota(jnp.int32, (8, 128), 0)
    sums_out[0] = jnp.where(place == 0, jnp.sum(own * own), jnp.sum(direction * direction))


def whole(shape):
    return pl.BlockSpec(shape, lambda *_: (0,) * len(shape))


def lead(shape, rest):
    return pl.BlockSpec(shape, lambda i, *_: (i,) + (0,) * rest)


SMEM = pl.BlockSpec(memory_space=pltpu.SMEM)


def call(kernel, grid, in_specs, out_specs, out_shape, scratch=(), cost=None):
    return pl.pallas_call(
        kernel,
        grid=(grid,),
        in_specs=in_specs,
        out_specs=out_specs,
        out_shape=[jax.ShapeDtypeStruct(*entry) for entry in out_shape],
        scratch_shapes=list(scratch),
        cost_estimate=None
        if cost is None
        else pl.CostEstimate(flops=cost, bytes_accessed=10_000_000, transcendentals=0),
        compiler_params=pltpu.CompilerParams(vmem_limit_bytes=VMEM_LIMIT),
    )


def swap(value, axis, bit):
    size = lax.axis_size(axis)
    return lax.ppermute(value, axis, [(i, i ^ bit) for i in range(size)])


def bits_of(axis):
    size = lax.axis_size(axis)
    assert size & (size - 1) == 0
    return [1 << i for i in range(size.bit_length() - 1)]


def gather_tensor(shard):
    parts = {0: shard}
    for bit in reversed(bits_of("tensor")):
        for place in list(parts):
            parts[place ^ bit] = swap(parts[place], "tensor", bit)
    return jnp.stack([parts[i] for i in range(len(parts))])


def reduce_tensor(blocks):
    parts = blocks
    for bit in bits_of("tensor"):
        pairs = parts.reshape((parts.shape[0] // 2, 2) + parts.shape[1:])
        got = swap(pairs[:, 1], "tensor", bit)
        parts = (pairs[:, 0].astype(F32) + got.astype(F32)).astype(BF16)
    return parts[0]


def sum_dp(value):
    for bit in bits_of("dp"):
        value = (value.astype(F32) + swap(value, "dp", bit).astype(F32)).astype(value.dtype)
    return value


def sum_all(value):
    for axis in ("tensor", "dp"):
        for bit in bits_of(axis):
            value = value + swap(value, axis, bit)
    return value


def merge_stats(one, two):
    mean_one, dev_one, count_one = one[0:1], one[1:2], one[2:3]
    mean_two, dev_two, count_two = two[0:1], two[1:2], two[2:3]
    count = count_one + count_two
    mean = (mean_one * count_one + mean_two * count_two) / count
    gap = mean_one - mean_two
    dev = dev_one + dev_two + gap * gap * (count_one * count_two / count)
    return jnp.concatenate([mean, dev, count], axis=0)


def pick_matrix():
    pick = np.zeros((WIDE, D), np.float32)
    for column in range(D):
        pick[column // HD * PAD + column % HD, column] = 1.0
    return pick


def turn_pad(shard):
    turned = jnp.swapaxes(shard, -1, -2)
    widths = [(0, 0)] * (turned.ndim - 2) + [(0, PAD - HD), (0, 0)]
    return jnp.pad(turned, widths)


def body(
    frames, cotangent, lengths, rate_kind, attn_w, attn_m, attn_v, ffin_w, ffin_m, ffin_v,
    ffout_w, ffout_m, ffout_v, convin_w, convin_m, convin_v, convout_w, convout_m, convout_v,
    depth_w, depth_m, depth_v, norm_w, norm_m, norm_v, bn_w, bn_m, bn_v, table_w, table_m, table_v,
):
    rank = lax.axis_index("tensor")
    rank_one = rank.reshape(1).astype(jnp.int32)
    rows = frames.shape[0]
    utts = rows // SLOT
    own_len = lax.dynamic_slice_in_dim(lengths, rank * utts, utts, 0)
    own_kind = lax.dynamic_slice_in_dim(rate_kind, rank * utts, utts, 0)
    slot_index = jnp.arange(SLOT, dtype=jnp.int32)
    weight_col = (slot_index[None, :] < own_len[:, None]).astype(F32).reshape(rows, 1)
    pick = jnp.asarray(pick_matrix(), BF16)
    pick_wide = jnp.asarray(pick_matrix(), F32)

    attn_all = gather_tensor(turn_pad(attn_w.astype(BF16)))
    ffin_low, ffout_low = ffin_w.astype(BF16), ffout_w.astype(BF16)
    ffin_all = [gather_tensor(ffin_low[i]) for i in range(2)]
    ffout_all = [gather_tensor(ffout_low[i]) for i in range(2)]
    convin_all = gather_tensor(turn_pad(convin_w.astype(BF16)))
    convout_low = jnp.pad(convout_w.astype(BF16), ((0, PAD - HD), (0, 0)))
    convout_xor = gather_tensor(convout_low)
    convout_all = jnp.concatenate(
        [lax.dynamic_index_in_dim(convout_xor, t ^ rank, 0, False) for t in range(HEADS)], axis=0
    )
    channel_rows = jnp.concatenate([depth_w, bn_w], axis=0)
    channel_rows = lax.dot_general(
        channel_rows, pick_wide, (((1,), (1,)), ((), ())), precision=PRECISE
    )
    taps, bn = channel_rows[:KERNEL], channel_rows[KERNEL:]
    norms = [jnp.stack([norm_w[i], norm_w[i + 4]]) for i in range(4)]

    rowspec = lead((SLOT, D), 1)
    chanspec = lead((SLOT, WIDE), 1)
    onespec = lead((SLOT, 1), 1)
    normspec = whole((2, D))
    attn_block = (HEADS, 4, PAD, D)
    qkv, mixed, lse, n1, s1, wout = call(
        attn_fwd_kernel,
        utts,
        [SMEM, SMEM, SMEM, rowspec, whole((RATES, D)), whole(attn_block), whole((WIDE, D)), normspec],
        [
            pl.BlockSpec((None, HEADS, 3 * PAD, SLOT), lambda i: (i, 0, 0, 0)),
            pl.BlockSpec((None, WIDE, SLOT), lambda i: (i, 0, 0)),
            pl.BlockSpec((None, HEADS, 1, SLOT), lambda i: (i, 0, 0, 0)),
            rowspec,
            onespec,
            whole((WIDE, D)),
        ],
        [
            ((utts, HEADS, 3 * PAD, SLOT), BF16),
            ((utts, WIDE, SLOT), BF16),
            ((utts, HEADS, 1, SLOT), F32),
            ((rows, D), F32),
            ((rows, 1), F32),
            ((WIDE, D), BF16),
        ],
        cost=8_000_000_000,
    )(rank_one, own_len, own_kind, frames, table_w, attn_all, pick, norms[0])

    hid = ffin_w.shape[2]
    groups = ffin_all[0].shape[0]
    wspec = lead((1, hid, D), 2)
    winspec = lead((1, D, hid), 2)
    hidspec = lead((1, rows, hid), 2)
    ffn_scratch = [pltpu.VMEM((rows, D), F32), pltpu.VMEM((rows, D), BF16)]
    hid_one, slope_one, n2, s2 = call(
        functools.partial(ffn_fwd_kernel, False),
        groups,
        [whole((rows, D)), normspec, normspec, winspec, wspec],
        [hidspec, hidspec, whole((rows, D)), whole((rows, 1))],
        [
            ((groups, rows, hid), BF16),
            ((groups, rows, hid), BF16),
            ((rows, D), F32),
            ((rows, 1), F32),
        ],
        ffn_scratch,
        cost=4_000_000_000,
    )(n1, norms[0], norms[1], ffin_all[0], ffout_all[0])

    convin_block = (HEADS, 2, PAD, D)
    value_pre, gate_sig, conv, stats = call(
        conv_fwd_kernel,
        utts,
        [SMEM, SMEM, rowspec, normspec, whole(convin_block), whole((KERNEL, WIDE))],
        [chanspec, chanspec, chanspec, pl.BlockSpec((None, 8, WIDE), lambda i: (i, 0, 0))],
        [((rows, WIDE), F32)] * 3 + [((utts, 8, WIDE), F32)],
        [pltpu.VMEM((8, SPAN, WIDE), F32)],
        cost=4_000_000_000,
    )(rank_one, own_len, n2, norms[1], convin_all, taps)

    stat = stats[0, :3]
    for i in range(1, utts):
        stat = merge_stats(stat, stats[i, :3])
    for axis in ("tensor", "dp"):
        for bit in bits_of(axis):
            stat = merge_stats(stat, swap(stat, axis, bit))
    valid_count = stat[2:3]
    bn_stats = jnp.concatenate(
        [stat[0:1], lax.rsqrt(stat[1:2] / valid_count + EPS_NORM)], axis=0
    )

    chan_two = whole((2, WIDE))
    act, n3, s3 = call(
        mid_fwd_kernel,
        utts,
        [chanspec, chan_two, chan_two, rowspec, normspec, whole((WIDE, D))],
        [chanspec, rowspec, onespec],
        [((rows, WIDE), BF16), ((rows, D), F32), ((rows, 1), F32)],
        cost=1_000_000_000,
    )(conv, bn_stats, bn, n2, norms[1], convout_all)

    hid_two, slope_two, out, grad_four, sums_four = call(
        functools.partial(ffn_fwd_kernel, True),
        groups,
        [whole((rows, D)), normspec, normspec, winspec, wspec, whole((rows, D)), whole((rows, 1))],
        [hidspec, hidspec, whole((rows, D)), whole((rows, D)), whole((8, D))],
        [
            ((groups, rows, hid), BF16),
            ((groups, rows, hid), BF16),
            ((rows, D), BF16),
            ((rows, D), F32),
            ((8, D), F32),
        ],
        ffn_scratch,
        cost=4_000_000_000,
    )(n3, norms[2], norms[3], ffin_all[1], ffout_all[1], cotangent, weight_col)

    def ffn_backward(up, normal, inv, norm_pair, w_in, w_out, hidden, slope):
        return call(
            ffn_bwd_kernel,
            groups,
            [whole((rows, D)), whole((rows, D)), whole((rows, 1)), normspec, winspec, wspec]
            + [hidspec, hidspec],
            [winspec, wspec, whole((rows, D)), whole((8, D))],
            [
                ((groups, D, hid), BF16),
                ((groups, D, hid), BF16),
                ((rows, D), F32),
                ((8, D), F32),
            ],
            [
                pltpu.VMEM((rows, D), F32),
                pltpu.VMEM((rows, D), BF16),
                pltpu.VMEM((D, rows), BF16),
                pltpu.VMEM((D, rows), BF16),
            ],
            cost=8_000_000_000,
        )(up, normal, inv, norm_pair, w_in, w_out, hidden, slope)

    fin_two, fout_two, grad_three, sums_three = ffn_backward(
        grad_four, n3, s3, norms[2], ffin_all[1], ffout_all[1], hid_two, slope_two
    )

    b_grad, cout_grad, bsums = call(
        mid_bwd_kernel,
        utts,
        [SMEM, chanspec, chan_two, chan_two, chanspec, rowspec, whole((WIDE, D))],
        [chanspec, whole((HEADS, PAD, D)), whole((8, WIDE))],
        [((rows, WIDE), F32), ((HEADS, PAD, D), BF16), ((8, WIDE), F32)],
        [pltpu.VMEM((WIDE, D), F32)],
        cost=2_000_000_000,
    )(rank_one, conv, bn_stats, bn, act, grad_three, convout_all)

    bsum_all = sum_all(bsums[:2])
    bsum_mean = bsum_all / valid_count

    grad_two, cin_grad, tap_sums, sums_two = call(
        conv_bwd_kernel,
        utts,
        [SMEM, SMEM] + [chanspec] * 4 + [chan_two] * 3
        + [whole((KERNEL, WIDE)), whole(convin_block), rowspec, onespec, normspec, rowspec],
        [rowspec, whole(convin_block), whole((KERNEL, 8, WIDE)), whole((8, D))],
        [
            ((rows, D), F32),
            (convin_block, BF16),
            ((KERNEL, 8, WIDE), F32),
            ((8, D), F32),
        ],
        [
            pltpu.VMEM((8, SPAN, WIDE), F32),
            pltpu.VMEM((8, SPAN, WIDE), F32),
            pltpu.VMEM((SLOT, WIDE), F32),
            pltpu.VMEM((SLOT, WIDE), F32),
            pltpu.VMEM((2, WIDE, D), F32),
        ],
        cost=8_000_000_000,
    )(
        rank_one, own_len, b_grad, conv, value_pre, gate_sig, bn_stats, bn, bsum_mean, taps,
        convin_all, n2, s2, norms[1], grad_three,
    )

    fin_one, fout_one, grad_one, sums_one = ffn_backward(
        grad_two, n1, s1, norms[0], ffin_all[0], ffout_all[0], hid_one, slope_one
    )

    in_grad, attn_grad, table_sums = call(
        attn_bwd_kernel,
        utts,
        [SMEM, SMEM, SMEM, rowspec, whole((RATES, D)), whole(attn_block), whole((WIDE, D))]
        + [
            whole((WIDE, D)),
            pl.BlockSpec((None, HEADS, 3 * PAD, SLOT), lambda i: (i, 0, 0, 0)),
            pl.BlockSpec((None, WIDE, SLOT), lambda i: (i, 0, 0)),
            pl.BlockSpec((None, HEADS, 1, SLOT), lambda i: (i, 0, 0, 0)),
            rowspec,
        ],
        [rowspec, whole(attn_block), whole((8, D))],
        [((rows, D), F32), (attn_block, BF16), ((8, D), F32)],
        [pltpu.VMEM((HEADS, 3 * PAD, D), F32), pltpu.VMEM((WIDE, D), F32)],
        cost=16_000_000_000,
    )(
        rank_one, own_len, own_kind, frames, table_w, attn_all, wout, pick, qkv, mixed, lse,
        grad_one,
    )

    fin_two_g, fout_two_g, cout_g = (
        sum_dp(reduce_tensor(g)) for g in (fin_two, fout_two, cout_grad)
    )
    fin_one_g, fout_one_g, cin_g = (
        sum_dp(reduce_tensor(g)) for g in (fin_one, fout_one, cin_grad)
    )
    attn_g = sum_dp(reduce_tensor(attn_grad))

    tap_grad = lax.dot_general(
        jnp.sum(tap_sums, axis=1), pick_wide, (((1,), (0,)), ((), ())), precision=PRECISE
    )
    vectors = sum_all(
        jnp.concatenate(
            [sums_one[:2], sums_two[:2], sums_three[:2], sums_four[:2], table_sums[:RATES], tap_grad],
            axis=0,
        )
    )
    bn_grads = lax.dot_general(bsum_all, pick_wide, (((1,), (0,)), ((), ())), precision=PRECISE)

    def lamb(turn, weight, first, second, grads):
        count, height, width = weight.shape
        spec = lead((1, height, width), 2)
        return call(
            functools.partial(lamb_kernel, turn),
            count,
            [spec, spec, spec, lead((1,) + grads.shape[1:], 2)],
            [spec, spec, spec, lead((1, 8, 128), 2)],
            [(weight.shape, F32)] * 3 + [((count, 8, 128), F32)],
            cost=1_000_000,
        )(weight, first, second, grads)

    sets = [
        (attn_w, lamb(True, attn_w, attn_m, attn_v, attn_g)),
        (ffin_w, lamb(False, ffin_w, ffin_m, ffin_v, jnp.stack([fin_one_g, fin_two_g]))),
        (ffout_w, lamb(True, ffout_w, ffout_m, ffout_v, jnp.stack([fout_one_g, fout_two_g]))),
        (convin_w, lamb(True, convin_w, convin_m, convin_v, cin_g)),
        (
            convout_w[None],
            lamb(False, convout_w[None], convout_m[None], convout_v[None], cout_g[None]),
        ),
    ]
    squares = jnp.concatenate([entry[1][3][:, :2, 0] for entry in sets], axis=0)
    for bit in bits_of("tensor"):
        squares = squares + swap(squares, "tensor", bit)
    shard_norms = jnp.sqrt(squares)
    trust = shard_norms[:, 0] / shard_norms[:, 1]
    new_weights = []
    begin = 0
    for weight, entry in sets:
        factor = trust[begin : begin + weight.shape[0]].reshape(-1, 1, 1)
        begin += weight.shape[0]
        new_weights.append(weight - RATE_MATRIX * factor * entry[2])

    depth_first, depth_second, depth_dir = adam_step(depth_m, depth_v, vectors[8 + RATES :])
    depth_dir = depth_dir + WEIGHT_DECAY * depth_w
    depth_wnorm = jnp.sqrt(jnp.sum(depth_w * depth_w))
    depth_unorm = jnp.sqrt(jnp.sum(depth_dir * depth_dir))
    depth_new = depth_w - RATE_MATRIX * (depth_wnorm / depth_unorm) * depth_dir
    weight_norms = jnp.concatenate([shard_norms[:, 0], depth_wnorm[None]])
    update_norms = jnp.concatenate([shard_norms[:, 1], depth_unorm[None]])
    norm_grad = jnp.concatenate([vectors[0:8:2], vectors[1:8:2]], axis=0)
    norm_first, norm_second, norm_dir = adam_step(norm_m, norm_v, norm_grad)
    table_first, table_second, table_dir = adam_step(table_m, table_v, vectors[8 : 8 + RATES])
    bn_first, bn_second, bn_dir = adam_step(bn_m, bn_v, bn_grads)
    m_of = [entry[1][0] for entry in sets]
    v_of = [entry[1][1] for entry in sets]
    return (
        out,
        in_grad,
        new_weights[0],
        m_of[0],
        v_of[0][:3],
        v_of[0][3],
        new_weights[1],
        m_of[1],
        v_of[1],
        new_weights[2],
        m_of[2],
        v_of[2],
        new_weights[3],
        m_of[3],
        v_of[3],
        new_weights[4][0],
        m_of[4][0],
        v_of[4][0],
        depth_new,
        depth_first,
        depth_second,
        norm_w - RATE_VECTOR * norm_dir,
        norm_first,
        norm_second,
        bn_w - RATE_VECTOR * bn_dir,
        bn_first,
        bn_second,
        table_w - RATE_VECTOR * table_dir,
        table_first,
        table_second,
        weight_norms,
        update_norms,
    )


def solution(mesh):
    rows = P(("dp", "tensor"), None)
    last = P(None, None, "tensor")
    mid = P(None, "tensor", None)
    first = P("tensor", None)
    placed = (rows, rows, P("dp"), P("dp")) + (last,) * 6 + (mid,) * 3 + (last,) * 3 + (first,) * 3
    results = (rows, rows) + (last,) * 3 + (P(None, "tensor"),) + (last,) * 3 + (mid,) * 3
    return jax.shard_map(
        body,
        mesh=mesh,
        in_specs=placed + (P(),) * 12,
        out_specs=results + (last,) * 3 + (first,) * 3 + (P(),) * 14,
        check_vma=False,
    )
```

```python
import functools
import math

import jax
import jax.numpy as jnp
import numpy as np
from jax import lax
from jax.experimental import pallas as pl
from jax.experimental.pallas import tpu as pltpu
from jax.sharding import PartitionSpec as P

D = 324
HEADS = 4
KERNEL = 31
HALF = KERNEL // 2
RATES = 3
STEP = 10
SLOT = 496
HD = 81
PAD = 96
WIDE = HEADS * PAD
FF_ROWS = 336
TAIL = 2 * FF_ROWS
CONV_IN_ROWS = 2 * PAD
VECTOR_ROWS = 80
LOWER_VEC = FF_ROWS
LOWER_SPLIT = FF_ROWS + VECTOR_ROWS
LOWER_UP = LOWER_SPLIT
LOWER_CONV = LOWER_UP + FF_ROWS
LOWER_ROWS = LOWER_CONV + CONV_IN_ROWS + 16

EPS_NORM = 1e-05
BETA_ONE = 0.9
BETA_TWO = 0.999
ADAM_EPS = 1e-06
WEIGHT_DECAY = 0.01
RATE_MATRIX = 0.3
RATE_VECTOR = 0.5
MASK_FILL = -1e30
SCALE = 1.0 / math.sqrt(HD)
PRECISE = lax.Precision.HIGHEST

F32 = jnp.float32
BF16 = jnp.bfloat16
LEAD = 16
SPAN = 544


def dot_nn(left, right):
    return lax.dot_general(left, right, (((1,), (0,)), ((), ())), preferred_element_type=F32)


def dot_nt(left, right):
    return lax.dot_general(left, right, (((1,), (1,)), ((), ())), preferred_element_type=F32)


def dot_tn(left, right):
    return lax.dot_general(left, right, (((0,), (0,)), ((), ())), preferred_element_type=F32)


def sigmoid(value):
    return 0.5 * jnp.tanh(0.5 * value) + 0.5


def ln_forward(resid):
    center = resid - jnp.mean(resid, axis=-1, keepdims=True)
    inv = lax.rsqrt(jnp.mean(center * center, axis=-1, keepdims=True) + EPS_NORM)
    return center * inv, inv


def ln_backward(upstream, normal, inv, gain):
    scaled = upstream * gain
    grad = inv * (
        scaled
        - jnp.mean(scaled, axis=-1, keepdims=True)
        - normal * jnp.mean(scaled * normal, axis=-1, keepdims=True)
    )
    gain_sum = jnp.sum(upstream * normal, axis=0, keepdims=True)
    shift_sum = jnp.sum(upstream, axis=0, keepdims=True)
    return grad, gain_sum, shift_sum


def put_sums(ref, first, gain_sum, shift_sum):
    @pl.when(first)
    def _():
        ref[...] = jnp.zeros_like(ref)

    ref[0:1, :] += gain_sum
    ref[1:2, :] += shift_sum


def valid_rows(count):
    return lax.broadcasted_iota(jnp.int32, (SLOT, 1), 0) < count


def assemble(scratch, parts, rank, first, count):
    for place, part in enumerate(parts):
        scratch[place ^ rank] = part[first : first + count, 0:D]


def attn_fwd_kernel(
    rank_ref, len_ref, kind_ref, frames, table, w0, w1, w2, w3, pick, norm,
    low_out, qkv_out, prob_out, mixed_out, n1_out, s1_out, wout_out, low_rows, weights,
):
    utt = pl.program_id(0)
    rank = rank_ref[0]
    which = rank * pl.num_programs(0) + utt

    @pl.when(utt == 0)
    def _():
        assemble(weights, (w0, w1, w2, w3), rank, 0, 4 * PAD)
        turned = jnp.concatenate([weights[t, 3 * PAD :, :] for t in range(HEADS)], axis=0)
        spaced = dot_nt(pick[...], turned).astype(BF16)
        wout_out[...] = dot_nn(spaced, pick[...]).astype(BF16)
        low_rows[...] = frames[...].T

    base = low_rows[pl.ds(utt * SLOT, SLOT), :].astype(F32) + table[pl.ds(kind_ref[which], 1), :]
    base_low = base.astype(BF16)
    low_out[...] = base_low
    valid = valid_rows(len_ref[which])
    for head in range(HEADS):
        qkv = dot_nt(weights[head, 0 : 3 * PAD, :], base_low).astype(BF16)
        qkv_out[head] = qkv
        queries, keys, values = qkv[:PAD], qkv[PAD : 2 * PAD], qkv[2 * PAD :]
        scores = jnp.where(valid, dot_tn(keys, queries) * SCALE, MASK_FILL)
        top = jnp.max(scores, axis=0, keepdims=True)
        expo = jnp.exp(scores - top)
        total = jnp.sum(expo, axis=0, keepdims=True)
        probs = (expo * (1.0 / total)).astype(BF16)
        prob_out[head] = probs
        mixed_out[head * PAD : (head + 1) * PAD, :] = dot_nn(values, probs).astype(BF16)
    attn_out = dot_tn(mixed_out[...], wout_out[...])
    normal, inv = ln_forward(base + attn_out)
    n1_out[...] = normal
    s1_out[...] = inv


def shifted(scratch):
    for shift in range(1, 8):
        scratch[shift, 0 : SPAN - 8, :] = scratch[0, pl.ds(shift, SPAN - 8), :]


def load_padded(scratch, signal):
    scratch[0, 0:LEAD, :] = jnp.zeros((LEAD, WIDE), F32)
    scratch[0, pl.ds(LEAD + SLOT, SPAN - LEAD - SLOT), :] = jnp.zeros((SPAN - LEAD - SLOT, WIDE), F32)
    scratch[0, pl.ds(LEAD, SLOT), :] = signal
    shifted(scratch)


LANES = 128
BLOCKS = ((0, 128), (128, 128), (256, 128), (384, 112))


def depth_tiles(body_fn):
    for row, count in BLOCKS:
        for tile in range(WIDE // LANES):
            body_fn(row, count, slice(tile * LANES, (tile + 1) * LANES))


def depth_sum(padded, row_of, chan, put):
    def block(row, count, lanes):
        total = jnp.zeros((count // 8, 8, LANES), F32)
        for shift in range(8):
            rows = padded[shift, pl.ds(row, count + 24), lanes]
            for lift in range(4):
                place = 8 * lift + shift
                if 1 <= place <= KERNEL:
                    tap = row_of(place)
                    part = rows[8 * lift : 8 * lift + count].reshape(count // 8, 8, LANES)
                    total = total + part * chan[tap, :, lanes][None]
        put(row, count, lanes, total.reshape(count, LANES))

    depth_tiles(block)


def depth_products(padded, own, sums):
    def block(row, count, lanes):
        mine = own[pl.ds(row, count), lanes]
        for shift in range(8):
            rows = padded[shift, pl.ds(row, count + 24), lanes]
            for lift in range(4):
                place = 8 * lift + shift
                if 1 <= place <= KERNEL:
                    part = rows[8 * lift : 8 * lift + count] * mine
                    part = jnp.sum(part.reshape(count // 8, 8, LANES), axis=0)
                    sums[place - 1, :, lanes] += part

    depth_tiles(block)


def merge_stats(one, two):
    mean_one, dev_one, count_one = one[0:1], one[1:2], one[2:3]
    mean_two, dev_two, count_two = two[0:1], two[1:2], two[2:3]
    count = count_one + count_two
    mean = (mean_one * count_one + mean_two * count_two) / count
    gap = mean_one - mean_two
    dev = dev_one + dev_two + gap * gap * (count_one * count_two / count)
    return jnp.concatenate([mean, dev, count], axis=0)


def bn_parts(conv, stat, chan):
    inv = lax.rsqrt(stat[1:2, :] / stat[2:3, :] + EPS_NORM)
    normal = (conv - stat[0:1, :]) * inv
    return normal, inv, normal * chan[32, 0:1, :] + chan[33, 0:1, :]


def utt_rows(utt):
    return pl.ds(pl.multiple_of(utt * SLOT, 16), SLOT)


def each_utt(rows, body_fn):
    def step(utt, carry):
        body_fn(utt, utt_rows(utt))
        return carry

    lax.fori_loop(0, rows // SLOT, step, 0)


class Copies:
    def __init__(self, sems):
        self.sems = sems
        self.count = 0
        self.open = []

    def start(self, source, target):
        copy = pltpu.make_async_copy(source, target, self.sems.at[self.count])
        self.count += 1
        copy.start()
        return copy

    def out(self, source, target):
        self.open.append(self.start(source, target))

    def finish(self):
        for copy in self.open:
            copy.wait()


def pack_kernel(
    depth, bn, pick, attn_in, ffin_in, ffout_in, convin_in, convout_in,
    attn_out, one_out, two_out, chan_out,
    attn, ffin, ffout, convin, convout, attn_low, one, two, sems,
):
    copies = Copies(sems)
    pairs = (attn_in, attn), (ffin_in, ffin), (ffout_in, ffout), (convin_in, convin), (convout_in, convout)
    loads = [copies.start(source, target) for source, target in pairs]
    for out in (attn_low, one, two):
        out[...] = jnp.zeros_like(out)
    loads[0].wait()
    for j in range(4):
        attn_low[j * PAD : j * PAD + HD, 0:D] = attn[:, j, :].astype(BF16)
    copies.out(attn_low, attn_out)
    loads[1].wait()
    loads[2].wait()
    for j, out in ((0, one), (1, two)):
        out[0:D, 0:D] = ffin[:, j, :].astype(BF16)
        out[FF_ROWS : FF_ROWS + D, 0:D] = ffout[:, j, :].astype(BF16)
    loads[3].wait()
    loads[4].wait()
    for j in range(2):
        one[TAIL + j * PAD : TAIL + j * PAD + HD, 0:D] = convin[:, j, :].astype(BF16)
    two[TAIL : TAIL + HD, 0:D] = convout[...].astype(BF16)
    copies.out(one, one_out)
    copies.out(two, two_out)
    def spread(rows):
        return lax.dot_general(
            rows, pick[...], (((1,), (1,)), ((), ())), precision=PRECISE, preferred_element_type=F32
        )

    for first, rows in ((0, spread(depth[...])), (32, spread(bn[...]))):
        count = rows.shape[0]
        chan_out[first : first + count] = jnp.broadcast_to(rows[:, None, :], (count, 8, WIDE))
    copies.finish()


def ffn_forward(z_low, weights, hid, slope, acc, done=None):
    def block(p, carry):
        pre = dot_nn(z_low[...], weights[p, 0:D, 0:D])
        sig = sigmoid(pre)
        hidden = pre * sig
        hid_low = hidden.astype(BF16)
        hid[p] = hid_low
        slope[p] = (sig + hidden * (1.0 - sig)).astype(BF16)
        acc[...] += dot_nn(hid_low, weights[p, FF_ROWS : FF_ROWS + D, 0:D])
        return carry

    if done is None:
        lax.fori_loop(0, HEADS, block, 0)
    else:
        for p in range(HEADS):
            block(p, 0)
            done(p)


def ffn_backward(up_low, up_turn, z_turn, weights, hid, slope, acc, grads, up_row, down_row, done=None):
    def block(p, carry):
        back = dot_nt(up_low[...], weights[p, FF_ROWS : FF_ROWS + D, 0:D])
        pre_grad = (back * slope[p].astype(F32)).astype(BF16)
        grads[p, down_row : down_row + D, 0:D] = dot_nn(up_turn[...], hid[p]).astype(BF16)
        grads[p, up_row : up_row + D, 0:D] = dot_nn(z_turn[...], pre_grad).astype(BF16)
        if acc is None:
            slope[p] = pre_grad
        else:
            acc[...] += dot_nt(pre_grad, weights[p, 0:D, 0:D])
        return carry

    if done is None:
        lax.fori_loop(0, HEADS, block, 0)
    else:
        for p in range(HEADS):
            block(p, 0)
            done(p)


def send_out(copies, grads, send, keep):
    for i in range(HEADS // 2):
        copies.out(grads.at[2 * i + 1], send.at[i])
        copies.out(grads.at[2 * i], keep.at[i])


def lower_fwd_kernel(
    rank_ref, len_ref, norm, chan, n1_in, w0, w1, w2, w3,
    hid_out, slope_out, n2_out, s2_out, value_out, sig_out, conv_out, stat_out,
    n1, weights, hid, slope, n2, s2, value, sig, conv, conv_w, padded, acc, z_low, sems,
):
    copies = Copies(sems)
    rank = rank_ref[0]
    rows = n1_in.shape[0]
    loads = [copies.start(n1_in, n1)]
    loads += [copies.start(part, weights.at[p]) for p, part in enumerate((w0, w1, w2, w3))]
    for load in loads:
        load.wait()
    z = n1[...] * norm[0:1, :] + norm[4:5, :]
    acc[...] = z
    z_low[...] = z.astype(BF16)

    def done(p):
        copies.out(hid.at[p], hid_out.at[p])
        copies.out(slope.at[p], slope_out.at[p])

    ffn_forward(z_low, weights, hid, slope, acc, done)
    normal, inv = ln_forward(acc[...])
    n2[...] = normal
    s2[...] = inv
    copies.out(n2, n2_out)
    copies.out(s2, s2_out)
    z_low[...] = (normal * norm[1:2, :] + norm[5:6, :]).astype(BF16)
    for p in range(HEADS):
        conv_w[p ^ rank] = weights[p, TAIL : TAIL + CONV_IN_ROWS, 0:D]
    value[...] = dot_nt(z_low[...], conv_w[:, 0:PAD, :].reshape(WIDE, D))
    copies.out(value, value_out)
    sig[...] = sigmoid(dot_nt(z_low[...], conv_w[:, PAD:, :].reshape(WIDE, D)))
    copies.out(sig, sig_out)
    utts = rows // SLOT

    def utterance(utt, here):
        count = len_ref[rank * utts + utt]
        valid = valid_rows(count).astype(F32)
        load_padded(padded, value[here, :] * sig[here, :] * valid)

        def put(row, number, lanes, total):
            conv[pl.ds(pl.multiple_of(utt * SLOT + row, 16), number), lanes] = total

        depth_sum(padded, lambda place: place - 1, chan, put)
        own = conv[here, :]
        number = count.astype(F32)
        mean = jnp.sum(own * valid, axis=0, keepdims=True) / number
        center = (own - mean) * valid
        dev = jnp.sum(center * center, axis=0, keepdims=True)
        stat = jnp.concatenate([mean, dev, jnp.zeros_like(mean) + number], axis=0)

        @pl.when(utt == 0)
        def _():
            stat_out[...] = stat

        @pl.when(utt > 0)
        def _():
            stat_out[...] = merge_stats(stat_out[...], stat)

    each_utt(rows, utterance)
    copies.out(conv, conv_out)
    copies.finish()


def upper_kernel(
    rank_ref, len_ref, norm, chan, stat, conv_in, n2_in, cot_in, w0, w1, w2, w3,
    out_out, grad_out, b_out, send, keep, bsums, sums_three, sums_four,
    conv, n2, cot, weights, conv_w, act, hid, slope, acc, n3, s3, z_low, z_turn, up_low, up_turn,
    out, b_grad, grads, conv_acc, sems,
):
    copies = Copies(sems)
    rank = rank_ref[0]
    rows = conv_in.shape[0]
    utts = rows // SLOT
    loads = [copies.start(part, weights.at[p]) for p, part in enumerate((w0, w1, w2, w3))]
    loads += [copies.start(conv_in, conv), copies.start(n2_in, n2)]
    cot_load = copies.start(cot_in, cot)
    for load in loads:
        load.wait()
    for p in range(HEADS):
        conv_w[p ^ rank] = weights[p, TAIL : TAIL + PAD, 0:D]
    bsums[...] = jnp.zeros_like(bsums)
    sums_three[...] = jnp.zeros_like(sums_three)
    sums_four[...] = jnp.zeros_like(sums_four)
    conv_acc[...] = jnp.zeros_like(conv_acc)

    def utterance_fwd(utt, here):
        _, _, bn_out = bn_parts(conv[here, :], stat, chan)
        act_low = (bn_out * sigmoid(bn_out)).astype(BF16)
        act[here, :] = act_low
        second = n2[here, :] * norm[1:2, :] + norm[5:6, :]
        normal, inv = ln_forward(second + dot_nn(act_low, conv_w[...].reshape(WIDE, D)))
        n3[here, :] = normal
        s3[here, :] = inv
        z = normal * norm[2:3, :] + norm[6:7, :]
        acc[here, :] = z
        z_low[here, :] = z.astype(BF16)

    each_utt(rows, utterance_fwd)
    z_turn[...] = z_low[...].T
    ffn_forward(z_low, weights, hid, slope, acc)
    normal, inv = ln_forward(acc[...])
    gain = norm[3:4, :]
    out[...] = (normal * gain + norm[7:8, :]).astype(BF16).T
    copies.out(out, out_out)
    cot_load.wait()
    valid = jnp.concatenate([valid_rows(len_ref[rank * utts + u]) for u in range(utts)], axis=0)
    upstream = jnp.where(valid, cot[...].T.astype(F32), 0.0)
    grad, gain_sum, shift_sum = ln_backward(upstream, normal, inv, gain)
    sums_four[0:1, :] = gain_sum
    sums_four[1:2, :] = shift_sum
    acc[...] = grad
    up_low[...] = grad.astype(BF16)
    up_turn[...] = up_low[...].T
    ffn_backward(up_low, up_turn, z_turn, weights, hid, slope, acc, grads, 0, FF_ROWS)
    grad, gain_sum, shift_sum = ln_backward(acc[...], n3[...], s3[...], norm[2:3, :])
    sums_three[0:1, :] = gain_sum
    sums_three[1:2, :] = shift_sum
    acc[...] = grad
    copies.out(acc, grad_out)
    up_low[...] = grad.astype(BF16)

    def utterance_bwd(utt, here):
        normal, _, bn_out = bn_parts(conv[here, :], stat, chan)
        sig = sigmoid(bn_out)
        low = up_low[here, :]
        own = dot_nt(low, conv_w[...].reshape(WIDE, D)) * (sig * (1.0 + bn_out * (1.0 - sig)))
        b_grad[here, :] = own
        bsums[0:1, :] += jnp.sum(own * normal, axis=0, keepdims=True)
        bsums[1:2, :] += jnp.sum(own, axis=0, keepdims=True)
        conv_acc[...] += dot_tn(act[here, :], low)

    each_utt(rows, utterance_bwd)
    copies.out(b_grad, b_out)
    for t in range(HEADS):
        place = t ^ rank
        grads[place, TAIL : TAIL + PAD, 0:D] = conv_acc[t * PAD : (t + 1) * PAD, :].astype(BF16)
    send_out(copies, grads, send, keep)
    copies.finish()


def conv_bwd_kernel(
    rank_ref, len_ref, norm, chan, stat, bsums, pick, sums_three, sums_four,
    b_in, conv_in, value_in, sig_in, n2_in, s2_in, grad_in, w0, w1, w2, w3,
    grad_out, wgrad_out, vec_out,
    b_grad, conv, value, sig, n2, s2, grad, parts, weights, glu_pad, cg_pad, cg_ref, gg_ref,
    conv_acc, tap_sums, sums_ref, sems,
):
    copies = Copies(sems)
    rank = rank_ref[0]
    rows = b_in.shape[0]
    utts = rows // SLOT
    first = pl.ds(0, SLOT)
    pairs = [(value_in, value), (sig_in, sig), (conv_in, conv), (b_in, b_grad)]
    loads = [copies.start(source.at[first], target.at[first]) for source, target in pairs]
    others = pl.ds(SLOT, rows - SLOT)
    later = [copies.start(source.at[others], target.at[others]) for source, target in pairs]
    later += [copies.start(n2_in, n2), copies.start(s2_in, s2), copies.start(grad_in, grad)]
    later += [
        copies.start(part.at[pl.ds(TAIL, CONV_IN_ROWS)], parts.at[p])
        for p, part in enumerate((w0, w1, w2, w3))
    ]
    tap_sums[...] = jnp.zeros_like(tap_sums)
    conv_acc[...] = jnp.zeros_like(conv_acc)
    sums_ref[...] = jnp.zeros_like(sums_ref)
    for load in loads:
        load.wait()

    def utterance(utt, here):
        valid = valid_rows(len_ref[rank * utts + utt]).astype(F32)
        gain = chan[32, 0:1, :]
        count = stat[2:3, :]
        load_padded(glu_pad, value[here, :] * sig[here, :] * valid)
        normal, inv, _ = bn_parts(conv[here, :], stat, chan)
        conv_grad = (valid * inv) * (
            b_grad[here, :] * gain
            - gain * (bsums[1:2, :] / count)
            - normal * (gain * (bsums[0:1, :] / count))
        )
        cg_ref[...] = conv_grad
        load_padded(cg_pad, conv_grad)
        depth_products(glu_pad, cg_ref, tap_sums)

        def put(row, number, lanes, total):
            gg_ref[pl.ds(row, number), lanes] = total

        depth_sum(cg_pad, lambda place: KERNEL - place, chan, put)

        @pl.when(utt == 0)
        def _():
            for load in later:
                load.wait()
            for p in range(HEADS):
                weights[p ^ rank] = parts[p, :, 0:D]

        glu_grad = gg_ref[...] * valid
        sig_now = sig[here, :]
        value_grad = (glu_grad * sig_now).astype(BF16)
        gate_grad = (glu_grad * value[here, :] * sig_now * (1.0 - sig_now)).astype(BF16)
        normal = n2[here, :]
        z_low = (normal * norm[1:2, :] + norm[5:6, :]).astype(BF16)
        conv_acc[0] += dot_tn(value_grad, z_low)
        conv_acc[1] += dot_tn(gate_grad, z_low)
        upstream = (
            grad[here, :]
            + dot_nn(value_grad, weights[:, 0:PAD, :].reshape(WIDE, D))
            + dot_nn(gate_grad, weights[:, PAD:, :].reshape(WIDE, D))
        )
        own, gain_sum, shift_sum = ln_backward(upstream, normal, s2[here, :], norm[1:2, :])
        grad[here, :] = own
        sums_ref[0:1, :] += gain_sum
        sums_ref[1:2, :] += shift_sum

    each_utt(rows, utterance)
    copies.out(grad, grad_out)
    for t in range(HEADS):
        for j in range(2):
            part = conv_acc[j, t * PAD : (t + 1) * PAD, :].astype(BF16)
            wgrad_out[t ^ rank, j * PAD : (j + 1) * PAD, :] = part
    taps = jnp.sum(tap_sums[...], axis=1).astype(BF16)
    vec = [dot_nn(taps, pick[...]), jnp.zeros((1, D), F32)]
    vec += [sums_ref[0:2, :], sums_three[0:2, :], sums_four[0:2, :]]
    vec += [jnp.zeros((VECTOR_ROWS - 38, D), F32)]
    vec_out[...] = jnp.concatenate(vec, axis=0).astype(BF16)
    copies.finish()


def lower_weights_kernel(
    norm, cin_grad, vectors, up_in, n1_in, w0, w1, w2, w3, hid_in, slope_in,
    pre_out, send, keep,
    up, n1, weights, hid, slope, up_low, up_turn, z_turn, grads, sems,
):
    copies = Copies(sems)
    loads = [copies.start(up_in, up), copies.start(n1_in, n1)]
    down = pl.ds(FF_ROWS, FF_ROWS)
    loads += [
        copies.start(part.at[down], weights.at[p, down]) for p, part in enumerate((w0, w1, w2, w3))
    ]
    loads += [copies.start(slope_in, slope), copies.start(hid_in, hid)]
    for load in loads[:2]:
        load.wait()
    up_low[...] = up[...].astype(BF16)
    up_turn[...] = up_low[...].T
    z_turn[...] = (n1[...] * norm[0:1, :] + norm[4:5, :]).astype(BF16).T
    for load in loads[2:]:
        load.wait()

    def done(p):
        copies.out(slope.at[p], pre_out.at[p])

    ffn_backward(up_low, up_turn, z_turn, weights, hid, slope, None, grads, LOWER_UP, 0, done)
    for p in range(HEADS):
        grads[p, LOWER_CONV : LOWER_CONV + CONV_IN_ROWS, 0:D] = cin_grad[p]
        grads[p, LOWER_VEC : LOWER_VEC + VECTOR_ROWS, 0:D] = vectors[...]
    send_out(copies, grads, send, keep)
    copies.finish()


def lower_bwd_kernel(
    norm, up_in, n1_in, s1_in, w0, w1, w2, w3, pre_in, grad_out, sums_one,
    acc, n1, s1, weights, pre, sems,
):
    copies = Copies(sems)
    up_rows = pl.ds(0, FF_ROWS)
    loads = [copies.start(up_in, acc)]
    for p, part in enumerate((w0, w1, w2, w3)):
        loads += [copies.start(part.at[up_rows], weights.at[p]), copies.start(pre_in.at[p], pre.at[p])]
    late = [copies.start(n1_in, n1), copies.start(s1_in, s1)]
    loads[0].wait()
    for p in range(HEADS):
        loads[2 * p + 1].wait()
        loads[2 * p + 2].wait()
        acc[...] += dot_nt(pre[p], weights[p, 0:D, 0:D])
    for load in late:
        load.wait()
    grad, gain_sum, shift_sum = ln_backward(acc[...], n1[...], s1[...], norm[0:1, :])
    acc[...] = grad
    copies.out(acc, grad_out)
    sums_one[...] = jnp.zeros_like(sums_one)
    sums_one[0:1, :] = gain_sum
    sums_one[1:2, :] = shift_sum
    copies.finish()


def attn_bwd_kernel(
    rank_ref, kind_ref, low_in, w0, w1, w2, w3, wout, pick, qkv_in, probs_in, mixed, grad, sums_one,
    grad_out, send, keep, acc, acc_out, rows_out, table_sums, weights,
):
    utt = pl.program_id(0)
    rank = rank_ref[0]

    @pl.when(utt == 0)
    def _():
        assemble(weights, (w0, w1, w2, w3), rank, 0, 3 * PAD)
        acc[...] = jnp.zeros_like(acc)
        acc_out[...] = jnp.zeros_like(acc_out)
        table_sums[...] = jnp.zeros_like(table_sums)

    base_low = low_in[...]
    upstream = grad[...]
    up_low = upstream.astype(BF16)
    acc_out[...] += dot_nn(mixed[...], up_low)
    mixed_grad = dot_nt(wout[...], up_low).astype(BF16)
    total = upstream
    for head in range(HEADS):
        queries = qkv_in[head, 0:PAD, :]
        keys = qkv_in[head, PAD : 2 * PAD, :]
        values = qkv_in[head, 2 * PAD :, :]
        up_head = mixed_grad[head * PAD : (head + 1) * PAD, :]
        probs_low = probs_in[head]
        probs = probs_low.astype(F32)
        prob_grad = dot_tn(values, up_head)
        delta = jnp.sum(prob_grad * probs, axis=0, keepdims=True)
        score_grad = (probs * (prob_grad - delta)).astype(BF16)
        query_grad = (dot_nn(keys, score_grad) * SCALE).astype(BF16)
        key_grad = (dot_nt(queries, score_grad) * SCALE).astype(BF16)
        value_grad = dot_nt(up_head, probs_low).astype(BF16)
        grads = jnp.concatenate([query_grad, key_grad, value_grad], axis=0)
        acc[head] += dot_nn(grads, base_low)
        total = total + dot_tn(grads, weights[head])
    rows_out[pl.ds(utt * SLOT, SLOT), :] = total
    column = jnp.sum(total, axis=0, keepdims=True)
    kind = kind_ref[rank * pl.num_programs(0) + utt]
    place = lax.broadcasted_iota(jnp.int32, table_sums.shape, 0)
    table_sums[...] += jnp.where(place == kind, column, 0.0)

    @pl.when(utt == pl.num_programs(0) - 1)
    def _():
        grad_out[...] = rows_out[...].T
        turned = dot_nt(pick[...], acc_out[...].astype(BF16)).astype(BF16)
        turned = dot_nn(turned, pick[...]).astype(BF16)
        extra = [table_sums[0:RATES, :], sums_one[0:2, :]]
        extra += [jnp.zeros((PAD - HD - RATES - 2, D), F32)]
        extra = jnp.concatenate(extra, axis=0).astype(BF16)
        rows_out[0:WIDE, :] = turned.astype(F32)
        for place in range(HEADS):
            t = place ^ rank
            out = send if place % 2 else keep
            out[place // 2, 0 : 3 * PAD, 0:D] = acc[t].astype(BF16)
            out[place // 2, HD:PAD, 0:D] = extra
            block = rows_out[pl.ds(pl.multiple_of(t * PAD, PAD), PAD), :]
            out[place // 2, 3 * PAD :, 0:D] = block.astype(BF16)


def adam_step(first, second, grad_full):
    first_new = BETA_ONE * first + (1.0 - BETA_ONE) * grad_full
    second_new = BETA_TWO * second + (1.0 - BETA_TWO) * grad_full * grad_full
    scaled = jnp.maximum(second_new * (1.0 / (1.0 - BETA_TWO**STEP)), 1e-30)
    below = scaled * lax.rsqrt(scaled) + ADAM_EPS
    inverse = pl.reciprocal(below, approx=True)
    inverse = inverse * (2.0 - below * inverse)
    direction = (first_new * (1.0 / (1.0 - BETA_ONE**STEP))) * inverse
    return (first_new, second_new, direction)


def total_of(array):
    return jnp.sum(jnp.sum(array, axis=1, keepdims=True), axis=0, keepdims=True)


def put_squares(sums_out, row, own, direction):
    if own.ndim == 3:
        own = jnp.sum(own * own, axis=0)
        direction = jnp.sum(direction * direction, axis=0)
        count = own.shape[0]
    else:
        own = jnp.sum(own * own, axis=0, keepdims=True)
        direction = jnp.sum(direction * direction, axis=0, keepdims=True)
        count = 1
    sums_out[row : row + count, :] = jnp.broadcast_to(
        jnp.sum(own, axis=1, keepdims=True), (count, 128)
    )
    sums_out[16 + row : 16 + row + count, :] = jnp.broadcast_to(
        jnp.sum(direction, axis=1, keepdims=True), (count, 128)
    )


def join_halves(spot, mine, other, scratch):
    half = mine.shape[0]
    scratch[pl.ds(pl.multiple_of(spot * half, 16), half), :] = mine[...].astype(F32)
    scratch[pl.ds(pl.multiple_of((1 - spot) * half, 16), half), :] = other[...].astype(F32)


def lamb_stack(weight, first, second, grads, stacked, sums_out, row):
    for j, grad in enumerate(grads):
        stacked[:, j, :] = grad
    own = weight[...]
    first_new, second_new, direction = adam_step(first[...], second[...], stacked[...])
    direction = direction + WEIGHT_DECAY * own
    put_squares(sums_out, row, own, direction)
    return first_new, second_new, direction


def lamb_down_kernel(
    spot_ref, one_mine, one_other, two_mine, two_other, fout_w, fout_m, fout_v, cout_w, cout_m, cout_v,
    fout_mo, fout_vo, fout_u, cout_mo, cout_vo, cout_u, fin_grad, vec_out, sums_out, one, two, wide,
):
    spot = spot_ref[0]
    join_halves(spot, one_mine, one_other, one)
    join_halves(spot, two_mine, two_other, two)
    sums_out[...] = jnp.zeros_like(sums_out)
    fin_grad[...] = one[0:D, 0:D]
    vec_out[...] = two[FF_ROWS : FF_ROWS + VECTOR_ROWS, 0:D]
    grads = (two[0:D, 0:D].T, one[FF_ROWS : FF_ROWS + D, 0:D].T)
    fout_mo[...], fout_vo[...], fout_u[...] = lamb_stack(
        fout_w, fout_m, fout_v, grads, wide, sums_out, 6
    )
    own = cout_w[...]
    grad = one[TAIL : TAIL + HD, 0:D]
    first_new, second_new, direction = adam_step(cout_m[...], cout_v[...], grad)
    direction = direction + WEIGHT_DECAY * own
    cout_mo[...], cout_vo[...], cout_u[...] = first_new, second_new, direction
    put_squares(sums_out, 10, own, direction)


def lamb_up_kernel(
    spot_ref, mine, other, fin_grad, fin_w, fin_m, fin_v, cin_w, cin_m, cin_v,
    fin_mo, fin_vo, fin_u, cin_mo, cin_vo, cin_u, sums_out, full, wide, narrow,
):
    join_halves(spot_ref[0], mine, other, full)
    sums_out[...] = jnp.zeros_like(sums_out)
    grads = (full[0:D, 0:D], fin_grad[...])
    fin_mo[...], fin_vo[...], fin_u[...] = lamb_stack(fin_w, fin_m, fin_v, grads, wide, sums_out, 4)
    grads = [full[FF_ROWS + j * PAD : FF_ROWS + j * PAD + HD, 0:D] for j in range(2)]
    cin_mo[...], cin_vo[...], cin_u[...] = lamb_stack(
        cin_w, cin_m, cin_v, grads, narrow, sums_out, 8
    )


def lamb_attn_kernel(
    share, spot_ref, mine, other, vec, bsums, pick, attn_w, attn_m, attn_v, depth_w, depth_m, depth_v,
    norm_w, norm_m, norm_v, bn_w, bn_m, bn_v, table_w, table_m, table_v,
    attn_mo, attn_vo, out_vo, attn_u, depth_wo, depth_mo, depth_vo, norm_wo, norm_mo, norm_vo,
    bn_wo, bn_mo, bn_vo, table_wo, table_mo, table_vo, sums_out, full, stacked,
):
    join_halves(spot_ref[0], mine, other, full)
    sums_out[...] = jnp.zeros_like(sums_out)
    grads = [full[j * PAD : j * PAD + HD, 0:D] for j in range(4)]
    first_new, second_new, direction = lamb_stack(
        attn_w, attn_m, attn_v, grads, stacked, sums_out, 0
    )
    attn_mo[...] = first_new
    attn_u[...] = direction
    for j in range(3):
        attn_vo[j] = second_new[:, j, :]
    out_vo[...] = second_new[:, 3, :]

    own = depth_w[...]
    depth_mo[...], depth_vo[...], direction = adam_step(depth_m[...], depth_v[...], vec[0:KERNEL, :])
    direction = direction + WEIGHT_DECAY * own
    own_norm = jnp.sqrt(total_of(own * own))
    step_norm = jnp.sqrt(total_of(direction * direction))
    depth_wo[...] = own - RATE_MATRIX * (own_norm / step_norm) * direction
    put_squares(sums_out, 11, own, direction)
    for row in (11, 27):
        sums_out[row : row + 1, :] = sums_out[row : row + 1, :] * share

    def vector(weight, first, second, grad, w_out, m_out, v_out):
        m_out[...], v_out[...], move = adam_step(first[...], second[...], grad)
        w_out[...] = weight[...] - RATE_VECTOR * move

    one = full[HD + RATES : HD + RATES + 2, 0:D]
    rows = [one[0:1]] + [vec[32 + 2 * i : 33 + 2 * i, :] for i in range(3)]
    rows += [one[1:2]] + [vec[33 + 2 * i : 34 + 2 * i, :] for i in range(3)]
    vector(norm_w, norm_m, norm_v, jnp.concatenate(rows, axis=0), norm_wo, norm_mo, norm_vo)
    bn_grad = lax.dot_general(
        bsums[...], pick[...], (((1,), (0,)), ((), ())), precision=PRECISE,
        preferred_element_type=F32,
    )
    vector(bn_w, bn_m, bn_v, bn_grad, bn_wo, bn_mo, bn_vo)
    table_grad = full[HD : HD + RATES, 0:D]
    vector(table_w, table_m, table_v, table_grad, table_wo, table_mo, table_vo)


def step_kernel(sums, *refs):
    weights, moves_in, outs, norm_outs = refs[:5], refs[5:10], refs[10:15], refs[15:17]
    moves, sems = refs[17:22], refs[22]
    copies = Copies(sems)
    loads = [copies.start(moves_in[i], moves[i]) for i in range(5)]
    norms = jnp.sqrt(sums[...])
    factor = RATE_MATRIX * (norms[0:16] / jnp.maximum(norms[16:32], 1e-37))
    shape = (16, 128)
    diagonal = lax.broadcasted_iota(jnp.int32, shape, 0) == lax.broadcasted_iota(jnp.int32, shape, 1)
    for i, out in enumerate(norm_outs):
        across = jnp.where(diagonal, norms[16 * i : 16 * i + 16], 0.0)
        out[...] = jnp.sum(across, axis=0, keepdims=True)[:, 0:12]
    for i, row in enumerate((4, 6, 0, 8, 10)):
        weight, move = weights[i], moves[i]
        stacked = len(weight.shape) == 3
        number = weight.shape[1] if stacked else 1
        loads[i].wait()
        scale = factor[row : row + number, 0:1]
        move[...] = weight[...] - (scale[None] if stacked else scale) * move[...]
        copies.out(move, outs[i])
    copies.finish()


SMEM = pl.BlockSpec(memory_space=pltpu.SMEM)


def whole(shape):
    return pl.BlockSpec(shape, lambda *_: (0,) * len(shape))


def lead(shape, rest, place=None):
    def index(i):
        return ((i if place is None else place(i)),) + (0,) * rest

    return pl.BlockSpec(shape, index)


def placed(entries, pinned):
    return [
        pltpu.HBM(*entry) if place in pinned else jax.ShapeDtypeStruct(*entry)
        for place, entry in enumerate(entries)
    ]


def call(kernel, grid, in_specs, out_specs, out_shape, scratch=(), cost=1_000_000, limit=40, pinned=()):
    return pl.pallas_call(
        kernel,
        grid=(grid,),
        in_specs=in_specs,
        out_specs=out_specs,
        out_shape=placed(out_shape, pinned),
        scratch_shapes=list(scratch),
        cost_estimate=pl.CostEstimate(flops=cost, bytes_accessed=10_000_000, transcendentals=0),
        compiler_params=pltpu.CompilerParams(vmem_limit_bytes=limit * 1024 * 1024),
    )


def call_whole(kernel, scalars, arrays, out_shape, scratch=(), limit=14):
    return pl.pallas_call(
        kernel,
        in_specs=[SMEM] * len(scalars) + [pl.BlockSpec(memory_space=pltpu.VMEM)] * len(arrays),
        out_specs=[pl.BlockSpec(memory_space=pltpu.VMEM)] * len(out_shape),
        out_shape=[jax.ShapeDtypeStruct(*entry) for entry in out_shape],
        scratch_shapes=list(scratch),
        cost_estimate=pl.CostEstimate(flops=1_000_000, bytes_accessed=2_000_000, transcendentals=0),
        compiler_params=pltpu.CompilerParams(vmem_limit_bytes=limit * 1024 * 1024),
    )(*scalars, *arrays)


ANY = pl.BlockSpec(memory_space=pl.ANY)
VMEM = pl.BlockSpec(memory_space=pltpu.VMEM)


def call_mixed(kernel, scalars, small, large, large_out, small_out, scratch, copies, cost, limit=56, pinned=()):
    return pl.pallas_call(
        kernel,
        in_specs=[SMEM] * len(scalars) + [VMEM] * len(small) + [ANY] * len(large),
        out_specs=[ANY] * len(large_out) + [VMEM] * len(small_out),
        out_shape=placed(large_out + small_out, pinned),
        scratch_shapes=[pltpu.VMEM(*entry) for entry in scratch] + [pltpu.SemaphoreType.DMA((copies,))],
        cost_estimate=pl.CostEstimate(flops=cost, bytes_accessed=10_000_000, transcendentals=0),
        compiler_params=pltpu.CompilerParams(vmem_limit_bytes=limit * 1024 * 1024),
    )(*scalars, *small, *large)


def swap(value, axis, bit):
    size = lax.axis_size(axis)
    return lax.ppermute(value, axis, [(i, i ^ bit) for i in range(size)])


def combine_all(value, merge, pause=None):
    for bit in bits_of("tensor"):
        value = merge(value, swap(value, "tensor", bit))
    if pause is not None:
        value = pause(value)
    for bit in bits_of("dp"):
        value = merge(value, swap(value, "dp", bit))
    return value


def bits_of(axis):
    size = lax.axis_size(axis)
    assert size & (size - 1) == 0
    return [1 << i for i in range(size.bit_length() - 1)]


def tie(*values):
    return lax.optimization_barrier(values)


def gather_tensor(shard):
    return gather_near(gather_far(shard))


def gather_far(shard):
    return shard, swap(shard, "tensor", 2)


def gather_near(parts):
    blocks = [parts[0], swap(parts[0], "tensor", 1), parts[1], swap(parts[1], "tensor", 1)]
    return [pltpu.with_memory_space_constraint(block, pltpu.HBM) for block in blocks]


def add_low(one, two):
    return (one.astype(F32) + two.astype(F32)).astype(BF16)


def dp_steps(mine, got, first=0, count=None):
    spot = lax.axis_index("dp") & 1
    half = (mine.shape[0] if count is None else count) // 2

    def cut(array, place):
        return lax.dynamic_slice_in_dim(array, first + place * half, half, 0)

    kept = add_low(cut(mine, spot), cut(got, spot))
    got = yield swap(add_low(cut(mine, 1 - spot), cut(got, 1 - spot)), "dp", 1)
    kept = add_low(kept, got)
    for bit in bits_of("dp")[1:]:
        got = yield swap(kept, "dp", bit)
        kept = add_low(kept, got)
    got = yield swap(kept, "dp", 1)
    return kept, got


def tensor_steps(send, keep):
    got = yield swap(send, "tensor", 1)
    mine = add_low(keep[0], got[0])
    got = yield swap(add_low(keep[1], got[1]), "tensor", 2)
    return mine, got


def reduce_steps(send, keep):
    mine, got = yield from tensor_steps(send, keep)
    return (yield from dp_steps(mine, got))


class Reduction:
    def __init__(self, steps):
        self.steps = steps
        self.flight = next(steps)
        self.result = None

    def advance(self, value):
        value, got = tie(value, self.flight)
        self.send(got)
        return value

    def send(self, got):
        try:
            self.flight = self.steps.send(got)
        except StopIteration as end:
            self.result = end.value

    def finish(self):
        while self.result is None:
            self.send(self.flight)
        return self.result


def pick_matrix():
    pick = np.zeros((WIDE, D), np.float32)
    for column in range(D):
        pick[column // HD * PAD + column % HD, column] = 1.0
    return pick


def body(
    frames, cotangent, lengths, rate_kind, attn_w, attn_m, attn_v, ffin_w, ffin_m, ffin_v,
    ffout_w, ffout_m, ffout_v, convin_w, convin_m, convin_v, convout_w, convout_m, convout_v,
    depth_w, depth_m, depth_v, norm_w, norm_m, norm_v, bn_w, bn_m, bn_v, table_w, table_m, table_v,
):
    rank = lax.axis_index("tensor")
    rank_one = rank.reshape(1).astype(jnp.int32)
    spot_one = (lax.axis_index("dp") & 1).reshape(1).astype(jnp.int32)
    rows = frames.shape[0]
    utts = rows // SLOT
    groups = lax.axis_size("tensor")
    hid = ffin_w.shape[2]
    pick = jnp.asarray(pick_matrix(), BF16)
    pick_wide = jnp.asarray(pick_matrix(), F32)

    attn_w, attn_m, attn_v = (jnp.transpose(a, (2, 0, 1)) for a in (attn_w, attn_m, attn_v))
    ffin_w, ffin_m, ffin_v = (jnp.transpose(a, (1, 0, 2)) for a in (ffin_w, ffin_m, ffin_v))
    ffout_w, ffout_m, ffout_v = (jnp.transpose(a, (1, 0, 2)) for a in (ffout_w, ffout_m, ffout_v))
    convin_w, convin_m, convin_v = (jnp.transpose(a, (2, 0, 1)) for a in (convin_w, convin_m, convin_v))

    pack_one_rows = TAIL + CONV_IN_ROWS
    pack_two_rows = TAIL + PAD
    shards = (attn_w, ffin_w, ffout_w, convin_w, convout_w)
    packs = [((count, WIDE), BF16) for count in (4 * PAD, pack_one_rows, pack_two_rows)]
    attn_low, pack_one, pack_two, chan = call_mixed(
        pack_kernel,
        (),
        (depth_w, bn_w, pick_wide),
        shards,
        packs,
        [((34, 8, WIDE), F32)],
        [(shard.shape, F32) for shard in shards] + packs,
        8,
        4_000_000_000,
    )
    attn_parts = gather_tensor(attn_low)
    attn_parts[2], pack_one = tie(attn_parts[2], pack_one)
    one_pair = gather_far(pack_one)

    rowspec = lead((SLOT, D), 1)
    chanspec = lead((SLOT, WIDE), 1)
    onespec = lead((SLOT, 1), 1)
    normspec = whole((8, D))
    allspec = whole((rows, D))
    turnspec = whole((D, rows))
    statspec = whole((3, WIDE))
    attn_specs = [whole((4 * PAD, WIDE))] * groups
    qkvspec = pl.BlockSpec((None, HEADS, 3 * PAD, SLOT), lambda i: (i, 0, 0, 0))
    mixspec = pl.BlockSpec((None, WIDE, SLOT), lambda i: (i, 0, 0))
    probspec = pl.BlockSpec((None, HEADS, SLOT, SLOT), lambda i: (i, 0, 0, 0))
    row_f32 = ((rows, D), F32)
    one_f32 = ((rows, 1), F32)
    sums_f32 = ((8, D), F32)
    base_low, qkv, probs, mixed, n1, s1, wout = call(
        attn_fwd_kernel,
        utts,
        [SMEM, SMEM, SMEM, turnspec, whole((RATES, D))] + attn_specs + [whole((WIDE, D)), normspec],
        [rowspec, qkvspec, probspec, mixspec, rowspec, onespec, whole((WIDE, D))],
        [
            ((rows, D), BF16),
            ((utts, HEADS, 3 * PAD, SLOT), BF16),
            ((utts, HEADS, SLOT, SLOT), BF16),
            ((utts, WIDE, SLOT), BF16),
            row_f32,
            one_f32,
            ((WIDE, D), BF16),
        ],
        [pltpu.VMEM((rows, D), BF16), pltpu.VMEM((HEADS, 4 * PAD, D), BF16)],
        cost=10_000_000_000,
        limit=56,
        pinned=range(6),
    )(rank_one, lengths, rate_kind, frames.T, table_w, *attn_parts, pick, norm_w)

    row_low = ((rows, D), BF16)
    turn_low = ((D, rows), BF16)
    hid_low = ((groups, rows, hid), BF16)
    chan_f32 = ((rows, WIDE), F32)
    one_rows = (groups, pack_one_rows, WIDE)
    two_rows = (groups, pack_two_rows, WIDE)
    conv_pad = ((8, SPAN, WIDE), F32)
    far, pack_two, n1 = tie(one_pair[1], pack_two, n1)
    one_parts = gather_near((one_pair[0], far))
    two_pair = gather_far(pack_two)
    hid_one, slope_one, n2, s2, value_pre, gate_sig, conv, stat = call_mixed(
        lower_fwd_kernel,
        (rank_one, lengths),
        (norm_w, chan),
        (n1, *one_parts),
        [hid_low, hid_low, row_f32, one_f32, chan_f32, chan_f32, chan_f32],
        [((3, WIDE), F32)],
        [
            row_f32, (one_rows, BF16), hid_low, hid_low, row_f32, one_f32, chan_f32, chan_f32, chan_f32,
            ((HEADS, CONV_IN_ROWS, D), BF16), conv_pad, row_f32, row_low,
        ],
        20,
        18_000_000_000,
        pinned=(2, 3),
    )

    far, stat = tie(two_pair[1], stat)
    two_parts = gather_near((two_pair[0], far))
    stat = combine_all(stat, merge_stats)

    out, grad_three, b_grad, send_one, keep_one, bsums, sums_three, sums_four = call_mixed(
        upper_kernel,
        (rank_one, lengths),
        (norm_w, chan, stat),
        (conv, n2, cotangent.T, *two_parts),
        [turn_low, row_f32, chan_f32] + [((groups // 2, pack_two_rows, WIDE), BF16)] * 2,
        [((8, WIDE), F32), sums_f32, sums_f32],
        [
            chan_f32, row_f32, turn_low, (two_rows, BF16), ((HEADS, PAD, D), BF16),
            ((rows, WIDE), BF16), hid_low, hid_low, row_f32, row_f32, one_f32, row_low, turn_low,
            row_low, turn_low, turn_low, chan_f32, (two_rows, BF16), ((WIDE, D), F32),
        ],
        16,
        30_000_000_000,
    )
    reduce_one = Reduction(reduce_steps(send_one, keep_one))
    bsums = bsums[:2]
    bsums = combine_all(bsums, jnp.add, reduce_one.advance)

    convin_block = (HEADS, CONV_IN_ROWS, D)
    grad_two, cin_grad, vectors = call_mixed(
        conv_bwd_kernel,
        (rank_one, lengths),
        (norm_w, chan, stat, bsums, pick, sums_three, sums_four),
        (b_grad, conv, value_pre, gate_sig, n2, s2, grad_three, *one_parts),
        [row_f32],
        [(convin_block, BF16), ((VECTOR_ROWS, D), BF16)],
        [
            chan_f32, chan_f32, chan_f32, chan_f32, row_f32, one_f32, row_f32,
            ((HEADS, CONV_IN_ROWS, WIDE), BF16), (convin_block, BF16), conv_pad, conv_pad,
            ((SLOT, WIDE), F32), ((SLOT, WIDE), F32), ((2, WIDE, D), F32), ((KERNEL, 8, WIDE), F32),
            sums_f32,
        ],
        16,
        14_000_000_000,
        pinned=(0,),
    )
    grad_two = reduce_one.advance(grad_two)

    lower_rows = (groups, LOWER_ROWS, WIDE)
    pre_one, send_two, keep_two = call_mixed(
        lower_weights_kernel,
        (),
        (norm_w, cin_grad, vectors),
        (grad_two, n1, *one_parts, hid_one, slope_one),
        [hid_low] + [((groups // 2, LOWER_ROWS, WIDE), BF16)] * 2,
        [],
        [
            row_f32, row_f32, ((groups, TAIL, WIDE), BF16), hid_low, hid_low, row_low, turn_low,
            turn_low, (lower_rows, BF16),
        ],
        16,
        12_000_000_000,
    )
    reduce_two = Reduction(tensor_steps(send_two, keep_two))
    pre_one = reduce_one.advance(pre_one)
    grad_one, sums_one = call_mixed(
        lower_bwd_kernel,
        (),
        (norm_w,),
        (grad_two, n1, s1, *one_parts, pre_one),
        [row_f32],
        [sums_f32],
        [row_f32, row_f32, one_f32, ((groups, FF_ROWS, WIDE), BF16), hid_low],
        12,
        8_000_000_000,
    )
    grad_one = reduce_one.advance(grad_one)
    grad_one = reduce_two.advance(grad_one)
    in_grad, attn_send, attn_keep = call(
        attn_bwd_kernel,
        utts,
        [SMEM, SMEM, rowspec] + attn_specs + [whole((WIDE, D)), whole((WIDE, D))]
        + [qkvspec, probspec, mixspec, rowspec, whole((8, D))],
        [turnspec, whole((2, 4 * PAD, WIDE)), whole((2, 4 * PAD, WIDE))],
        [((D, rows), F32)] + [((2, 4 * PAD, WIDE), BF16)] * 2,
        [
            pltpu.VMEM((HEADS, 3 * PAD, D), F32),
            pltpu.VMEM((WIDE, D), F32),
            pltpu.VMEM((rows, D), F32),
            pltpu.VMEM((8, D), F32),
            pltpu.VMEM((HEADS, 3 * PAD, D), BF16),
        ],
        cost=16_000_000_000,
    )(
        rank_one, rate_kind, base_low, *attn_parts, wout, pick, qkv, probs, mixed, grad_one, sums_one,
    )
    attn_send = reduce_one.advance(attn_send)
    attn_send = reduce_two.advance(attn_send)
    reduce_attn = Reduction(reduce_steps(attn_send, attn_keep))
    mine, got = reduce_two.result
    reduce_down = Reduction(dp_steps(mine, got, 0, LOWER_SPLIT))
    reduce_up = Reduction(dp_steps(mine, got, LOWER_SPLIT, LOWER_ROWS - LOWER_SPLIT))
    token = bsums
    chains = (reduce_attn, reduce_down, reduce_up, reduce_down, reduce_attn, reduce_up, reduce_attn)
    for chain in chains + (reduce_one, reduce_down, reduce_attn, reduce_up, reduce_down):
        token = chain.advance(token)
    one_halves = reduce_one.finish()
    down_halves = reduce_down.finish()

    def like(*arrays):
        return [(a.shape, F32) for a in arrays]

    down = call_whole(
        lamb_down_kernel,
        (spot_one,),
        (*one_halves, *down_halves, ffout_w, ffout_m, ffout_v, convout_w, convout_m, convout_v),
        like(*[ffout_w] * 3, *[convout_w] * 3)
        + [((D, D), F32), ((VECTOR_ROWS, D), F32), ((32, 128), F32)],
        [
            pltpu.VMEM((pack_two_rows, WIDE), F32),
            pltpu.VMEM((LOWER_SPLIT, WIDE), F32),
            pltpu.VMEM(ffout_w.shape, F32),
        ],
    )
    token = reduce_attn.advance(tie(token, down[8])[0])
    token = reduce_up.advance(token)
    up_halves = reduce_up.finish()
    while reduce_attn.result is None:
        token = reduce_attn.advance(token)
    up = call_whole(
        lamb_up_kernel,
        (spot_one,),
        (*up_halves, down[6], ffin_w, ffin_m, ffin_v, convin_w, convin_m, convin_v),
        like(*[ffin_w] * 3, *[convin_w] * 3) + [((32, 128), F32)],
        [
            pltpu.VMEM((LOWER_ROWS - LOWER_SPLIT, WIDE), F32),
            pltpu.VMEM(ffin_w.shape, F32),
            pltpu.VMEM(convin_w.shape, F32),
        ],
    )
    attn_halves = reduce_attn.result
    small = (depth_w, depth_m, depth_v, norm_w, norm_m, norm_v, bn_w, bn_m, bn_v, table_w, table_m, table_v)
    last = call_whole(
        functools.partial(lamb_attn_kernel, 1.0 / groups),
        (spot_one,),
        (*attn_halves, down[7], bsums, pick_wide, attn_w, attn_m, attn_v) + small,
        like(attn_w) + [((3, HD, D), F32), ((HD, D), F32)] + like(attn_w, *small) + [((32, 128), F32)],
        [pltpu.VMEM((4 * PAD, WIDE), F32), pltpu.VMEM(attn_w.shape, F32)],
    )
    squares = down[8] + up[6] + last[16]
    for bit in bits_of("tensor"):
        squares = squares + swap(squares, "tensor", bit)
    matrices = (ffin_w, ffout_w, attn_w, convin_w, convout_w)
    moves = (up[2], down[2], last[3], up[5], down[5])
    ffin_new, ffout_new, attn_new, convin_new, convout_new, weight_norms, update_norms = call_mixed(
        step_kernel,
        (),
        (squares, *matrices),
        moves,
        like(*matrices),
        [((1, 12), F32)] * 2,
        like(*matrices),
        10,
        1_000_000,
        limit=14,
    )

    def back_chan(array):
        return jnp.transpose(array, (1, 2, 0))

    def back_mid(array):
        return jnp.transpose(array, (1, 0, 2))

    small_new = last[4:16]
    return (
        out.T,
        in_grad.T,
        back_chan(attn_new),
        back_chan(last[0]),
        jnp.transpose(last[1], (0, 2, 1)),
        last[2].T,
        back_mid(ffin_new),
        back_mid(up[0]),
        back_mid(up[1]),
        back_mid(ffout_new),
        back_mid(down[0]),
        back_mid(down[1]),
        back_chan(convin_new),
        back_chan(up[3]),
        back_chan(up[4]),
        convout_new,
        down[3],
        down[4],
        *small_new,
        weight_norms.reshape(12),
        update_norms.reshape(12),
    )


def solution(mesh):
    rows = P(("dp", "tensor"), None)
    last = P(None, None, "tensor")
    mid = P(None, "tensor", None)
    first = P("tensor", None)
    placed = (rows, rows, P("dp"), P("dp")) + (last,) * 6 + (mid,) * 3 + (last,) * 3 + (first,) * 3
    results = (rows, rows) + (last,) * 3 + (P(None, "tensor"),) + (last,) * 3 + (mid,) * 3
    return jax.shard_map(
        body,
        mesh=mesh,
        in_specs=placed + (P(),) * 12,
        out_specs=results + (last,) * 3 + (first,) * 3 + (P(),) * 14,
        check_vma=False,
    )
```

```python
import functools
import math

import jax
import jax.numpy as jnp
import numpy as np
from jax import lax
from jax.experimental import pallas as pl
from jax.experimental.pallas import tpu as pltpu
from jax.sharding import PartitionSpec as P

D = 324
HEADS = 4
KERNEL = 31
HALF = KERNEL // 2
RATES = 3
STEP = 10
SLOT = 496
HD = 81
PAD = 96
WIDE = HEADS * PAD
FF_ROWS = 336
TAIL = 2 * FF_ROWS
CONV_IN_ROWS = 2 * PAD
VECTOR_ROWS = 48
LOWER_VEC = FF_ROWS
LOWER_SPLIT = FF_ROWS + VECTOR_ROWS
LOWER_UP = LOWER_SPLIT
LOWER_CONV = LOWER_UP + FF_ROWS
LOWER_ROWS = LOWER_CONV + CONV_IN_ROWS + 16

EPS_NORM = 1e-05
BETA_ONE = 0.9
BETA_TWO = 0.999
ADAM_EPS = 1e-06
WEIGHT_DECAY = 0.01
RATE_MATRIX = 0.3
RATE_VECTOR = 0.5
MASK_FILL = -1e30
SCALE = 1.0 / math.sqrt(HD)
PRECISE = lax.Precision.HIGHEST

F32 = jnp.float32
BF16 = jnp.bfloat16
LEAD = 16
SPAN = 544


def dot_nn(left, right):
    return lax.dot_general(left, right, (((1,), (0,)), ((), ())), preferred_element_type=F32)


def dot_nt(left, right):
    return lax.dot_general(left, right, (((1,), (1,)), ((), ())), preferred_element_type=F32)


def dot_tn(left, right):
    return lax.dot_general(left, right, (((0,), (0,)), ((), ())), preferred_element_type=F32)


def sigmoid(value):
    return 0.5 * jnp.tanh(0.5 * value) + 0.5


def ln_forward(resid):
    center = resid - jnp.mean(resid, axis=-1, keepdims=True)
    inv = lax.rsqrt(jnp.mean(center * center, axis=-1, keepdims=True) + EPS_NORM)
    return center * inv, inv


def ln_backward(upstream, normal, inv, gain):
    scaled = upstream * gain
    grad = inv * (
        scaled
        - jnp.mean(scaled, axis=-1, keepdims=True)
        - normal * jnp.mean(scaled * normal, axis=-1, keepdims=True)
    )
    gain_sum = jnp.sum(upstream * normal, axis=0, keepdims=True)
    shift_sum = jnp.sum(upstream, axis=0, keepdims=True)
    return grad, gain_sum, shift_sum


def put_sums(ref, first, gain_sum, shift_sum):
    @pl.when(first)
    def _():
        ref[...] = jnp.zeros_like(ref)

    ref[0:1, :] += gain_sum
    ref[1:2, :] += shift_sum


def valid_rows(count):
    return lax.broadcasted_iota(jnp.int32, (SLOT, 1), 0) < count


FOLD = (False, False, False)


def assemble(scratch, parts, rank, first, count):
    for place, part in enumerate(parts):
        scratch[place ^ rank] = part[first : first + count, 0:D]


def attn_fwd_kernel(
    rank_ref, len_ref, kind_ref, frames, table, w0, w1, w2, w3, pick, norm,
    low_out, qkv_out, prob_out, mixed_out, n1_out, s1_out, wout_out, low_rows, weights,
):
    utt = pl.program_id(0)
    rank = rank_ref[0]
    which = rank * pl.num_programs(0) + utt

    @pl.when(utt == 0)
    def _():
        assemble(weights, (w0, w1, w2, w3), rank, 0, 4 * PAD)
        turned = jnp.concatenate([weights[t, 3 * PAD :, :] for t in range(HEADS)], axis=0)
        spaced = dot_nt(pick[...], turned).astype(BF16)
        wout_out[...] = dot_nn(spaced, pick[...]).astype(BF16)
        low_rows[...] = frames[...].T

    base = low_rows[pl.ds(utt * SLOT, SLOT), :].astype(F32) + table[pl.ds(kind_ref[which], 1), :]
    base_low = base.astype(BF16)
    low_out[...] = base_low
    valid = valid_rows(len_ref[which])

    def project(head):
        qkv = dot_nt(weights[head, 0 : 3 * PAD, :], base_low).astype(BF16)
        qkv_out[head] = qkv
        return qkv, dot_tn(qkv[PAD : 2 * PAD], qkv[:PAD])

    later = project(0)
    for head in range(HEADS):
        qkv, products = later
        if head + 1 < HEADS:
            later = project(head + 1)
        scores = jnp.where(valid, products * SCALE, MASK_FILL)
        top = jnp.max(scores, axis=0, keepdims=True)
        expo = jnp.exp(scores - top)
        total = jnp.sum(expo, axis=0, keepdims=True)
        probs = (expo * (1.0 / total)).astype(BF16)
        prob_out[head] = probs
        mixed_out[head * PAD : (head + 1) * PAD, :] = dot_nn(qkv[2 * PAD :], probs).astype(BF16)
    attn_out = dot_tn(mixed_out[...], wout_out[...])
    normal, inv = ln_forward(base + attn_out)
    n1_out[...] = normal
    s1_out[...] = inv


def shifted(scratch):
    for shift in range(1, 8):
        scratch[shift, 0 : SPAN - 8, :] = scratch[0, pl.ds(shift, SPAN - 8), :]


def load_padded(scratch, signal):
    scratch[0, 0:LEAD, :] = jnp.zeros((LEAD, WIDE), F32)
    scratch[0, pl.ds(LEAD + SLOT, SPAN - LEAD - SLOT), :] = jnp.zeros((SPAN - LEAD - SLOT, WIDE), F32)
    scratch[0, pl.ds(LEAD, SLOT), :] = signal
    shifted(scratch)


LANES = 128
BLOCKS = ((0, 128), (128, 128), (256, 128), (384, 112))


def depth_tiles(body_fn):
    for row, count in BLOCKS:
        for tile in range(WIDE // LANES):
            body_fn(row, count, slice(tile * LANES, (tile + 1) * LANES))


def depth_sum(padded, row_of, chan, put):
    def block(row, count, lanes):
        total = jnp.zeros((count // 8, 8, LANES), F32)
        for shift in range(8):
            rows = padded[shift, pl.ds(row, count + 24), lanes]
            for lift in range(4):
                place = 8 * lift + shift
                if 1 <= place <= KERNEL:
                    tap = row_of(place)
                    part = rows[8 * lift : 8 * lift + count].reshape(count // 8, 8, LANES)
                    total = total + part * chan[tap, :, lanes][None]
        put(row, count, lanes, total.reshape(count, LANES))

    depth_tiles(block)


def depth_products(padded, own, sums):
    def block(row, count, lanes):
        mine = own[pl.ds(row, count), lanes]
        for shift in range(8):
            rows = padded[shift, pl.ds(row, count + 24), lanes]
            for lift in range(4):
                place = 8 * lift + shift
                if 1 <= place <= KERNEL:
                    part = rows[8 * lift : 8 * lift + count] * mine
                    part = jnp.sum(part.reshape(count // 8, 8, LANES), axis=0)
                    sums[place - 1, :, lanes] += part

    depth_tiles(block)


def merge_stats(one, two):
    mean_one, dev_one, count_one = one[0:1], one[1:2], one[2:3]
    mean_two, dev_two, count_two = two[0:1], two[1:2], two[2:3]
    count = count_one + count_two
    mean = (mean_one * count_one + mean_two * count_two) / count
    gap = mean_one - mean_two
    dev = dev_one + dev_two + gap * gap * (count_one * count_two / count)
    return jnp.concatenate([mean, dev, count], axis=0)


def bn_parts(conv, stat, chan):
    inv = lax.rsqrt(stat[1:2, :] / stat[2:3, :] + EPS_NORM)
    normal = (conv - stat[0:1, :]) * inv
    return normal, inv, normal * chan[32, 0:1, :] + chan[33, 0:1, :]


def utt_rows(utt):
    return pl.ds(pl.multiple_of(utt * SLOT, 16), SLOT)


def each_utt(rows, body_fn):
    def step(utt, carry):
        body_fn(utt, utt_rows(utt))
        return carry

    lax.fori_loop(0, rows // SLOT, step, 0)


class Copies:
    def __init__(self, sems):
        self.sems = sems
        self.count = 0
        self.open = []

    def start(self, source, target):
        copy = pltpu.make_async_copy(source, target, self.sems.at[self.count])
        self.count += 1
        copy.start()
        return copy

    def out(self, source, target):
        self.open.append(self.start(source, target))

    def finish(self):
        for copy in self.open:
            copy.wait()


def attn_pack_kernel(attn_in, out, attn, low, sems):
    copies = Copies(sems)
    load = copies.start(attn_in, attn)
    low[...] = jnp.zeros_like(low)
    load.wait()
    for j in range(4):
        low[j * PAD : j * PAD + HD, 0:D] = attn[:, j, :].astype(BF16)
    copies.out(low, out)
    copies.finish()


def rest_pack_kernel(
    depth, bn, pick, ffin_in, ffout_in, convin_in, convout_in, one_out, two_out, chan_out,
    ffin, ffout, convin, convout, one, two, sems,
):
    copies = Copies(sems)
    pairs = (ffin_in, ffin), (ffout_in, ffout), (convin_in, convin), (convout_in, convout)
    loads = [copies.start(source, target) for source, target in pairs]

    def spread(rows):
        return lax.dot_general(
            rows, pick[...], (((1,), (1,)), ((), ())), precision=PRECISE, preferred_element_type=F32
        )

    for first, rows in ((0, spread(depth[...])), (32, spread(bn[...]))):
        count = rows.shape[0]
        chan_out[first : first + count] = jnp.broadcast_to(rows[:, None, :], (count, 8, WIDE))
    for out in (one, two):
        out[...] = jnp.zeros_like(out)
    for load in loads:
        load.wait()
    for j, out in ((0, one), (1, two)):
        out[0:D, 0:D] = ffin[:, j, :].astype(BF16)
        out[FF_ROWS : FF_ROWS + D, 0:D] = ffout[:, j, :].astype(BF16)
    for j in range(2):
        one[TAIL + j * PAD : TAIL + j * PAD + HD, 0:D] = convin[:, j, :].astype(BF16)
    two[TAIL : TAIL + HD, 0:D] = convout[...].astype(BF16)
    copies.out(one, one_out)
    copies.out(two, two_out)
    copies.finish()


def ffn_forward(z_low, weights, hid, slope, acc, done=None):
    def block(p, carry):
        pre = dot_nn(z_low[...], weights[p, 0:D, 0:D])
        sig = sigmoid(pre)
        hidden = pre * sig
        hid_low = hidden.astype(BF16)
        hid[p] = hid_low
        slope[p] = (sig + hidden * (1.0 - sig)).astype(BF16)
        acc[...] += dot_nn(hid_low, weights[p, FF_ROWS : FF_ROWS + D, 0:D])
        return carry

    if done is None:
        lax.fori_loop(0, HEADS, block, 0)
    else:
        for p in range(HEADS):
            block(p, 0)
            done(p)


def ffn_backward(up_low, up_turn, z_turn, weights, hid, slope, acc, grads, up_row, down_row, done=None):
    def block(p, carry):
        back = dot_nt(up_low[...], weights[p, FF_ROWS : FF_ROWS + D, 0:D])
        pre_grad = (back * slope[p].astype(F32)).astype(BF16)
        grads[p, down_row : down_row + D, 0:D] = dot_nn(up_turn[...], hid[p]).astype(BF16)
        grads[p, up_row : up_row + D, 0:D] = dot_nn(z_turn[...], pre_grad).astype(BF16)
        if acc is None:
            slope[p] = pre_grad
        else:
            acc[...] += dot_nt(pre_grad, weights[p, 0:D, 0:D])
        return carry

    if done is None:
        lax.fori_loop(0, HEADS, block, 0)
    else:
        for p in range(HEADS):
            block(p, 0)
            done(p)


def send_out(copies, grads, send, keep):
    for i in range(HEADS // 2):
        copies.out(grads.at[2 * i + 1], send.at[i])
        copies.out(grads.at[2 * i], keep.at[i])


def lower_fwd_kernel(
    rank_ref, len_ref, norm, chan, n1_in, w0, w1, w2, w3,
    hid_out, slope_out, n2_out, s2_out, value_out, sig_out, conv_out, stat_out,
    n1, weights, hid, slope, n2, s2, value, sig, conv, conv_w, padded, acc, z_low, sems,
):
    copies = Copies(sems)
    rank = rank_ref[0]
    rows = n1_in.shape[0]
    loads = [copies.start(n1_in, n1)]
    loads += [copies.start(part, weights.at[p]) for p, part in enumerate((w0, w1, w2, w3))]
    for load in loads:
        load.wait()
    z = n1[...] * norm[0:1, :] + norm[4:5, :]
    acc[...] = z
    z_low[...] = z.astype(BF16)

    def done(p):
        copies.out(hid.at[p], hid_out.at[p])
        copies.out(slope.at[p], slope_out.at[p])

    ffn_forward(z_low, weights, hid, slope, acc, done)
    normal, inv = ln_forward(acc[...])
    n2[...] = normal
    s2[...] = inv
    copies.out(n2, n2_out)
    copies.out(s2, s2_out)
    z_low[...] = (normal * norm[1:2, :] + norm[5:6, :]).astype(BF16)
    for p in range(HEADS):
        conv_w[p ^ rank] = weights[p, TAIL : TAIL + CONV_IN_ROWS, 0:D]
    value[...] = dot_nt(z_low[...], conv_w[:, 0:PAD, :].reshape(WIDE, D))
    copies.out(value, value_out)
    sig[...] = sigmoid(dot_nt(z_low[...], conv_w[:, PAD:, :].reshape(WIDE, D)))
    copies.out(sig, sig_out)
    utts = rows // SLOT

    def utterance(utt, here):
        count = len_ref[rank * utts + utt]
        valid = valid_rows(count).astype(F32)
        load_padded(padded, value[here, :] * sig[here, :] * valid)

        def put(row, number, lanes, total):
            conv[pl.ds(pl.multiple_of(utt * SLOT + row, 16), number), lanes] = total

        depth_sum(padded, lambda place: place - 1, chan, put)
        own = conv[here, :]
        number = count.astype(F32)
        mean = jnp.sum(own * valid, axis=0, keepdims=True) / number
        center = (own - mean) * valid
        dev = jnp.sum(center * center, axis=0, keepdims=True)
        stat = jnp.concatenate([mean, dev, jnp.zeros_like(mean) + number], axis=0)

        @pl.when(utt == 0)
        def _():
            stat_out[...] = stat

        @pl.when(utt > 0)
        def _():
            stat_out[...] = merge_stats(stat_out[...], stat)

    each_utt(rows, utterance)
    copies.out(conv, conv_out)
    copies.finish()


def upper_kernel(
    rank_ref, len_ref, norm, chan, stat, conv_in, n2_in, cot_in, w0, w1, w2, w3,
    out_out, grad_out, b_out, send, keep, bsums, sums_three, sums_four,
    conv, n2, cot, weights, conv_w, act, hid, slope, acc, n3, s3, z_low, z_turn, up_low, up_turn,
    out, b_grad, grads, conv_acc, sems,
):
    copies = Copies(sems)
    rank = rank_ref[0]
    rows = conv_in.shape[0]
    utts = rows // SLOT
    loads = [copies.start(part, weights.at[p]) for p, part in enumerate((w0, w1, w2, w3))]
    loads += [copies.start(conv_in, conv), copies.start(n2_in, n2)]
    cot_load = copies.start(cot_in, cot)
    for load in loads:
        load.wait()
    for p in range(HEADS):
        conv_w[p ^ rank] = weights[p, TAIL : TAIL + PAD, 0:D]
    bsums[...] = jnp.zeros_like(bsums)
    sums_three[...] = jnp.zeros_like(sums_three)
    sums_four[...] = jnp.zeros_like(sums_four)
    conv_acc[...] = jnp.zeros_like(conv_acc)

    def utterance_fwd(utt, here):
        _, _, bn_out = bn_parts(conv[here, :], stat, chan)
        act_low = (bn_out * sigmoid(bn_out)).astype(BF16)
        act[here, :] = act_low
        second = n2[here, :] * norm[1:2, :] + norm[5:6, :]
        normal, inv = ln_forward(second + dot_nn(act_low, conv_w[...].reshape(WIDE, D)))
        n3[here, :] = normal
        s3[here, :] = inv
        z = normal * norm[2:3, :] + norm[6:7, :]
        acc[here, :] = z
        z_low[here, :] = z.astype(BF16)

    each_utt(rows, utterance_fwd)
    z_turn[...] = z_low[...].T
    ffn_forward(z_low, weights, hid, slope, acc)
    normal, inv = ln_forward(acc[...])
    gain = norm[3:4, :]
    out[...] = (normal * gain + norm[7:8, :]).astype(BF16).T
    copies.out(out, out_out)
    cot_load.wait()
    valid = jnp.concatenate([valid_rows(len_ref[rank * utts + u]) for u in range(utts)], axis=0)
    upstream = jnp.where(valid, cot[...].T.astype(F32), 0.0)
    grad, gain_sum, shift_sum = ln_backward(upstream, normal, inv, gain)
    sums_four[0:1, :] = gain_sum
    sums_four[1:2, :] = shift_sum
    acc[...] = grad
    up_low[...] = grad.astype(BF16)
    up_turn[...] = up_low[...].T
    ffn_backward(up_low, up_turn, z_turn, weights, hid, slope, acc, grads, 0, FF_ROWS)
    grad, gain_sum, shift_sum = ln_backward(acc[...], n3[...], s3[...], norm[2:3, :])
    sums_three[0:1, :] = gain_sum
    sums_three[1:2, :] = shift_sum
    acc[...] = grad
    copies.out(acc, grad_out)
    up_low[...] = grad.astype(BF16)

    def utterance_bwd(utt, here):
        normal, _, bn_out = bn_parts(conv[here, :], stat, chan)
        sig = sigmoid(bn_out)
        low = up_low[here, :]
        own = dot_nt(low, conv_w[...].reshape(WIDE, D)) * (sig * (1.0 + bn_out * (1.0 - sig)))
        b_grad[here, :] = own
        bsums[0:1, :] += jnp.sum(own * normal, axis=0, keepdims=True)
        bsums[1:2, :] += jnp.sum(own, axis=0, keepdims=True)
        conv_acc[...] += dot_tn(act[here, :], low)

    each_utt(rows, utterance_bwd)
    copies.out(b_grad, b_out)
    for t in range(HEADS):
        place = t ^ rank
        grads[place, TAIL : TAIL + PAD, 0:D] = conv_acc[t * PAD : (t + 1) * PAD, :].astype(BF16)
    send_out(copies, grads, send, keep)
    copies.finish()


def conv_bwd_kernel(
    rank_ref, len_ref, norm, chan, stat, bsums, pick, sums_three, sums_four,
    b_in, conv_in, value_in, sig_in, n2_in, s2_in, grad_in, w0, w1, w2, w3,
    grad_out, wgrad_out, vec_out,
    b_grad, conv, value, sig, n2, s2, grad, parts, weights, glu_pad, cg_pad, cg_ref, gg_ref,
    conv_acc, tap_sums, sums_ref, sems,
):
    copies = Copies(sems)
    rank = rank_ref[0]
    rows = b_in.shape[0]
    utts = rows // SLOT
    first = pl.ds(0, SLOT)
    pairs = [(value_in, value), (sig_in, sig), (conv_in, conv), (b_in, b_grad)]
    loads = [copies.start(source.at[first], target.at[first]) for source, target in pairs]
    others = pl.ds(SLOT, rows - SLOT)
    later = [copies.start(source.at[others], target.at[others]) for source, target in pairs]
    later += [copies.start(n2_in, n2), copies.start(s2_in, s2), copies.start(grad_in, grad)]
    later += [
        copies.start(part.at[pl.ds(TAIL, CONV_IN_ROWS)], parts.at[p])
        for p, part in enumerate((w0, w1, w2, w3))
    ]
    tap_sums[...] = jnp.zeros_like(tap_sums)
    conv_acc[...] = jnp.zeros_like(conv_acc)
    sums_ref[...] = jnp.zeros_like(sums_ref)
    for load in loads:
        load.wait()

    def utterance(utt, here):
        valid = valid_rows(len_ref[rank * utts + utt]).astype(F32)
        gain = chan[32, 0:1, :]
        count = stat[2:3, :]
        load_padded(glu_pad, value[here, :] * sig[here, :] * valid)
        normal, inv, _ = bn_parts(conv[here, :], stat, chan)
        conv_grad = (valid * inv) * (
            b_grad[here, :] * gain
            - gain * (bsums[1:2, :] / count)
            - normal * (gain * (bsums[0:1, :] / count))
        )
        cg_ref[...] = conv_grad
        load_padded(cg_pad, conv_grad)
        depth_products(glu_pad, cg_ref, tap_sums)

        def put(row, number, lanes, total):
            gg_ref[pl.ds(row, number), lanes] = total

        depth_sum(cg_pad, lambda place: KERNEL - place, chan, put)

        @pl.when(utt == 0)
        def _():
            for load in later:
                load.wait()
            for p in range(HEADS):
                weights[p ^ rank] = parts[p, :, 0:D]

        glu_grad = gg_ref[...] * valid
        sig_now = sig[here, :]
        value_grad = (glu_grad * sig_now).astype(BF16)
        gate_grad = (glu_grad * value[here, :] * sig_now * (1.0 - sig_now)).astype(BF16)
        normal = n2[here, :]
        z_low = (normal * norm[1:2, :] + norm[5:6, :]).astype(BF16)
        conv_acc[0] += dot_tn(value_grad, z_low)
        conv_acc[1] += dot_tn(gate_grad, z_low)
        upstream = (
            grad[here, :]
            + dot_nn(value_grad, weights[:, 0:PAD, :].reshape(WIDE, D))
            + dot_nn(gate_grad, weights[:, PAD:, :].reshape(WIDE, D))
        )
        own, gain_sum, shift_sum = ln_backward(upstream, normal, s2[here, :], norm[1:2, :])
        grad[here, :] = own
        sums_ref[0:1, :] += gain_sum
        sums_ref[1:2, :] += shift_sum

    each_utt(rows, utterance)
    copies.out(grad, grad_out)
    for t in range(HEADS):
        for j in range(2):
            part = conv_acc[j, t * PAD : (t + 1) * PAD, :].astype(BF16)
            wgrad_out[t ^ rank, j * PAD : (j + 1) * PAD, :] = part
    taps = jnp.sum(tap_sums[...], axis=1).astype(BF16)
    vec = [dot_nn(taps, pick[...]), jnp.zeros((1, D), F32)]
    vec += [sums_ref[0:2, :], sums_three[0:2, :], sums_four[0:2, :]]
    vec += [jnp.zeros((VECTOR_ROWS - 38, D), F32)]
    vec_out[...] = jnp.concatenate(vec, axis=0).astype(BF16)
    copies.finish()


def lower_weights_kernel(
    norm, cin_grad, vectors, up_in, n1_in, w0, w1, w2, w3, hid_in, slope_in,
    pre_out, send, keep,
    up, n1, weights, hid, slope, up_low, up_turn, z_turn, grads, sems,
):
    copies = Copies(sems)
    loads = [copies.start(up_in, up), copies.start(n1_in, n1)]
    down = pl.ds(FF_ROWS, FF_ROWS)
    loads += [
        copies.start(part.at[down], weights.at[p, down]) for p, part in enumerate((w0, w1, w2, w3))
    ]
    loads += [copies.start(slope_in, slope), copies.start(hid_in, hid)]
    for load in loads[:2]:
        load.wait()
    up_low[...] = up[...].astype(BF16)
    up_turn[...] = up_low[...].T
    z_turn[...] = (n1[...] * norm[0:1, :] + norm[4:5, :]).astype(BF16).T
    for load in loads[2:]:
        load.wait()

    def done(p):
        copies.out(slope.at[p], pre_out.at[p])

    ffn_backward(up_low, up_turn, z_turn, weights, hid, slope, None, grads, LOWER_UP, 0, done)
    for p in range(HEADS):
        grads[p, LOWER_CONV : LOWER_CONV + CONV_IN_ROWS, 0:D] = cin_grad[p]
        grads[p, LOWER_VEC : LOWER_VEC + VECTOR_ROWS, 0:D] = vectors[...]
    send_out(copies, grads, send, keep)
    copies.finish()


def lower_bwd_kernel(
    norm, up_in, n1_in, s1_in, w0, w1, w2, w3, pre_in, grad_out, sums_one,
    acc, n1, s1, weights, pre, sems,
):
    copies = Copies(sems)
    up_rows = pl.ds(0, FF_ROWS)
    loads = [copies.start(up_in, acc)]
    for p, part in enumerate((w0, w1, w2, w3)):
        loads += [copies.start(part.at[up_rows], weights.at[p]), copies.start(pre_in.at[p], pre.at[p])]
    late = [copies.start(n1_in, n1), copies.start(s1_in, s1)]
    loads[0].wait()
    for p in range(HEADS):
        loads[2 * p + 1].wait()
        loads[2 * p + 2].wait()
        acc[...] += dot_nt(pre[p], weights[p, 0:D, 0:D])
    for load in late:
        load.wait()
    grad, gain_sum, shift_sum = ln_backward(acc[...], n1[...], s1[...], norm[0:1, :])
    acc[...] = grad
    copies.out(acc, grad_out)
    sums_one[...] = jnp.zeros_like(sums_one)
    sums_one[0:1, :] = gain_sum
    sums_one[1:2, :] = shift_sum
    copies.finish()


def attn_bwd_kernel(
    rank_ref, kind_ref, low_in, w0, w1, w2, w3, wout, pick, qkv_in, probs_in, mixed, grad, sums_one,
    grad_out, send, keep, acc, acc_out, rows_out, table_sums, weights,
):
    utt = pl.program_id(0)
    rank = rank_ref[0]

    @pl.when(utt == 0)
    def _():
        assemble(weights, (w0, w1, w2, w3), rank, 0, 3 * PAD)
        acc[...] = jnp.zeros_like(acc)
        acc_out[...] = jnp.zeros_like(acc_out)
        table_sums[...] = jnp.zeros_like(table_sums)

    base_low = low_in[...]
    upstream = grad[...]
    up_low = upstream.astype(BF16)
    mixed_grad = dot_nt(wout[...], up_low).astype(BF16)

    def up_head(head):
        return mixed_grad[head * PAD : (head + 1) * PAD, :]

    def prob_product(head):
        return dot_tn(qkv_in[head, 2 * PAD :, :], up_head(head))

    later = prob_product(0)
    acc_out[...] += dot_nn(mixed[...], up_low)
    total = upstream
    waiting = None
    for head in range(HEADS + 1):
        if head < HEADS:
            prob_grad = later
            if head + 1 < HEADS:
                later = prob_product(head + 1)
            probs_low = probs_in[head]
            probs = probs_low.astype(F32)
            delta = jnp.sum(prob_grad * probs, axis=0, keepdims=True)
            score_grad = (probs * (prob_grad - delta)).astype(BF16)
        if waiting is not None:
            acc[head - 1] += dot_nn(waiting, base_low)
            total = total + dot_tn(waiting, weights[head - 1])
        if head < HEADS:
            queries = qkv_in[head, 0:PAD, :]
            keys = qkv_in[head, PAD : 2 * PAD, :]
            value_grad = dot_nt(up_head(head), probs_low).astype(BF16)
            query_grad = (dot_nn(keys, score_grad) * SCALE).astype(BF16)
            key_grad = (dot_nt(queries, score_grad) * SCALE).astype(BF16)
            waiting = jnp.concatenate([query_grad, key_grad, value_grad], axis=0)
    rows_out[pl.ds(utt * SLOT, SLOT), :] = total
    column = jnp.sum(total, axis=0, keepdims=True)
    kind = kind_ref[rank * pl.num_programs(0) + utt]
    place = lax.broadcasted_iota(jnp.int32, table_sums.shape, 0)
    table_sums[...] += jnp.where(place == kind, column, 0.0)

    @pl.when(utt == pl.num_programs(0) - 1)
    def _():
        grad_out[...] = rows_out[...].T
        turned = dot_nt(pick[...], acc_out[...].astype(BF16)).astype(BF16)
        turned = dot_nn(turned, pick[...]).astype(BF16)
        extra = [table_sums[0:RATES, :], sums_one[0:2, :]]
        extra += [jnp.zeros((PAD - HD - RATES - 2, D), F32)]
        extra = jnp.concatenate(extra, axis=0).astype(BF16)
        rows_out[0:WIDE, :] = turned.astype(F32)
        for place in range(HEADS):
            t = place ^ rank
            out = send if place % 2 else keep
            out[place // 2, 0 : 3 * PAD, 0:D] = acc[t].astype(BF16)
            out[place // 2, HD:PAD, 0:D] = extra
            block = rows_out[pl.ds(pl.multiple_of(t * PAD, PAD), PAD), :]
            out[place // 2, 3 * PAD :, 0:D] = block.astype(BF16)


def adam_step(first, second, grad_full):
    first_new = BETA_ONE * first + (1.0 - BETA_ONE) * grad_full
    second_new = BETA_TWO * second + (1.0 - BETA_TWO) * grad_full * grad_full
    scaled = jnp.maximum(second_new * (1.0 / (1.0 - BETA_TWO**STEP)), 1e-30)
    below = scaled * lax.rsqrt(scaled) + ADAM_EPS
    inverse = pl.reciprocal(below, approx=True)
    inverse = inverse * (2.0 - below * inverse)
    direction = (first_new * (1.0 / (1.0 - BETA_ONE**STEP))) * inverse
    return (first_new, second_new, direction)


def total_of(array):
    return jnp.sum(jnp.sum(array, axis=1, keepdims=True), axis=0, keepdims=True)


def put_squares(sums_out, row, own, direction):
    if own.ndim == 3:
        own = jnp.sum(own * own, axis=0)
        direction = jnp.sum(direction * direction, axis=0)
        count = own.shape[0]
    else:
        own = jnp.sum(own * own, axis=0, keepdims=True)
        direction = jnp.sum(direction * direction, axis=0, keepdims=True)
        count = 1
    sums_out[row : row + count, :] = jnp.broadcast_to(
        jnp.sum(own, axis=1, keepdims=True), (count, 128)
    )
    sums_out[16 + row : 16 + row + count, :] = jnp.broadcast_to(
        jnp.sum(direction, axis=1, keepdims=True), (count, 128)
    )


def join_halves(spot, mine, other, scratch):
    half = mine.shape[0]
    scratch[pl.ds(pl.multiple_of(spot * half, 16), half), :] = mine[...].astype(F32)
    scratch[pl.ds(pl.multiple_of((1 - spot) * half, 16), half), :] = other[...].astype(F32)


def lamb_stack(weight, first, second, grads, stacked, sums_out, row):
    for j, grad in enumerate(grads):
        stacked[:, j, :] = grad
    own = weight[...]
    first_new, second_new, direction = adam_step(first[...], second[...], stacked[...])
    direction = direction + WEIGHT_DECAY * own
    put_squares(sums_out, row, own, direction)
    return first_new, second_new, direction


def lamb_down_kernel(
    spot_ref, one_mine, one_other, two_mine, two_other, fout_w, fout_m, fout_v, cout_w, cout_m, cout_v,
    fout_mo, fout_vo, fout_u, cout_mo, cout_vo, cout_u, fin_grad, vec_out, sums_out, one, two, wide,
):
    spot = spot_ref[0]
    join_halves(spot, one_mine, one_other, one)
    join_halves(spot, two_mine, two_other, two)
    sums_out[...] = jnp.zeros_like(sums_out)
    fin_grad[...] = one[0:D, 0:D]
    vec_out[...] = two[FF_ROWS : FF_ROWS + VECTOR_ROWS, 0:D]
    grads = (two[0:D, 0:D].T, one[FF_ROWS : FF_ROWS + D, 0:D].T)
    fout_mo[...], fout_vo[...], fout_u[...] = lamb_stack(
        fout_w, fout_m, fout_v, grads, wide, sums_out, 6
    )
    own = cout_w[...]
    grad = one[TAIL : TAIL + HD, 0:D]
    first_new, second_new, direction = adam_step(cout_m[...], cout_v[...], grad)
    direction = direction + WEIGHT_DECAY * own
    cout_mo[...], cout_vo[...], cout_u[...] = first_new, second_new, direction
    put_squares(sums_out, 10, own, direction)


def lamb_up_kernel(
    spot_ref, mine, other, fin_grad, fin_w, fin_m, fin_v, cin_w, cin_m, cin_v,
    fin_mo, fin_vo, fin_u, cin_mo, cin_vo, cin_u, sums_out, full, wide, narrow,
):
    join_halves(spot_ref[0], mine, other, full)
    sums_out[...] = jnp.zeros_like(sums_out)
    grads = (full[0:D, 0:D], fin_grad[...])
    fin_mo[...], fin_vo[...], fin_u[...] = lamb_stack(fin_w, fin_m, fin_v, grads, wide, sums_out, 4)
    grads = [full[FF_ROWS + j * PAD : FF_ROWS + j * PAD + HD, 0:D] for j in range(2)]
    cin_mo[...], cin_vo[...], cin_u[...] = lamb_stack(
        cin_w, cin_m, cin_v, grads, narrow, sums_out, 8
    )


def lamb_attn_kernel(
    share, spot_ref, mine, other, vec, bsums, pick, attn_w, attn_m, attn_v, depth_w, depth_m, depth_v,
    norm_w, norm_m, norm_v, bn_w, bn_m, bn_v, table_w, table_m, table_v,
    attn_mo, attn_vo, out_vo, attn_u, depth_wo, depth_mo, depth_vo, norm_wo, norm_mo, norm_vo,
    bn_wo, bn_mo, bn_vo, table_wo, table_mo, table_vo, sums_out, full, stacked,
):
    join_halves(spot_ref[0], mine, other, full)
    sums_out[...] = jnp.zeros_like(sums_out)
    grads = [full[j * PAD : j * PAD + HD, 0:D] for j in range(4)]
    first_new, second_new, direction = lamb_stack(
        attn_w, attn_m, attn_v, grads, stacked, sums_out, 0
    )
    attn_mo[...] = first_new
    attn_u[...] = direction
    for j in range(3):
        attn_vo[j] = second_new[:, j, :]
    out_vo[...] = second_new[:, 3, :]

    own = depth_w[...]
    depth_mo[...], depth_vo[...], direction = adam_step(depth_m[...], depth_v[...], vec[0:KERNEL, :])
    direction = direction + WEIGHT_DECAY * own
    own_norm = jnp.sqrt(total_of(own * own))
    step_norm = jnp.sqrt(total_of(direction * direction))
    depth_wo[...] = own - RATE_MATRIX * (own_norm / step_norm) * direction
    put_squares(sums_out, 11, own, direction)
    for row in (11, 27):
        sums_out[row : row + 1, :] = sums_out[row : row + 1, :] * share

    def vector(weight, first, second, grad, w_out, m_out, v_out):
        m_out[...], v_out[...], move = adam_step(first[...], second[...], grad)
        w_out[...] = weight[...] - RATE_VECTOR * move

    one = full[HD + RATES : HD + RATES + 2, 0:D]
    rows = [one[0:1]] + [vec[32 + 2 * i : 33 + 2 * i, :] for i in range(3)]
    rows += [one[1:2]] + [vec[33 + 2 * i : 34 + 2 * i, :] for i in range(3)]
    vector(norm_w, norm_m, norm_v, jnp.concatenate(rows, axis=0), norm_wo, norm_mo, norm_vo)
    bn_grad = lax.dot_general(
        bsums[...], pick[...], (((1,), (0,)), ((), ())), precision=PRECISE,
        preferred_element_type=F32,
    )
    vector(bn_w, bn_m, bn_v, bn_grad, bn_wo, bn_mo, bn_vo)
    table_grad = full[HD : HD + RATES, 0:D]
    vector(table_w, table_m, table_v, table_grad, table_wo, table_mo, table_vo)


def step_kernel(sums, *refs):
    weights, moves_in, outs, norm_outs = refs[:5], refs[5:10], refs[10:15], refs[15:17]
    moves, sems = refs[17:22], refs[22]
    copies = Copies(sems)
    loads = [copies.start(moves_in[i], moves[i]) for i in range(5)]
    norms = jnp.sqrt(sums[...])
    factor = RATE_MATRIX * (norms[0:16] / jnp.maximum(norms[16:32], 1e-37))
    shape = (16, 128)
    diagonal = lax.broadcasted_iota(jnp.int32, shape, 0) == lax.broadcasted_iota(jnp.int32, shape, 1)
    for i, out in enumerate(norm_outs):
        across = jnp.where(diagonal, norms[16 * i : 16 * i + 16], 0.0)
        out[...] = jnp.sum(across, axis=0, keepdims=True)[:, 0:12]
    for i, row in enumerate((4, 6, 0, 8, 10)):
        weight, move = weights[i], moves[i]
        stacked = len(weight.shape) == 3
        number = weight.shape[1] if stacked else 1
        loads[i].wait()
        scale = factor[row : row + number, 0:1]
        move[...] = weight[...] - (scale[None] if stacked else scale) * move[...]
        copies.out(move, outs[i])
    copies.finish()


SMEM = pl.BlockSpec(memory_space=pltpu.SMEM)


def whole(shape):
    return pl.BlockSpec(shape, lambda *_: (0,) * len(shape))


def lead(shape, rest, place=None):
    def index(i):
        return ((i if place is None else place(i)),) + (0,) * rest

    return pl.BlockSpec(shape, index)


def placed(entries, pinned):
    return [
        pltpu.HBM(*entry) if place in pinned else jax.ShapeDtypeStruct(*entry)
        for place, entry in enumerate(entries)
    ]


def call(kernel, grid, in_specs, out_specs, out_shape, scratch=(), cost=1_000_000, limit=40, pinned=()):
    return pl.pallas_call(
        kernel,
        grid=(grid,),
        in_specs=in_specs,
        out_specs=out_specs,
        out_shape=placed(out_shape, pinned),
        scratch_shapes=list(scratch),
        cost_estimate=pl.CostEstimate(flops=cost, bytes_accessed=cost // 1000, transcendentals=0),
        compiler_params=pltpu.CompilerParams(vmem_limit_bytes=limit * 1024 * 1024),
    )


def call_whole(kernel, scalars, arrays, out_shape, scratch=(), limit=14):
    return pl.pallas_call(
        kernel,
        in_specs=[SMEM] * len(scalars) + [pl.BlockSpec(memory_space=pltpu.VMEM)] * len(arrays),
        out_specs=[pl.BlockSpec(memory_space=pltpu.VMEM)] * len(out_shape),
        out_shape=[jax.ShapeDtypeStruct(*entry) for entry in out_shape],
        scratch_shapes=list(scratch),
        cost_estimate=pl.CostEstimate(flops=1_000_000, bytes_accessed=2_000_000, transcendentals=0),
        compiler_params=pltpu.CompilerParams(vmem_limit_bytes=limit * 1024 * 1024),
    )(*scalars, *arrays)


ANY = pl.BlockSpec(memory_space=pl.ANY)
VMEM = pl.BlockSpec(memory_space=pltpu.VMEM)


def call_mixed(kernel, scalars, small, large, large_out, small_out, scratch, copies, cost, limit=56, pinned=()):
    return pl.pallas_call(
        kernel,
        in_specs=[SMEM] * len(scalars) + [VMEM] * len(small) + [ANY] * len(large),
        out_specs=[ANY] * len(large_out) + [VMEM] * len(small_out),
        out_shape=placed(large_out + small_out, pinned),
        scratch_shapes=[pltpu.VMEM(*entry) for entry in scratch] + [pltpu.SemaphoreType.DMA((copies,))],
        cost_estimate=pl.CostEstimate(flops=cost, bytes_accessed=cost // 1000, transcendentals=0),
        compiler_params=pltpu.CompilerParams(vmem_limit_bytes=limit * 1024 * 1024),
    )(*scalars, *small, *large)


def swap(value, axis, bit):
    size = lax.axis_size(axis)
    return lax.ppermute(value, axis, [(i, i ^ bit) for i in range(size)])


def combine_all(value, merge, pause=None):
    def over(value, axis, bits):
        if len(bits) == 1:
            return merge(value, swap(value, axis, bits[0]))
        one, two = bits
        others = [swap(value, axis, bit) for bit in (one, two, one ^ two)]
        return merge(merge(value, others[0]), merge(others[1], others[2]))

    def axis_sum(value, axis):
        bits = bits_of(axis)
        first = len(bits) % 2
        if first:
            value = over(value, axis, bits[:1])
        for i in range(first, len(bits), 2):
            value = over(value, axis, bits[i : i + 2])
        return value

    value = axis_sum(value, "tensor")
    if pause is not None:
        value = pause(value)
    return axis_sum(value, "dp")


def bits_of(axis):
    size = lax.axis_size(axis)
    assert size & (size - 1) == 0
    return [1 << i for i in range(size.bit_length() - 1)]


def tie(*values):
    return lax.optimization_barrier(values)


def gather_tensor(shard):
    return gather_near(gather_far(shard))


def gather_far(shard):
    return shard, swap(shard, "tensor", 2)


def gather_near(parts):
    blocks = [parts[0], swap(parts[0], "tensor", 1), parts[1], swap(parts[1], "tensor", 1)]
    return [pltpu.with_memory_space_constraint(block, pltpu.HBM) for block in blocks]


def add_low(one, two):
    return (one.astype(F32) + two.astype(F32)).astype(BF16)


def vanish(value):
    return jnp.minimum(jnp.abs(value[0, 0].astype(F32)), 0.0)


def put_after(array, value):
    return (array.astype(F32) + vanish(value)).astype(array.dtype)


def dp_steps(mine, got, first=0, count=None, fold=False, after=None):
    spot = lax.axis_index("dp") & 1
    half = (mine.shape[0] - first if count is None else count) // 2
    if after is not None:
        got = put_after(got, after)

    def cut(array, place):
        return lax.dynamic_slice_in_dim(array, first + place * half, half, 0)

    kept = add_low(cut(mine, spot), cut(got, spot))
    got = yield swap(add_low(cut(mine, 1 - spot), cut(got, 1 - spot)), "dp", 1)
    bits = bits_of("dp")[1:]
    if fold:
        zed = lax.axis_index("dp") // 2 & 1
        part = half // 2

        def cut_again(array, place):
            return lax.dynamic_slice_in_dim(array, place * part, part, 0)

        mine = add_low(cut_again(kept, zed), cut_again(got, zed))
        got = yield swap(add_low(cut_again(kept, 1 - zed), cut_again(got, 1 - zed)), "dp", bits[0])
        kept = add_low(mine, got)
        for bit in bits[1:]:
            got = yield swap(kept, "dp", bit)
            kept = add_low(kept, got)
        got = yield swap(kept, "dp", bits[0])
        kept = jnp.where(zed == 0, jnp.concatenate([kept, got]), jnp.concatenate([got, kept]))
    else:
        kept = add_low(kept, got)
        for bit in bits:
            got = yield swap(kept, "dp", bit)
            kept = add_low(kept, got)
    got = yield swap(kept, "dp", 1)
    return kept, got


def tensor_steps(send, keep):
    got = yield swap(send, "tensor", 1)
    mine = add_low(keep[0], got[0])
    got = yield swap(add_low(keep[1], got[1]), "tensor", 2)
    return mine, got


def reduce_steps(send, keep, fold=False):
    mine, got = yield from tensor_steps(send, keep)
    return (yield from dp_steps(mine, got, fold=fold))


class Reduction:
    def __init__(self, steps):
        self.steps = steps
        self.flight = next(steps)
        self.result = None

    def advance(self, value, after=None):
        if self.result is not None:
            return value
        value, got = tie(value, self.flight)
        if after is not None:
            got = put_after(got, after)
        self.send(got)
        return value

    def send(self, got):
        self.last = got
        try:
            self.flight = self.steps.send(got)
        except StopIteration as end:
            self.result = end.value

    def finish(self):
        while self.result is None:
            self.send(self.flight)
        return self.result


def pick_matrix():
    pick = np.zeros((WIDE, D), np.float32)
    for column in range(D):
        pick[column // HD * PAD + column % HD, column] = 1.0
    return pick


def body(
    frames, cotangent, lengths, rate_kind, attn_w, attn_m, attn_v, ffin_w, ffin_m, ffin_v,
    ffout_w, ffout_m, ffout_v, convin_w, convin_m, convin_v, convout_w, convout_m, convout_v,
    depth_w, depth_m, depth_v, norm_w, norm_m, norm_v, bn_w, bn_m, bn_v, table_w, table_m, table_v,
):
    rank = lax.axis_index("tensor")
    rank_one = rank.reshape(1).astype(jnp.int32)
    spot_one = (lax.axis_index("dp") & 1).reshape(1).astype(jnp.int32)
    rows = frames.shape[0]
    utts = rows // SLOT
    groups = lax.axis_size("tensor")
    hid = ffin_w.shape[2]
    pick = jnp.asarray(pick_matrix(), BF16)
    pick_wide = jnp.asarray(pick_matrix(), F32)

    attn_w, attn_m, attn_v = (jnp.transpose(a, (2, 0, 1)) for a in (attn_w, attn_m, attn_v))
    ffin_w, ffin_m, ffin_v = (jnp.transpose(a, (1, 0, 2)) for a in (ffin_w, ffin_m, ffin_v))
    ffout_w, ffout_m, ffout_v = (jnp.transpose(a, (1, 0, 2)) for a in (ffout_w, ffout_m, ffout_v))
    convin_w, convin_m, convin_v = (jnp.transpose(a, (2, 0, 1)) for a in (convin_w, convin_m, convin_v))

    pack_one_rows = TAIL + CONV_IN_ROWS
    pack_two_rows = TAIL + PAD
    attn_pack = ((4 * PAD, WIDE), BF16)
    (attn_low,) = call_mixed(
        attn_pack_kernel,
        (),
        (),
        (attn_w,),
        [attn_pack],
        [],
        [(attn_w.shape, F32), attn_pack],
        2,
        1_000,
    )
    shards = (ffin_w, ffout_w, convin_w, convout_w)
    packs = [((count, WIDE), BF16) for count in (pack_one_rows, pack_two_rows)]
    attn_low, depth_early = tie(attn_low, depth_w)
    pack_one, pack_two, chan = call_mixed(
        rest_pack_kernel,
        (),
        (depth_early, bn_w, pick_wide),
        shards,
        packs,
        [((34, 8, WIDE), F32)],
        [(shard.shape, F32) for shard in shards] + packs,
        6,
        1_000,
    )
    attn_parts = gather_tensor(attn_low)
    attn_parts[2], pack_one = tie(attn_parts[2], pack_one)
    one_pair = gather_far(pack_one)

    rowspec = lead((SLOT, D), 1)
    chanspec = lead((SLOT, WIDE), 1)
    onespec = lead((SLOT, 1), 1)
    normspec = whole((8, D))
    allspec = whole((rows, D))
    turnspec = whole((D, rows))
    statspec = whole((3, WIDE))
    attn_specs = [whole((4 * PAD, WIDE))] * groups
    qkvspec = pl.BlockSpec((None, HEADS, 3 * PAD, SLOT), lambda i: (i, 0, 0, 0))
    mixspec = pl.BlockSpec((None, WIDE, SLOT), lambda i: (i, 0, 0))
    probspec = pl.BlockSpec((None, HEADS, SLOT, SLOT), lambda i: (i, 0, 0, 0))
    row_f32 = ((rows, D), F32)
    one_f32 = ((rows, 1), F32)
    sums_f32 = ((8, D), F32)
    base_low, qkv, probs, mixed, n1, s1, wout = call(
        attn_fwd_kernel,
        utts,
        [SMEM, SMEM, SMEM, turnspec, whole((RATES, D))] + attn_specs + [whole((WIDE, D)), normspec],
        [rowspec, qkvspec, probspec, mixspec, rowspec, onespec, whole((WIDE, D))],
        [
            ((rows, D), BF16),
            ((utts, HEADS, 3 * PAD, SLOT), BF16),
            ((utts, HEADS, SLOT, SLOT), BF16),
            ((utts, WIDE, SLOT), BF16),
            row_f32,
            one_f32,
            ((WIDE, D), BF16),
        ],
        [pltpu.VMEM((rows, D), BF16), pltpu.VMEM((HEADS, 4 * PAD, D), BF16)],
        cost=1_000,
        limit=56,
        pinned=range(6),
    )(rank_one, lengths, rate_kind, frames.T, table_w, *attn_parts, pick, norm_w)

    row_low = ((rows, D), BF16)
    turn_low = ((D, rows), BF16)
    hid_low = ((groups, rows, hid), BF16)
    chan_f32 = ((rows, WIDE), F32)
    one_rows = (groups, pack_one_rows, WIDE)
    two_rows = (groups, pack_two_rows, WIDE)
    conv_pad = ((8, SPAN, WIDE), F32)
    far, pack_two, n1 = tie(one_pair[1], pack_two, n1)
    one_parts = gather_near((one_pair[0], far))
    two_pair = gather_far(pack_two)
    hid_one, slope_one, n2, s2, value_pre, gate_sig, conv, stat = call_mixed(
        lower_fwd_kernel,
        (rank_one, lengths),
        (norm_w, chan),
        (n1, *one_parts),
        [hid_low, hid_low, row_f32, one_f32, chan_f32, chan_f32, chan_f32],
        [((3, WIDE), F32)],
        [
            row_f32, (one_rows, BF16), hid_low, hid_low, row_f32, one_f32, chan_f32, chan_f32, chan_f32,
            ((HEADS, CONV_IN_ROWS, D), BF16), conv_pad, row_f32, row_low,
        ],
        20,
        1_000,
        pinned=(2, 3),
    )

    far, stat = tie(two_pair[1], stat)
    two_parts = gather_near((two_pair[0], far))
    stat = combine_all(stat, merge_stats)

    out, grad_three, b_grad, send_one, keep_one, bsums, sums_three, sums_four = call_mixed(
        upper_kernel,
        (rank_one, lengths),
        (norm_w, chan, stat),
        (conv, n2, cotangent.T, *two_parts),
        [turn_low, row_f32, chan_f32] + [((groups // 2, pack_two_rows, WIDE), BF16)] * 2,
        [((2, WIDE), F32), sums_f32, sums_f32],
        [
            chan_f32, row_f32, turn_low, (two_rows, BF16), ((HEADS, PAD, D), BF16),
            ((rows, WIDE), BF16), hid_low, hid_low, row_f32, row_f32, one_f32, row_low, turn_low,
            row_low, turn_low, turn_low, chan_f32, (two_rows, BF16), ((WIDE, D), F32),
        ],
        16,
        1_000,
    )
    reduce_one = Reduction(reduce_steps(send_one, keep_one))
    bsums = combine_all(bsums, jnp.add, reduce_one.advance)

    convin_block = (HEADS, CONV_IN_ROWS, D)
    grad_two, cin_grad, vectors = call_mixed(
        conv_bwd_kernel,
        (rank_one, lengths),
        (norm_w, chan, stat, bsums, pick, sums_three, sums_four),
        (b_grad, conv, value_pre, gate_sig, n2, s2, grad_three, *one_parts),
        [row_f32],
        [(convin_block, BF16), ((VECTOR_ROWS, D), BF16)],
        [
            chan_f32, chan_f32, chan_f32, chan_f32, row_f32, one_f32, row_f32,
            ((HEADS, CONV_IN_ROWS, WIDE), BF16), (convin_block, BF16), conv_pad, conv_pad,
            ((SLOT, WIDE), F32), ((SLOT, WIDE), F32), ((2, WIDE, D), F32), ((KERNEL, 8, WIDE), F32),
            sums_f32,
        ],
        16,
        14_000_000_000,
        pinned=(0,),
    )
    grad_two = reduce_one.advance(grad_two)

    lower_rows = (groups, LOWER_ROWS, WIDE)
    pre_one, send_two, keep_two = call_mixed(
        lower_weights_kernel,
        (),
        (norm_w, cin_grad, vectors),
        (grad_two, n1, *one_parts, hid_one, slope_one),
        [hid_low] + [((groups // 2, LOWER_ROWS, WIDE), BF16)] * 2,
        [],
        [
            row_f32, row_f32, ((groups, TAIL, WIDE), BF16), hid_low, hid_low, row_low, turn_low,
            turn_low, (lower_rows, BF16),
        ],
        16,
        12_000_000_000,
    )
    reduce_two = Reduction(tensor_steps(send_two, keep_two))
    pre_one = reduce_one.advance(pre_one)
    grad_one, sums_one = call_mixed(
        lower_bwd_kernel,
        (),
        (norm_w,),
        (grad_two, n1, s1, *one_parts, pre_one),
        [row_f32],
        [sums_f32],
        [row_f32, row_f32, one_f32, ((groups, FF_ROWS, WIDE), BF16), hid_low],
        12,
        8_000_000_000,
    )
    grad_one = reduce_one.advance(grad_one)
    grad_one = reduce_two.advance(grad_one)
    in_grad, attn_send, attn_keep = call(
        attn_bwd_kernel,
        utts,
        [SMEM, SMEM, rowspec] + attn_specs + [whole((WIDE, D)), whole((WIDE, D))]
        + [qkvspec, probspec, mixspec, rowspec, whole((8, D))],
        [turnspec, whole((2, 4 * PAD, WIDE)), whole((2, 4 * PAD, WIDE))],
        [((D, rows), F32)] + [((2, 4 * PAD, WIDE), BF16)] * 2,
        [
            pltpu.VMEM((HEADS, 3 * PAD, D), F32),
            pltpu.VMEM((WIDE, D), F32),
            pltpu.VMEM((rows, D), F32),
            pltpu.VMEM((8, D), F32),
            pltpu.VMEM((HEADS, 3 * PAD, D), BF16),
        ],
        cost=16_000_000_000,
    )(
        rank_one, rate_kind, base_low, *attn_parts, wout, pick, qkv, probs, mixed, grad_one, sums_one,
    )
    attn_send = reduce_two.advance(attn_send)
    mine, got = reduce_two.result
    reduce_attn = Reduction(reduce_steps(attn_send, attn_keep, FOLD[0]))
    reduce_down = Reduction(dp_steps(mine, got, 0, LOWER_SPLIT, FOLD[1]))
    token = reduce_attn.advance(bsums)
    token = reduce_down.advance(token)
    reduce_up = Reduction(dp_steps(mine, got, LOWER_SPLIT, None, FOLD[2], reduce_down.last))
    token = reduce_up.advance(token)
    token = reduce_one.advance(token, reduce_up.last)
    for chain in (reduce_down, reduce_attn, reduce_up, reduce_down, reduce_attn, reduce_up, reduce_down):
        token = chain.advance(token)
    one_halves = reduce_one.finish()
    down_halves = reduce_down.finish()

    def like(*arrays):
        return [(a.shape, F32) for a in arrays]

    down = call_whole(
        lamb_down_kernel,
        (spot_one,),
        (*one_halves, *down_halves, ffout_w, ffout_m, ffout_v, convout_w, convout_m, convout_v),
        like(*[ffout_w] * 3, *[convout_w] * 3)
        + [((D, D), F32), ((VECTOR_ROWS, D), F32), ((32, 128), F32)],
        [
            pltpu.VMEM((pack_two_rows, WIDE), F32),
            pltpu.VMEM((LOWER_SPLIT, WIDE), F32),
            pltpu.VMEM(ffout_w.shape, F32),
        ],
    )
    token = reduce_attn.advance(token)
    token = reduce_attn.advance(token, down[8])
    up_halves = reduce_up.finish()
    attn_halves = reduce_attn.finish()
    up = call_whole(
        lamb_up_kernel,
        (spot_one,),
        (*up_halves, down[6], ffin_w, ffin_m, ffin_v, convin_w, convin_m, convin_v),
        like(*[ffin_w] * 3, *[convin_w] * 3) + [((32, 128), F32)],
        [
            pltpu.VMEM((LOWER_ROWS - LOWER_SPLIT, WIDE), F32),
            pltpu.VMEM(ffin_w.shape, F32),
            pltpu.VMEM(convin_w.shape, F32),
        ],
    )
    small = (depth_w, depth_m, depth_v, norm_w, norm_m, norm_v, bn_w, bn_m, bn_v, table_w, table_m, table_v)
    last = call_whole(
        functools.partial(lamb_attn_kernel, 1.0 / groups),
        (spot_one,),
        (*attn_halves, down[7], bsums, pick_wide, attn_w, attn_m, attn_v) + small,
        like(attn_w) + [((3, HD, D), F32), ((HD, D), F32)] + like(attn_w, *small) + [((32, 128), F32)],
        [pltpu.VMEM((4 * PAD, WIDE), F32), pltpu.VMEM(attn_w.shape, F32)],
    )
    squares = down[8] + up[6] + last[16]
    for bit in bits_of("tensor"):
        squares = squares + swap(squares, "tensor", bit)
    matrices = (ffin_w, ffout_w, attn_w, convin_w, convout_w)
    moves = (up[2], down[2], last[3], up[5], down[5])
    ffin_new, ffout_new, attn_new, convin_new, convout_new, weight_norms, update_norms = call_mixed(
        step_kernel,
        (),
        (squares, *matrices),
        moves,
        like(*matrices),
        [((1, 12), F32)] * 2,
        like(*matrices),
        10,
        1_000_000,
        limit=14,
    )

    def back_chan(array):
        return jnp.transpose(array, (1, 2, 0))

    def back_mid(array):
        return jnp.transpose(array, (1, 0, 2))

    small_new = last[4:16]
    return (
        out.T,
        in_grad.T,
        back_chan(attn_new),
        back_chan(last[0]),
        jnp.transpose(last[1], (0, 2, 1)),
        last[2].T,
        back_mid(ffin_new),
        back_mid(up[0]),
        back_mid(up[1]),
        back_mid(ffout_new),
        back_mid(down[0]),
        back_mid(down[1]),
        back_chan(convin_new),
        back_chan(up[3]),
        back_chan(up[4]),
        convout_new,
        down[3],
        down[4],
        *small_new,
        weight_norms.reshape(12),
        update_norms.reshape(12),
    )


def solution(mesh):
    rows = P(("dp", "tensor"), None)
    last = P(None, None, "tensor")
    mid = P(None, "tensor", None)
    first = P("tensor", None)
    placed = (rows, rows, P("dp"), P("dp")) + (last,) * 6 + (mid,) * 3 + (last,) * 3 + (first,) * 3
    results = (rows, rows) + (last,) * 3 + (P(None, "tensor"),) + (last,) * 3 + (mid,) * 3
    return jax.shard_map(
        body,
        mesh=mesh,
        in_specs=placed + (P(),) * 12,
        out_specs=results + (last,) * 3 + (first,) * 3 + (P(),) * 14,
        check_vma=False,
    )
```

```python
import functools
import math

import jax
import jax.numpy as jnp
import numpy as np
from jax import lax
from jax.experimental import pallas as pl
from jax.experimental.pallas import tpu as pltpu
from jax.sharding import PartitionSpec as P

D = 324
HEADS = 4
KERNEL = 31
HALF = KERNEL // 2
RATES = 3
STEP = 10
SLOT = 496
HD = 81
PAD = 96
WIDE = HEADS * PAD
FF_ROWS = 336
TAIL = 2 * FF_ROWS
CONV_IN_ROWS = 2 * PAD
VECTOR_ROWS = 48
LOWER_VEC = FF_ROWS
LOWER_SPLIT = FF_ROWS + VECTOR_ROWS
LOWER_UP = LOWER_SPLIT
LOWER_CONV = LOWER_UP + FF_ROWS
LOWER_ROWS = LOWER_CONV + CONV_IN_ROWS + 16

EPS_NORM = 1e-05
BETA_ONE = 0.9
BETA_TWO = 0.999
ADAM_EPS = 1e-06
WEIGHT_DECAY = 0.01
RATE_MATRIX = 0.3
RATE_VECTOR = 0.5
MASK_FILL = -1e30
SCALE = 1.0 / math.sqrt(HD)
PRECISE = lax.Precision.HIGHEST

F32 = jnp.float32
BF16 = jnp.bfloat16
LEAD = 16
SPAN = 544


def dot_nn(left, right):
    return lax.dot_general(left, right, (((1,), (0,)), ((), ())), preferred_element_type=F32)


def dot_nt(left, right):
    return lax.dot_general(left, right, (((1,), (1,)), ((), ())), preferred_element_type=F32)


def dot_tn(left, right):
    return lax.dot_general(left, right, (((0,), (0,)), ((), ())), preferred_element_type=F32)


def sigmoid(value):
    return 0.5 * jnp.tanh(0.5 * value) + 0.5


def ln_forward(resid):
    center = resid - jnp.mean(resid, axis=-1, keepdims=True)
    inv = lax.rsqrt(jnp.mean(center * center, axis=-1, keepdims=True) + EPS_NORM)
    return center * inv, inv


def ln_backward(upstream, normal, inv, gain):
    scaled = upstream * gain
    grad = inv * (
        scaled
        - jnp.mean(scaled, axis=-1, keepdims=True)
        - normal * jnp.mean(scaled * normal, axis=-1, keepdims=True)
    )
    gain_sum = jnp.sum(upstream * normal, axis=0, keepdims=True)
    shift_sum = jnp.sum(upstream, axis=0, keepdims=True)
    return grad, gain_sum, shift_sum


def put_sums(ref, first, gain_sum, shift_sum):
    @pl.when(first)
    def _():
        ref[...] = jnp.zeros_like(ref)

    ref[0:1, :] += gain_sum
    ref[1:2, :] += shift_sum


def valid_rows(count):
    return lax.broadcasted_iota(jnp.int32, (SLOT, 1), 0) < count


FOLD = (False, False, False)


def assemble(scratch, parts, rank, first, count):
    for place, part in enumerate(parts):
        scratch[place ^ rank] = part[first : first + count, 0:D]


def attn_fwd_kernel(
    rank_ref, len_ref, kind_ref, frames, table, w0, w1, w2, w3, pick, norm,
    low_out, qkv_out, prob_out, mixed_out, n1_out, s1_out, wout_out, low_rows, weights,
):
    utt = pl.program_id(0)
    rank = rank_ref[0]
    which = rank * pl.num_programs(0) + utt

    @pl.when(utt == 0)
    def _():
        assemble(weights, (w0, w1, w2, w3), rank, 0, 4 * PAD)
        turned = jnp.concatenate([weights[t, 3 * PAD :, :] for t in range(HEADS)], axis=0)
        spaced = dot_nt(pick[...], turned).astype(BF16)
        wout_out[...] = dot_nn(spaced, pick[...]).astype(BF16)
        low_rows[...] = frames[...].T

    base = low_rows[pl.ds(utt * SLOT, SLOT), :].astype(F32) + table[pl.ds(kind_ref[which], 1), :]
    base_low = base.astype(BF16)
    low_out[...] = base_low
    valid = valid_rows(len_ref[which])

    def project(head):
        qkv = dot_nt(weights[head, 0 : 3 * PAD, :], base_low).astype(BF16)
        qkv_out[head] = qkv
        return qkv, dot_tn(qkv[PAD : 2 * PAD], qkv[:PAD])

    later = project(0)
    for head in range(HEADS):
        qkv, products = later
        if head + 1 < HEADS:
            later = project(head + 1)
        scores = jnp.where(valid, products * SCALE, MASK_FILL)
        top = jnp.max(scores, axis=0, keepdims=True)
        expo = jnp.exp(scores - top)
        total = jnp.sum(expo, axis=0, keepdims=True)
        probs = (expo * (1.0 / total)).astype(BF16)
        prob_out[head] = probs
        mixed_out[head * PAD : (head + 1) * PAD, :] = dot_nn(qkv[2 * PAD :], probs).astype(BF16)
    attn_out = dot_tn(mixed_out[...], wout_out[...])
    normal, inv = ln_forward(base + attn_out)
    n1_out[...] = normal
    s1_out[...] = inv


def shifted(scratch):
    for shift in range(1, 8):
        scratch[shift, 0 : SPAN - 8, :] = scratch[0, pl.ds(shift, SPAN - 8), :]


def load_padded(scratch, signal):
    scratch[0, 0:LEAD, :] = jnp.zeros((LEAD, WIDE), F32)
    scratch[0, pl.ds(LEAD + SLOT, SPAN - LEAD - SLOT), :] = jnp.zeros((SPAN - LEAD - SLOT, WIDE), F32)
    scratch[0, pl.ds(LEAD, SLOT), :] = signal
    shifted(scratch)


LANES = 128
BLOCKS = ((0, 128), (128, 128), (256, 128), (384, 112))


def depth_tiles(body_fn):
    for row, count in BLOCKS:
        for tile in range(WIDE // LANES):
            body_fn(row, count, slice(tile * LANES, (tile + 1) * LANES))


def depth_sum(padded, row_of, chan, put):
    def block(row, count, lanes):
        total = jnp.zeros((count // 8, 8, LANES), F32)
        for shift in range(8):
            rows = padded[shift, pl.ds(row, count + 24), lanes]
            for lift in range(4):
                place = 8 * lift + shift
                if 1 <= place <= KERNEL:
                    tap = row_of(place)
                    part = rows[8 * lift : 8 * lift + count].reshape(count // 8, 8, LANES)
                    total = total + part * chan[tap, :, lanes][None]
        put(row, count, lanes, total.reshape(count, LANES))

    depth_tiles(block)


def depth_products(padded, own, sums):
    def block(row, count, lanes):
        mine = own[pl.ds(row, count), lanes]
        for shift in range(8):
            rows = padded[shift, pl.ds(row, count + 24), lanes]
            for lift in range(4):
                place = 8 * lift + shift
                if 1 <= place <= KERNEL:
                    part = rows[8 * lift : 8 * lift + count] * mine
                    part = jnp.sum(part.reshape(count // 8, 8, LANES), axis=0)
                    sums[place - 1, :, lanes] += part

    depth_tiles(block)


def merge_stats(one, two):
    mean_one, dev_one, count_one = one[0:1], one[1:2], one[2:3]
    mean_two, dev_two, count_two = two[0:1], two[1:2], two[2:3]
    count = count_one + count_two
    mean = (mean_one * count_one + mean_two * count_two) / count
    gap = mean_one - mean_two
    dev = dev_one + dev_two + gap * gap * (count_one * count_two / count)
    return jnp.concatenate([mean, dev, count], axis=0)


def bn_parts(conv, stat, chan):
    inv = lax.rsqrt(stat[1:2, :] / stat[2:3, :] + EPS_NORM)
    normal = (conv - stat[0:1, :]) * inv
    return normal, inv, normal * chan[32, 0:1, :] + chan[33, 0:1, :]


def utt_rows(utt):
    return pl.ds(pl.multiple_of(utt * SLOT, 16), SLOT)


def each_utt(rows, body_fn):
    def step(utt, carry):
        body_fn(utt, utt_rows(utt))
        return carry

    lax.fori_loop(0, rows // SLOT, step, 0)


class Copies:
    def __init__(self, sems):
        self.sems = sems
        self.count = 0
        self.open = []

    def start(self, source, target):
        copy = pltpu.make_async_copy(source, target, self.sems.at[self.count])
        self.count += 1
        copy.start()
        return copy

    def out(self, source, target):
        self.open.append(self.start(source, target))

    def finish(self):
        for copy in self.open:
            copy.wait()


def attn_pack_kernel(attn_in, out, attn, low, sems):
    copies = Copies(sems)
    load = copies.start(attn_in, attn)
    low[...] = jnp.zeros_like(low)
    load.wait()
    for j in range(4):
        low[j * PAD : j * PAD + HD, 0:D] = attn[:, j, :].astype(BF16)
    copies.out(low, out)
    copies.finish()


def rest_pack_kernel(
    depth, bn, pick, ffin_in, ffout_in, convin_in, convout_in, one_out, two_out, chan_out,
    ffin, ffout, convin, convout, one, two, sems,
):
    copies = Copies(sems)
    pairs = (ffin_in, ffin), (ffout_in, ffout), (convin_in, convin), (convout_in, convout)
    loads = [copies.start(source, target) for source, target in pairs]

    def spread(rows):
        return lax.dot_general(
            rows, pick[...], (((1,), (1,)), ((), ())), precision=PRECISE, preferred_element_type=F32
        )

    for first, rows in ((0, spread(depth[...])), (32, spread(bn[...]))):
        count = rows.shape[0]
        chan_out[first : first + count] = jnp.broadcast_to(rows[:, None, :], (count, 8, WIDE))
    for out in (one, two):
        out[...] = jnp.zeros_like(out)
    for load in loads:
        load.wait()
    for j, out in ((0, one), (1, two)):
        out[0:D, 0:D] = ffin[:, j, :].astype(BF16)
        out[FF_ROWS : FF_ROWS + D, 0:D] = ffout[:, j, :].astype(BF16)
    for j in range(2):
        one[TAIL + j * PAD : TAIL + j * PAD + HD, 0:D] = convin[:, j, :].astype(BF16)
    two[TAIL : TAIL + HD, 0:D] = convout[...].astype(BF16)
    copies.out(one, one_out)
    copies.out(two, two_out)
    copies.finish()


def ffn_forward(z_low, weights, hid, slope, acc, ready=None, done=None):
    def block(p, carry):
        pre = dot_nn(z_low[...], weights[p, 0:D, 0:D])
        sig = sigmoid(pre)
        hidden = pre * sig
        hid_low = hidden.astype(BF16)
        hid[p] = hid_low
        slope[p] = (sig + hidden * (1.0 - sig)).astype(BF16)
        acc[...] += dot_nn(hid_low, weights[p, FF_ROWS : FF_ROWS + D, 0:D])
        return carry

    if done is None:
        lax.fori_loop(0, HEADS, block, 0)
    else:
        for p in range(HEADS):
            ready(p)
            block(p, 0)
            done(p)


def ffn_backward(up_low, up_turn, z_turn, weights, hid, slope, acc, grads, up_row, down_row, ready=None, done=None):
    def block(p, carry):
        back = dot_nt(up_low[...], weights[p, FF_ROWS : FF_ROWS + D, 0:D])
        pre_grad = (back * slope[p].astype(F32)).astype(BF16)
        grads[p, down_row : down_row + D, 0:D] = dot_nn(up_turn[...], hid[p]).astype(BF16)
        grads[p, up_row : up_row + D, 0:D] = dot_nn(z_turn[...], pre_grad).astype(BF16)
        if acc is None:
            slope[p] = pre_grad
        else:
            acc[...] += dot_nt(pre_grad, weights[p, 0:D, 0:D])
        return carry

    if done is None:
        lax.fori_loop(0, HEADS, block, 0)
    else:
        for p in range(HEADS):
            ready(p)
            block(p, 0)
            done(p)


def send_out(copies, grads, send, keep):
    for i in range(HEADS // 2):
        copies.out(grads.at[2 * i + 1], send.at[i])
        copies.out(grads.at[2 * i], keep.at[i])


def lower_fwd_kernel(
    rank_ref, len_ref, norm, chan, n1_in, w0, w1, w2, w3,
    hid_out, slope_out, n2_out, s2_out, value_out, sig_out, conv_out, stat_out,
    n1, weights, hid, slope, n2, s2, value, sig, conv, conv_w, padded, acc, z_low, sems,
):
    copies = Copies(sems)
    rank = rank_ref[0]
    rows = n1_in.shape[0]
    parts = (w0, w1, w2, w3)
    first = copies.start(n1_in, n1)
    ffn_rows, conv_rows = pl.ds(0, TAIL), pl.ds(TAIL, CONV_IN_ROWS)
    loads = [copies.start(part.at[ffn_rows], weights.at[p, ffn_rows]) for p, part in enumerate(parts)]
    later = [copies.start(part.at[conv_rows], weights.at[p, conv_rows]) for p, part in enumerate(parts)]
    first.wait()
    z = n1[...] * norm[0:1, :] + norm[4:5, :]
    acc[...] = z
    z_low[...] = z.astype(BF16)

    def ready(p):
        loads[p].wait()

    def done(p):
        copies.out(hid.at[p], hid_out.at[p])
        copies.out(slope.at[p], slope_out.at[p])

    ffn_forward(z_low, weights, hid, slope, acc, ready, done)
    normal, inv = ln_forward(acc[...])
    n2[...] = normal
    s2[...] = inv
    copies.out(n2, n2_out)
    copies.out(s2, s2_out)
    z_low[...] = (normal * norm[1:2, :] + norm[5:6, :]).astype(BF16)
    for load in later:
        load.wait()
    for p in range(HEADS):
        conv_w[p ^ rank] = weights[p, TAIL : TAIL + CONV_IN_ROWS, 0:D]
    value[...] = dot_nt(z_low[...], conv_w[:, 0:PAD, :].reshape(WIDE, D))
    copies.out(value, value_out)
    sig[...] = sigmoid(dot_nt(z_low[...], conv_w[:, PAD:, :].reshape(WIDE, D)))
    copies.out(sig, sig_out)
    utts = rows // SLOT

    def utterance(utt, here):
        count = len_ref[rank * utts + utt]
        valid = valid_rows(count).astype(F32)
        load_padded(padded, value[here, :] * sig[here, :] * valid)

        def put(row, number, lanes, total):
            conv[pl.ds(pl.multiple_of(utt * SLOT + row, 16), number), lanes] = total

        depth_sum(padded, lambda place: place - 1, chan, put)
        own = conv[here, :]
        number = count.astype(F32)
        mean = jnp.sum(own * valid, axis=0, keepdims=True) / number
        center = (own - mean) * valid
        dev = jnp.sum(center * center, axis=0, keepdims=True)
        stat = jnp.concatenate([mean, dev, jnp.zeros_like(mean) + number], axis=0)

        @pl.when(utt == 0)
        def _():
            stat_out[...] = stat

        @pl.when(utt > 0)
        def _():
            stat_out[...] = merge_stats(stat_out[...], stat)

    each_utt(rows, utterance)
    copies.out(conv, conv_out)
    copies.finish()


def upper_kernel(
    rank_ref, len_ref, norm, chan, stat, conv_in, n2_in, cot_in, w0, w1, w2, w3,
    out_out, grad_out, b_out, send, keep, bsums, sums_three, sums_four,
    conv, n2, cot, weights, conv_w, act, hid, slope, acc, n3, s3, z_low, z_turn, up_low, up_turn,
    out, b_grad, grads, conv_acc, sems,
):
    copies = Copies(sems)
    rank = rank_ref[0]
    rows = conv_in.shape[0]
    utts = rows // SLOT
    parts = (w0, w1, w2, w3)
    ffn_rows, conv_rows = pl.ds(0, TAIL), pl.ds(TAIL, PAD)
    loads = [copies.start(part.at[conv_rows], weights.at[p, conv_rows]) for p, part in enumerate(parts)]
    loads += [copies.start(conv_in, conv), copies.start(n2_in, n2)]
    later = [copies.start(part.at[ffn_rows], weights.at[p, ffn_rows]) for p, part in enumerate(parts)]
    cot_load = copies.start(cot_in, cot)
    for load in loads:
        load.wait()
    for p in range(HEADS):
        conv_w[p ^ rank] = weights[p, TAIL : TAIL + PAD, 0:D]
    bsums[...] = jnp.zeros_like(bsums)
    sums_three[...] = jnp.zeros_like(sums_three)
    sums_four[...] = jnp.zeros_like(sums_four)
    conv_acc[...] = jnp.zeros_like(conv_acc)

    def utterance_fwd(utt, here):
        _, _, bn_out = bn_parts(conv[here, :], stat, chan)
        act_low = (bn_out * sigmoid(bn_out)).astype(BF16)
        act[here, :] = act_low
        second = n2[here, :] * norm[1:2, :] + norm[5:6, :]
        normal, inv = ln_forward(second + dot_nn(act_low, conv_w[...].reshape(WIDE, D)))
        n3[here, :] = normal
        s3[here, :] = inv
        z = normal * norm[2:3, :] + norm[6:7, :]
        acc[here, :] = z
        z_low[here, :] = z.astype(BF16)

    each_utt(rows, utterance_fwd)
    z_turn[...] = z_low[...].T
    for load in later:
        load.wait()
    ffn_forward(z_low, weights, hid, slope, acc)
    normal, inv = ln_forward(acc[...])
    gain = norm[3:4, :]
    out[...] = (normal * gain + norm[7:8, :]).astype(BF16).T
    copies.out(out, out_out)
    cot_load.wait()
    valid = jnp.concatenate([valid_rows(len_ref[rank * utts + u]) for u in range(utts)], axis=0)
    upstream = jnp.where(valid, cot[...].T.astype(F32), 0.0)
    grad, gain_sum, shift_sum = ln_backward(upstream, normal, inv, gain)
    sums_four[0:1, :] = gain_sum
    sums_four[1:2, :] = shift_sum
    acc[...] = grad
    up_low[...] = grad.astype(BF16)
    up_turn[...] = up_low[...].T
    ffn_backward(up_low, up_turn, z_turn, weights, hid, slope, acc, grads, 0, FF_ROWS)
    grad, gain_sum, shift_sum = ln_backward(acc[...], n3[...], s3[...], norm[2:3, :])
    sums_three[0:1, :] = gain_sum
    sums_three[1:2, :] = shift_sum
    acc[...] = grad
    copies.out(acc, grad_out)
    up_low[...] = grad.astype(BF16)

    def utterance_bwd(utt, here):
        normal, _, bn_out = bn_parts(conv[here, :], stat, chan)
        sig = sigmoid(bn_out)
        low = up_low[here, :]
        own = dot_nt(low, conv_w[...].reshape(WIDE, D)) * (sig * (1.0 + bn_out * (1.0 - sig)))
        b_grad[here, :] = own
        bsums[0:1, :] += jnp.sum(own * normal, axis=0, keepdims=True)
        bsums[1:2, :] += jnp.sum(own, axis=0, keepdims=True)
        conv_acc[...] += dot_tn(act[here, :], low)

    each_utt(rows, utterance_bwd)
    copies.out(b_grad, b_out)
    for t in range(HEADS):
        place = t ^ rank
        grads[place, TAIL : TAIL + PAD, 0:D] = conv_acc[t * PAD : (t + 1) * PAD, :].astype(BF16)
    send_out(copies, grads, send, keep)
    copies.finish()


def conv_bwd_kernel(
    rank_ref, len_ref, norm, chan, stat, bsums, pick, sums_three, sums_four,
    b_in, conv_in, value_in, sig_in, n2_in, s2_in, grad_in, w0, w1, w2, w3,
    grad_out, wgrad_out, vec_out,
    b_grad, conv, value, sig, n2, s2, grad, parts, weights, glu_pad, cg_pad, cg_ref, gg_ref,
    conv_acc, tap_sums, sums_ref, sems,
):
    copies = Copies(sems)
    rank = rank_ref[0]
    rows = b_in.shape[0]
    utts = rows // SLOT
    first = pl.ds(0, SLOT)
    pairs = [(value_in, value), (sig_in, sig), (conv_in, conv), (b_in, b_grad)]
    loads = [copies.start(source.at[first], target.at[first]) for source, target in pairs]
    others = pl.ds(SLOT, rows - SLOT)
    later = [copies.start(source.at[others], target.at[others]) for source, target in pairs]
    later += [copies.start(n2_in, n2), copies.start(s2_in, s2), copies.start(grad_in, grad)]
    later += [
        copies.start(part.at[pl.ds(TAIL, CONV_IN_ROWS)], parts.at[p])
        for p, part in enumerate((w0, w1, w2, w3))
    ]
    tap_sums[...] = jnp.zeros_like(tap_sums)
    conv_acc[...] = jnp.zeros_like(conv_acc)
    sums_ref[...] = jnp.zeros_like(sums_ref)
    for load in loads:
        load.wait()

    def utterance(utt, here):
        valid = valid_rows(len_ref[rank * utts + utt]).astype(F32)
        gain = chan[32, 0:1, :]
        count = stat[2:3, :]
        load_padded(glu_pad, value[here, :] * sig[here, :] * valid)
        normal, inv, _ = bn_parts(conv[here, :], stat, chan)
        conv_grad = (valid * inv) * (
            b_grad[here, :] * gain
            - gain * (bsums[1:2, :] / count)
            - normal * (gain * (bsums[0:1, :] / count))
        )
        cg_ref[...] = conv_grad
        load_padded(cg_pad, conv_grad)
        depth_products(glu_pad, cg_ref, tap_sums)

        def put(row, number, lanes, total):
            gg_ref[pl.ds(row, number), lanes] = total

        depth_sum(cg_pad, lambda place: KERNEL - place, chan, put)

        @pl.when(utt == 0)
        def _():
            for load in later:
                load.wait()
            for p in range(HEADS):
                weights[p ^ rank] = parts[p, :, 0:D]

        glu_grad = gg_ref[...] * valid
        sig_now = sig[here, :]
        value_grad = (glu_grad * sig_now).astype(BF16)
        gate_grad = (glu_grad * value[here, :] * sig_now * (1.0 - sig_now)).astype(BF16)
        normal = n2[here, :]
        z_low = (normal * norm[1:2, :] + norm[5:6, :]).astype(BF16)
        conv_acc[0] += dot_tn(value_grad, z_low)
        conv_acc[1] += dot_tn(gate_grad, z_low)
        upstream = (
            grad[here, :]
            + dot_nn(value_grad, weights[:, 0:PAD, :].reshape(WIDE, D))
            + dot_nn(gate_grad, weights[:, PAD:, :].reshape(WIDE, D))
        )
        own, gain_sum, shift_sum = ln_backward(upstream, normal, s2[here, :], norm[1:2, :])
        grad[here, :] = own
        sums_ref[0:1, :] += gain_sum
        sums_ref[1:2, :] += shift_sum

    each_utt(rows, utterance)
    copies.out(grad, grad_out)
    for t in range(HEADS):
        for j in range(2):
            part = conv_acc[j, t * PAD : (t + 1) * PAD, :].astype(BF16)
            wgrad_out[t ^ rank, j * PAD : (j + 1) * PAD, :] = part
    taps = jnp.sum(tap_sums[...], axis=1).astype(BF16)
    vec = [dot_nn(taps, pick[...]), jnp.zeros((1, D), F32)]
    vec += [sums_ref[0:2, :], sums_three[0:2, :], sums_four[0:2, :]]
    vec += [jnp.zeros((VECTOR_ROWS - 38, D), F32)]
    vec_out[...] = jnp.concatenate(vec, axis=0).astype(BF16)
    copies.finish()


def lower_weights_kernel(
    norm, cin_grad, vectors, up_in, n1_in, w0, w1, w2, w3, hid_in, slope_in,
    pre_out, send, keep,
    up, n1, weights, hid, slope, up_low, up_turn, z_turn, grads, sems,
):
    copies = Copies(sems)
    loads = [copies.start(up_in, up), copies.start(n1_in, n1)]
    down = pl.ds(FF_ROWS, FF_ROWS)
    loads += [
        copies.start(part.at[down], weights.at[p, down]) for p, part in enumerate((w0, w1, w2, w3))
    ]
    later = [
        (copies.start(slope_in.at[p], slope.at[p]), copies.start(hid_in.at[p], hid.at[p]))
        for p in range(HEADS)
    ]
    for load in loads[:2]:
        load.wait()
    up_low[...] = up[...].astype(BF16)
    up_turn[...] = up_low[...].T
    z_turn[...] = (n1[...] * norm[0:1, :] + norm[4:5, :]).astype(BF16).T

    def ready(p):
        for load in (loads[2 + p], *later[p]):
            load.wait()

    def done(p):
        copies.out(slope.at[p], pre_out.at[p])

    ffn_backward(up_low, up_turn, z_turn, weights, hid, slope, None, grads, LOWER_UP, 0, ready, done)
    for p in range(HEADS):
        grads[p, LOWER_CONV : LOWER_CONV + CONV_IN_ROWS, 0:D] = cin_grad[p]
        grads[p, LOWER_VEC : LOWER_VEC + VECTOR_ROWS, 0:D] = vectors[...]
    send_out(copies, grads, send, keep)
    copies.finish()


def lower_bwd_kernel(
    norm, up_in, n1_in, s1_in, w0, w1, w2, w3, pre_in, grad_out, sums_one,
    acc, n1, s1, weights, pre, sems,
):
    copies = Copies(sems)
    up_rows = pl.ds(0, FF_ROWS)
    loads = [copies.start(up_in, acc)]
    for p, part in enumerate((w0, w1, w2, w3)):
        loads += [copies.start(part.at[up_rows], weights.at[p]), copies.start(pre_in.at[p], pre.at[p])]
    late = [copies.start(n1_in, n1), copies.start(s1_in, s1)]
    loads[0].wait()
    for p in range(HEADS):
        loads[2 * p + 1].wait()
        loads[2 * p + 2].wait()
        acc[...] += dot_nt(pre[p], weights[p, 0:D, 0:D])
    for load in late:
        load.wait()
    grad, gain_sum, shift_sum = ln_backward(acc[...], n1[...], s1[...], norm[0:1, :])
    acc[...] = grad
    copies.out(acc, grad_out)
    sums_one[...] = jnp.zeros_like(sums_one)
    sums_one[0:1, :] = gain_sum
    sums_one[1:2, :] = shift_sum
    copies.finish()


def attn_bwd_kernel(
    rank_ref, kind_ref, low_in, w0, w1, w2, w3, wout, pick, qkv_in, probs_in, mixed, grad, sums_one,
    grad_out, send, keep, acc, acc_out, rows_out, table_sums, weights,
):
    utt = pl.program_id(0)
    rank = rank_ref[0]

    @pl.when(utt == 0)
    def _():
        assemble(weights, (w0, w1, w2, w3), rank, 0, 3 * PAD)
        acc[...] = jnp.zeros_like(acc)
        acc_out[...] = jnp.zeros_like(acc_out)
        table_sums[...] = jnp.zeros_like(table_sums)

    base_low = low_in[...]
    upstream = grad[...]
    up_low = upstream.astype(BF16)
    mixed_grad = dot_nt(wout[...], up_low).astype(BF16)

    def up_head(head):
        return mixed_grad[head * PAD : (head + 1) * PAD, :]

    def prob_product(head):
        return dot_tn(qkv_in[head, 2 * PAD :, :], up_head(head))

    later = prob_product(0)
    acc_out[...] += dot_nn(mixed[...], up_low)
    total = upstream
    waiting = None
    for head in range(HEADS + 1):
        if head < HEADS:
            prob_grad = later
            if head + 1 < HEADS:
                later = prob_product(head + 1)
            probs_low = probs_in[head]
            probs = probs_low.astype(F32)
            delta = jnp.sum(prob_grad * probs, axis=0, keepdims=True)
            score_grad = (probs * (prob_grad - delta)).astype(BF16)
        if waiting is not None:
            acc[head - 1] += dot_nn(waiting, base_low)
            total = total + dot_tn(waiting, weights[head - 1])
        if head < HEADS:
            queries = qkv_in[head, 0:PAD, :]
            keys = qkv_in[head, PAD : 2 * PAD, :]
            value_grad = dot_nt(up_head(head), probs_low).astype(BF16)
            query_grad = (dot_nn(keys, score_grad) * SCALE).astype(BF16)
            key_grad = (dot_nt(queries, score_grad) * SCALE).astype(BF16)
            waiting = jnp.concatenate([query_grad, key_grad, value_grad], axis=0)
    rows_out[pl.ds(utt * SLOT, SLOT), :] = total
    column = jnp.sum(total, axis=0, keepdims=True)
    kind = kind_ref[rank * pl.num_programs(0) + utt]
    place = lax.broadcasted_iota(jnp.int32, table_sums.shape, 0)
    table_sums[...] += jnp.where(place == kind, column, 0.0)

    @pl.when(utt == pl.num_programs(0) - 1)
    def _():
        grad_out[...] = rows_out[...].T
        turned = dot_nt(pick[...], acc_out[...].astype(BF16)).astype(BF16)
        turned = dot_nn(turned, pick[...]).astype(BF16)
        extra = [table_sums[0:RATES, :], sums_one[0:2, :]]
        extra += [jnp.zeros((PAD - HD - RATES - 2, D), F32)]
        extra = jnp.concatenate(extra, axis=0).astype(BF16)
        rows_out[0:WIDE, :] = turned.astype(F32)
        for place in range(HEADS):
            t = place ^ rank
            out = send if place % 2 else keep
            out[place // 2, 0 : 3 * PAD, 0:D] = acc[t].astype(BF16)
            out[place // 2, HD:PAD, 0:D] = extra
            block = rows_out[pl.ds(pl.multiple_of(t * PAD, PAD), PAD), :]
            out[place // 2, 3 * PAD :, 0:D] = block.astype(BF16)


def adam_step(first, second, grad_full):
    first_new = BETA_ONE * first + (1.0 - BETA_ONE) * grad_full
    second_new = BETA_TWO * second + (1.0 - BETA_TWO) * grad_full * grad_full
    scaled = jnp.maximum(second_new * (1.0 / (1.0 - BETA_TWO**STEP)), 1e-30)
    below = scaled * lax.rsqrt(scaled) + ADAM_EPS
    inverse = pl.reciprocal(below, approx=True)
    inverse = inverse * (2.0 - below * inverse)
    direction = (first_new * (1.0 / (1.0 - BETA_ONE**STEP))) * inverse
    return (first_new, second_new, direction)


def total_of(array):
    return jnp.sum(jnp.sum(array, axis=1, keepdims=True), axis=0, keepdims=True)


def put_squares(sums_out, row, own, direction):
    if own.ndim == 3:
        own = jnp.sum(own * own, axis=0)
        direction = jnp.sum(direction * direction, axis=0)
        count = own.shape[0]
    else:
        own = jnp.sum(own * own, axis=0, keepdims=True)
        direction = jnp.sum(direction * direction, axis=0, keepdims=True)
        count = 1
    sums_out[row : row + count, :] = jnp.broadcast_to(
        jnp.sum(own, axis=1, keepdims=True), (count, 128)
    )
    sums_out[16 + row : 16 + row + count, :] = jnp.broadcast_to(
        jnp.sum(direction, axis=1, keepdims=True), (count, 128)
    )


def join_halves(spot, mine, other, scratch):
    half = mine.shape[0]
    scratch[pl.ds(pl.multiple_of(spot * half, 16), half), :] = mine[...].astype(F32)
    scratch[pl.ds(pl.multiple_of((1 - spot) * half, 16), half), :] = other[...].astype(F32)


def lamb_stack(weight, first, second, grads, stacked, sums_out, row):
    for j, grad in enumerate(grads):
        stacked[:, j, :] = grad
    own = weight[...]
    first_new, second_new, direction = adam_step(first[...], second[...], stacked[...])
    direction = direction + WEIGHT_DECAY * own
    put_squares(sums_out, row, own, direction)
    return first_new, second_new, direction


def lamb_down_kernel(
    spot_ref, one_mine, one_other, two_mine, two_other, fout_w, fout_m, fout_v, cout_w, cout_m, cout_v,
    fout_mo, fout_vo, fout_u, cout_mo, cout_vo, cout_u, fin_grad, vec_out, sums_out, one, two, wide,
):
    spot = spot_ref[0]
    join_halves(spot, one_mine, one_other, one)
    join_halves(spot, two_mine, two_other, two)
    sums_out[...] = jnp.zeros_like(sums_out)
    fin_grad[...] = one[0:D, 0:D]
    vec_out[...] = two[FF_ROWS : FF_ROWS + VECTOR_ROWS, 0:D]
    grads = (two[0:D, 0:D].T, one[FF_ROWS : FF_ROWS + D, 0:D].T)
    fout_mo[...], fout_vo[...], fout_u[...] = lamb_stack(
        fout_w, fout_m, fout_v, grads, wide, sums_out, 6
    )
    own = cout_w[...]
    grad = one[TAIL : TAIL + HD, 0:D]
    first_new, second_new, direction = adam_step(cout_m[...], cout_v[...], grad)
    direction = direction + WEIGHT_DECAY * own
    cout_mo[...], cout_vo[...], cout_u[...] = first_new, second_new, direction
    put_squares(sums_out, 10, own, direction)


def lamb_up_kernel(
    spot_ref, mine, other, fin_grad, fin_w, fin_m, fin_v, cin_w, cin_m, cin_v,
    fin_mo, fin_vo, fin_u, cin_mo, cin_vo, cin_u, sums_out, full, wide, narrow,
):
    join_halves(spot_ref[0], mine, other, full)
    sums_out[...] = jnp.zeros_like(sums_out)
    grads = (full[0:D, 0:D], fin_grad[...])
    fin_mo[...], fin_vo[...], fin_u[...] = lamb_stack(fin_w, fin_m, fin_v, grads, wide, sums_out, 4)
    grads = [full[FF_ROWS + j * PAD : FF_ROWS + j * PAD + HD, 0:D] for j in range(2)]
    cin_mo[...], cin_vo[...], cin_u[...] = lamb_stack(
        cin_w, cin_m, cin_v, grads, narrow, sums_out, 8
    )


def lamb_attn_kernel(
    share, spot_ref, mine, other, vec, bsums, pick, attn_w, attn_m, attn_v, depth_w, depth_m, depth_v,
    norm_w, norm_m, norm_v, bn_w, bn_m, bn_v, table_w, table_m, table_v,
    attn_mo, attn_vo, out_vo, attn_u, depth_wo, depth_mo, depth_vo, norm_wo, norm_mo, norm_vo,
    bn_wo, bn_mo, bn_vo, table_wo, table_mo, table_vo, sums_out, full, stacked,
):
    join_halves(spot_ref[0], mine, other, full)
    sums_out[...] = jnp.zeros_like(sums_out)
    grads = [full[j * PAD : j * PAD + HD, 0:D] for j in range(4)]
    first_new, second_new, direction = lamb_stack(
        attn_w, attn_m, attn_v, grads, stacked, sums_out, 0
    )
    attn_mo[...] = first_new
    attn_u[...] = direction
    for j in range(3):
        attn_vo[j] = second_new[:, j, :]
    out_vo[...] = second_new[:, 3, :]

    own = depth_w[...]
    depth_mo[...], depth_vo[...], direction = adam_step(depth_m[...], depth_v[...], vec[0:KERNEL, :])
    direction = direction + WEIGHT_DECAY * own
    own_norm = jnp.sqrt(total_of(own * own))
    step_norm = jnp.sqrt(total_of(direction * direction))
    depth_wo[...] = own - RATE_MATRIX * (own_norm / step_norm) * direction
    put_squares(sums_out, 11, own, direction)
    for row in (11, 27):
        sums_out[row : row + 1, :] = sums_out[row : row + 1, :] * share

    def vector(weight, first, second, grad, w_out, m_out, v_out):
        m_out[...], v_out[...], move = adam_step(first[...], second[...], grad)
        w_out[...] = weight[...] - RATE_VECTOR * move

    one = full[HD + RATES : HD + RATES + 2, 0:D]
    rows = [one[0:1]] + [vec[32 + 2 * i : 33 + 2 * i, :] for i in range(3)]
    rows += [one[1:2]] + [vec[33 + 2 * i : 34 + 2 * i, :] for i in range(3)]
    vector(norm_w, norm_m, norm_v, jnp.concatenate(rows, axis=0), norm_wo, norm_mo, norm_vo)
    bn_grad = lax.dot_general(
        bsums[...], pick[...], (((1,), (0,)), ((), ())), precision=PRECISE,
        preferred_element_type=F32,
    )
    vector(bn_w, bn_m, bn_v, bn_grad, bn_wo, bn_mo, bn_vo)
    table_grad = full[HD : HD + RATES, 0:D]
    vector(table_w, table_m, table_v, table_grad, table_wo, table_mo, table_vo)


def step_kernel(sums, *refs):
    weights, moves_in, outs, norm_outs = refs[:5], refs[5:10], refs[10:15], refs[15:17]
    moves, sems = refs[17:22], refs[22]
    copies = Copies(sems)
    loads = [copies.start(moves_in[i], moves[i]) for i in range(5)]
    norms = jnp.sqrt(sums[...])
    factor = RATE_MATRIX * (norms[0:16] / jnp.maximum(norms[16:32], 1e-37))
    shape = (16, 128)
    diagonal = lax.broadcasted_iota(jnp.int32, shape, 0) == lax.broadcasted_iota(jnp.int32, shape, 1)
    for i, out in enumerate(norm_outs):
        across = jnp.where(diagonal, norms[16 * i : 16 * i + 16], 0.0)
        out[...] = jnp.sum(across, axis=0, keepdims=True)[:, 0:12]
    for i, row in enumerate((4, 6, 0, 8, 10)):
        weight, move = weights[i], moves[i]
        stacked = len(weight.shape) == 3
        number = weight.shape[1] if stacked else 1
        loads[i].wait()
        scale = factor[row : row + number, 0:1]
        move[...] = weight[...] - (scale[None] if stacked else scale) * move[...]
        copies.out(move, outs[i])
    copies.finish()


SMEM = pl.BlockSpec(memory_space=pltpu.SMEM)


def whole(shape):
    return pl.BlockSpec(shape, lambda *_: (0,) * len(shape))


def lead(shape, rest, place=None):
    def index(i):
        return ((i if place is None else place(i)),) + (0,) * rest

    return pl.BlockSpec(shape, index)


def placed(entries, pinned):
    return [
        pltpu.HBM(*entry) if place in pinned else jax.ShapeDtypeStruct(*entry)
        for place, entry in enumerate(entries)
    ]


def call(kernel, grid, in_specs, out_specs, out_shape, scratch=(), cost=1_000_000, limit=40, pinned=()):
    return pl.pallas_call(
        kernel,
        grid=(grid,),
        in_specs=in_specs,
        out_specs=out_specs,
        out_shape=placed(out_shape, pinned),
        scratch_shapes=list(scratch),
        cost_estimate=pl.CostEstimate(flops=cost, bytes_accessed=cost // 1000, transcendentals=0),
        compiler_params=pltpu.CompilerParams(vmem_limit_bytes=limit * 1024 * 1024),
    )


def call_whole(kernel, scalars, arrays, out_shape, scratch=(), limit=14):
    return pl.pallas_call(
        kernel,
        in_specs=[SMEM] * len(scalars) + [pl.BlockSpec(memory_space=pltpu.VMEM)] * len(arrays),
        out_specs=[pl.BlockSpec(memory_space=pltpu.VMEM)] * len(out_shape),
        out_shape=[jax.ShapeDtypeStruct(*entry) for entry in out_shape],
        scratch_shapes=list(scratch),
        cost_estimate=pl.CostEstimate(flops=1_000_000, bytes_accessed=2_000_000, transcendentals=0),
        compiler_params=pltpu.CompilerParams(vmem_limit_bytes=limit * 1024 * 1024),
    )(*scalars, *arrays)


ANY = pl.BlockSpec(memory_space=pl.ANY)
VMEM = pl.BlockSpec(memory_space=pltpu.VMEM)


def call_mixed(kernel, scalars, small, large, large_out, small_out, scratch, copies, cost, limit=56, pinned=()):
    return pl.pallas_call(
        kernel,
        in_specs=[SMEM] * len(scalars) + [VMEM] * len(small) + [ANY] * len(large),
        out_specs=[ANY] * len(large_out) + [VMEM] * len(small_out),
        out_shape=placed(large_out + small_out, pinned),
        scratch_shapes=[pltpu.VMEM(*entry) for entry in scratch] + [pltpu.SemaphoreType.DMA((copies,))],
        cost_estimate=pl.CostEstimate(flops=cost, bytes_accessed=cost // 1000, transcendentals=0),
        compiler_params=pltpu.CompilerParams(vmem_limit_bytes=limit * 1024 * 1024),
    )(*scalars, *small, *large)


def swap(value, axis, bit):
    size = lax.axis_size(axis)
    return lax.ppermute(value, axis, [(i, i ^ bit) for i in range(size)])


def combine_all(value, merge, pause=None):
    def over(value, axis, bits):
        if len(bits) == 1:
            return merge(value, swap(value, axis, bits[0]))
        one, two = bits
        others = [swap(value, axis, bit) for bit in (one, two, one ^ two)]
        return merge(merge(value, others[0]), merge(others[1], others[2]))

    def axis_sum(value, axis):
        bits = bits_of(axis)
        first = len(bits) % 2
        if first:
            value = over(value, axis, bits[:1])
        for i in range(first, len(bits), 2):
            value = over(value, axis, bits[i : i + 2])
        return value

    value = axis_sum(value, "tensor")
    if pause is not None:
        value = pause(value)
    return axis_sum(value, "dp")


def bits_of(axis):
    size = lax.axis_size(axis)
    assert size & (size - 1) == 0
    return [1 << i for i in range(size.bit_length() - 1)]


def tie(*values):
    return lax.optimization_barrier(values)


def gather_tensor(shard):
    return gather_near(gather_far(shard))


def gather_far(shard):
    return shard, swap(shard, "tensor", 2)


def gather_near(parts):
    blocks = [parts[0], swap(parts[0], "tensor", 1), parts[1], swap(parts[1], "tensor", 1)]
    return [pltpu.with_memory_space_constraint(block, pltpu.HBM) for block in blocks]


def add_low(one, two):
    return (one.astype(F32) + two.astype(F32)).astype(BF16)


def vanish(value):
    return jnp.minimum(jnp.abs(value[0, 0].astype(F32)), 0.0)


def put_after(array, value):
    return (array.astype(F32) + vanish(value)).astype(array.dtype)


def dp_steps(mine, got, first=0, count=None, fold=False, after=None):
    spot = lax.axis_index("dp") & 1
    half = (mine.shape[0] - first if count is None else count) // 2
    if after is not None:
        got = put_after(got, after)

    def cut(array, place):
        return lax.dynamic_slice_in_dim(array, first + place * half, half, 0)

    kept = add_low(cut(mine, spot), cut(got, spot))
    got = yield swap(add_low(cut(mine, 1 - spot), cut(got, 1 - spot)), "dp", 1)
    bits = bits_of("dp")[1:]
    if fold:
        zed = lax.axis_index("dp") // 2 & 1
        part = half // 2

        def cut_again(array, place):
            return lax.dynamic_slice_in_dim(array, place * part, part, 0)

        mine = add_low(cut_again(kept, zed), cut_again(got, zed))
        got = yield swap(add_low(cut_again(kept, 1 - zed), cut_again(got, 1 - zed)), "dp", bits[0])
        kept = add_low(mine, got)
        for bit in bits[1:]:
            got = yield swap(kept, "dp", bit)
            kept = add_low(kept, got)
        got = yield swap(kept, "dp", bits[0])
        kept = jnp.where(zed == 0, jnp.concatenate([kept, got]), jnp.concatenate([got, kept]))
    else:
        kept = add_low(kept, got)
        for bit in bits:
            got = yield swap(kept, "dp", bit)
            kept = add_low(kept, got)
    got = yield swap(kept, "dp", 1)
    return kept, got


def tensor_steps(send, keep):
    got = yield swap(send, "tensor", 1)
    mine = add_low(keep[0], got[0])
    got = yield swap(add_low(keep[1], got[1]), "tensor", 2)
    return mine, got


def reduce_steps(send, keep, fold=False):
    mine, got = yield from tensor_steps(send, keep)
    return (yield from dp_steps(mine, got, fold=fold))


class Reduction:
    def __init__(self, steps):
        self.steps = steps
        self.flight = next(steps)
        self.result = None

    def advance(self, value, after=None):
        if self.result is not None:
            return value
        value, got = tie(value, self.flight)
        if after is not None:
            got = put_after(got, after)
        self.send(got)
        return value

    def send(self, got):
        self.last = got
        try:
            self.flight = self.steps.send(got)
        except StopIteration as end:
            self.result = end.value

    def finish(self):
        while self.result is None:
            self.send(self.flight)
        return self.result


def pick_matrix():
    pick = np.zeros((WIDE, D), np.float32)
    for column in range(D):
        pick[column // HD * PAD + column % HD, column] = 1.0
    return pick


def body(
    frames, cotangent, lengths, rate_kind, attn_w, attn_m, attn_v, ffin_w, ffin_m, ffin_v,
    ffout_w, ffout_m, ffout_v, convin_w, convin_m, convin_v, convout_w, convout_m, convout_v,
    depth_w, depth_m, depth_v, norm_w, norm_m, norm_v, bn_w, bn_m, bn_v, table_w, table_m, table_v,
):
    rank = lax.axis_index("tensor")
    rank_one = rank.reshape(1).astype(jnp.int32)
    spot_one = (lax.axis_index("dp") & 1).reshape(1).astype(jnp.int32)
    rows = frames.shape[0]
    utts = rows // SLOT
    groups = lax.axis_size("tensor")
    hid = ffin_w.shape[2]
    pick = jnp.asarray(pick_matrix(), BF16)
    pick_wide = jnp.asarray(pick_matrix(), F32)

    attn_w, attn_m, attn_v = (jnp.transpose(a, (2, 0, 1)) for a in (attn_w, attn_m, attn_v))
    ffin_w, ffin_m, ffin_v = (jnp.transpose(a, (1, 0, 2)) for a in (ffin_w, ffin_m, ffin_v))
    ffout_w, ffout_m, ffout_v = (jnp.transpose(a, (1, 0, 2)) for a in (ffout_w, ffout_m, ffout_v))
    convin_w, convin_m, convin_v = (jnp.transpose(a, (2, 0, 1)) for a in (convin_w, convin_m, convin_v))

    pack_one_rows = TAIL + CONV_IN_ROWS
    pack_two_rows = TAIL + PAD
    attn_pack = ((4 * PAD, WIDE), BF16)
    (attn_low,) = call_mixed(
        attn_pack_kernel,
        (),
        (),
        (attn_w,),
        [attn_pack],
        [],
        [(attn_w.shape, F32), attn_pack],
        2,
        1_000,
    )
    shards = (ffin_w, ffout_w, convin_w, convout_w)
    packs = [((count, WIDE), BF16) for count in (pack_one_rows, pack_two_rows)]
    attn_low, depth_early = tie(attn_low, depth_w)
    pack_one, pack_two, chan = call_mixed(
        rest_pack_kernel,
        (),
        (depth_early, bn_w, pick_wide),
        shards,
        packs,
        [((34, 8, WIDE), F32)],
        [(shard.shape, F32) for shard in shards] + packs,
        6,
        1_000,
    )
    attn_parts = gather_tensor(attn_low)
    attn_parts[2], pack_one = tie(attn_parts[2], pack_one)
    one_pair = gather_far(pack_one)

    rowspec = lead((SLOT, D), 1)
    chanspec = lead((SLOT, WIDE), 1)
    onespec = lead((SLOT, 1), 1)
    normspec = whole((8, D))
    allspec = whole((rows, D))
    turnspec = whole((D, rows))
    statspec = whole((3, WIDE))
    attn_specs = [whole((4 * PAD, WIDE))] * groups
    qkvspec = pl.BlockSpec((None, HEADS, 3 * PAD, SLOT), lambda i: (i, 0, 0, 0))
    mixspec = pl.BlockSpec((None, WIDE, SLOT), lambda i: (i, 0, 0))
    probspec = pl.BlockSpec((None, HEADS, SLOT, SLOT), lambda i: (i, 0, 0, 0))
    row_f32 = ((rows, D), F32)
    one_f32 = ((rows, 1), F32)
    sums_f32 = ((8, D), F32)
    base_low, qkv, probs, mixed, n1, s1, wout = call(
        attn_fwd_kernel,
        utts,
        [SMEM, SMEM, SMEM, turnspec, whole((RATES, D))] + attn_specs + [whole((WIDE, D)), normspec],
        [rowspec, qkvspec, probspec, mixspec, rowspec, onespec, whole((WIDE, D))],
        [
            ((rows, D), BF16),
            ((utts, HEADS, 3 * PAD, SLOT), BF16),
            ((utts, HEADS, SLOT, SLOT), BF16),
            ((utts, WIDE, SLOT), BF16),
            row_f32,
            one_f32,
            ((WIDE, D), BF16),
        ],
        [pltpu.VMEM((rows, D), BF16), pltpu.VMEM((HEADS, 4 * PAD, D), BF16)],
        cost=1_000,
        limit=56,
        pinned=range(6),
    )(rank_one, lengths, rate_kind, frames.T, table_w, *attn_parts, pick, norm_w)

    row_low = ((rows, D), BF16)
    turn_low = ((D, rows), BF16)
    hid_low = ((groups, rows, hid), BF16)
    chan_f32 = ((rows, WIDE), F32)
    one_rows = (groups, pack_one_rows, WIDE)
    two_rows = (groups, pack_two_rows, WIDE)
    conv_pad = ((8, SPAN, WIDE), F32)
    far, pack_two, n1 = tie(one_pair[1], pack_two, n1)
    one_parts = gather_near((one_pair[0], far))
    two_pair = gather_far(pack_two)
    hid_one, slope_one, n2, s2, value_pre, gate_sig, conv, stat = call_mixed(
        lower_fwd_kernel,
        (rank_one, lengths),
        (norm_w, chan),
        (n1, *one_parts),
        [hid_low, hid_low, row_f32, one_f32, chan_f32, chan_f32, chan_f32],
        [((3, WIDE), F32)],
        [
            row_f32, (one_rows, BF16), hid_low, hid_low, row_f32, one_f32, chan_f32, chan_f32, chan_f32,
            ((HEADS, CONV_IN_ROWS, D), BF16), conv_pad, row_f32, row_low,
        ],
        24,
        1_000,
        pinned=(2, 3),
    )

    far, stat = tie(two_pair[1], stat)
    two_parts = gather_near((two_pair[0], far))
    stat = combine_all(stat, merge_stats)

    out, grad_three, b_grad, send_one, keep_one, bsums, sums_three, sums_four = call_mixed(
        upper_kernel,
        (rank_one, lengths),
        (norm_w, chan, stat),
        (conv, n2, cotangent.T, *two_parts),
        [turn_low, row_f32, chan_f32] + [((groups // 2, pack_two_rows, WIDE), BF16)] * 2,
        [((2, WIDE), F32), sums_f32, sums_f32],
        [
            chan_f32, row_f32, turn_low, (two_rows, BF16), ((HEADS, PAD, D), BF16),
            ((rows, WIDE), BF16), hid_low, hid_low, row_f32, row_f32, one_f32, row_low, turn_low,
            row_low, turn_low, turn_low, chan_f32, (two_rows, BF16), ((WIDE, D), F32),
        ],
        20,
        1_000,
    )
    reduce_one = Reduction(reduce_steps(send_one, keep_one))
    bsums = combine_all(bsums, jnp.add, reduce_one.advance)

    convin_block = (HEADS, CONV_IN_ROWS, D)
    grad_two, cin_grad, vectors = call_mixed(
        conv_bwd_kernel,
        (rank_one, lengths),
        (norm_w, chan, stat, bsums, pick, sums_three, sums_four),
        (b_grad, conv, value_pre, gate_sig, n2, s2, grad_three, *one_parts),
        [row_f32],
        [(convin_block, BF16), ((VECTOR_ROWS, D), BF16)],
        [
            chan_f32, chan_f32, chan_f32, chan_f32, row_f32, one_f32, row_f32,
            ((HEADS, CONV_IN_ROWS, WIDE), BF16), (convin_block, BF16), conv_pad, conv_pad,
            ((SLOT, WIDE), F32), ((SLOT, WIDE), F32), ((2, WIDE, D), F32), ((KERNEL, 8, WIDE), F32),
            sums_f32,
        ],
        16,
        14_000_000_000,
        pinned=(0,),
    )
    grad_two = reduce_one.advance(grad_two)

    lower_rows = (groups, LOWER_ROWS, WIDE)
    pre_one, send_two, keep_two = call_mixed(
        lower_weights_kernel,
        (),
        (norm_w, cin_grad, vectors),
        (grad_two, n1, *one_parts, hid_one, slope_one),
        [hid_low] + [((groups // 2, LOWER_ROWS, WIDE), BF16)] * 2,
        [],
        [
            row_f32, row_f32, ((groups, TAIL, WIDE), BF16), hid_low, hid_low, row_low, turn_low,
            turn_low, (lower_rows, BF16),
        ],
        24,
        12_000_000_000,
    )
    reduce_two = Reduction(tensor_steps(send_two, keep_two))
    pre_one = reduce_one.advance(pre_one)
    grad_one, sums_one = call_mixed(
        lower_bwd_kernel,
        (),
        (norm_w,),
        (grad_two, n1, s1, *one_parts, pre_one),
        [row_f32],
        [sums_f32],
        [row_f32, row_f32, one_f32, ((groups, FF_ROWS, WIDE), BF16), hid_low],
        12,
        8_000_000_000,
    )
    grad_one = reduce_one.advance(grad_one)
    grad_one = reduce_two.advance(grad_one)
    in_grad, attn_send, attn_keep = call(
        attn_bwd_kernel,
        utts,
        [SMEM, SMEM, rowspec] + attn_specs + [whole((WIDE, D)), whole((WIDE, D))]
        + [qkvspec, probspec, mixspec, rowspec, whole((8, D))],
        [turnspec, whole((2, 4 * PAD, WIDE)), whole((2, 4 * PAD, WIDE))],
        [((D, rows), F32)] + [((2, 4 * PAD, WIDE), BF16)] * 2,
        [
            pltpu.VMEM((HEADS, 3 * PAD, D), F32),
            pltpu.VMEM((WIDE, D), F32),
            pltpu.VMEM((rows, D), F32),
            pltpu.VMEM((8, D), F32),
            pltpu.VMEM((HEADS, 3 * PAD, D), BF16),
        ],
        cost=16_000_000_000,
    )(
        rank_one, rate_kind, base_low, *attn_parts, wout, pick, qkv, probs, mixed, grad_one, sums_one,
    )
    attn_send = reduce_two.advance(attn_send)
    mine, got = reduce_two.result
    reduce_attn = Reduction(reduce_steps(attn_send, attn_keep, FOLD[0]))
    reduce_down = Reduction(dp_steps(mine, got, 0, LOWER_SPLIT, FOLD[1]))
    token = reduce_attn.advance(bsums)
    token = reduce_down.advance(token)
    reduce_up = Reduction(dp_steps(mine, got, LOWER_SPLIT, None, FOLD[2], reduce_down.last))
    token = reduce_up.advance(token)
    token = reduce_one.advance(token, reduce_up.last)
    for chain in (reduce_down, reduce_attn, reduce_up, reduce_down, reduce_attn, reduce_up, reduce_down):
        token = chain.advance(token)
    one_halves = reduce_one.finish()
    down_halves = reduce_down.finish()

    def like(*arrays):
        return [(a.shape, F32) for a in arrays]

    down = call_whole(
        lamb_down_kernel,
        (spot_one,),
        (*one_halves, *down_halves, ffout_w, ffout_m, ffout_v, convout_w, convout_m, convout_v),
        like(*[ffout_w] * 3, *[convout_w] * 3)
        + [((D, D), F32), ((VECTOR_ROWS, D), F32), ((32, 128), F32)],
        [
            pltpu.VMEM((pack_two_rows, WIDE), F32),
            pltpu.VMEM((LOWER_SPLIT, WIDE), F32),
            pltpu.VMEM(ffout_w.shape, F32),
        ],
    )
    token = reduce_attn.advance(token)
    token = reduce_attn.advance(token, down[8])
    up_halves = reduce_up.finish()
    attn_halves = reduce_attn.finish()
    up = call_whole(
        lamb_up_kernel,
        (spot_one,),
        (*up_halves, down[6], ffin_w, ffin_m, ffin_v, convin_w, convin_m, convin_v),
        like(*[ffin_w] * 3, *[convin_w] * 3) + [((32, 128), F32)],
        [
            pltpu.VMEM((LOWER_ROWS - LOWER_SPLIT, WIDE), F32),
            pltpu.VMEM(ffin_w.shape, F32),
            pltpu.VMEM(convin_w.shape, F32),
        ],
    )
    small = (depth_w, depth_m, depth_v, norm_w, norm_m, norm_v, bn_w, bn_m, bn_v, table_w, table_m, table_v)
    last = call_whole(
        functools.partial(lamb_attn_kernel, 1.0 / groups),
        (spot_one,),
        (*attn_halves, down[7], bsums, pick_wide, attn_w, attn_m, attn_v) + small,
        like(attn_w) + [((3, HD, D), F32), ((HD, D), F32)] + like(attn_w, *small) + [((32, 128), F32)],
        [pltpu.VMEM((4 * PAD, WIDE), F32), pltpu.VMEM(attn_w.shape, F32)],
    )
    squares = down[8] + up[6] + last[16]
    for bit in bits_of("tensor"):
        squares = squares + swap(squares, "tensor", bit)
    matrices = (ffin_w, ffout_w, attn_w, convin_w, convout_w)
    moves = (up[2], down[2], last[3], up[5], down[5])
    ffin_new, ffout_new, attn_new, convin_new, convout_new, weight_norms, update_norms = call_mixed(
        step_kernel,
        (),
        (squares, *matrices),
        moves,
        like(*matrices),
        [((1, 12), F32)] * 2,
        like(*matrices),
        10,
        1_000_000,
        limit=14,
    )

    def back_chan(array):
        return jnp.transpose(array, (1, 2, 0))

    def back_mid(array):
        return jnp.transpose(array, (1, 0, 2))

    small_new = last[4:16]
    return (
        out.T,
        in_grad.T,
        back_chan(attn_new),
        back_chan(last[0]),
        jnp.transpose(last[1], (0, 2, 1)),
        last[2].T,
        back_mid(ffin_new),
        back_mid(up[0]),
        back_mid(up[1]),
        back_mid(ffout_new),
        back_mid(down[0]),
        back_mid(down[1]),
        back_chan(convin_new),
        back_chan(up[3]),
        back_chan(up[4]),
        convout_new,
        down[3],
        down[4],
        *small_new,
        weight_norms.reshape(12),
        update_norms.reshape(12),
    )


def solution(mesh):
    rows = P(("dp", "tensor"), None)
    last = P(None, None, "tensor")
    mid = P(None, "tensor", None)
    first = P("tensor", None)
    placed = (rows, rows, P("dp"), P("dp")) + (last,) * 6 + (mid,) * 3 + (last,) * 3 + (first,) * 3
    results = (rows, rows) + (last,) * 3 + (P(None, "tensor"),) + (last,) * 3 + (mid,) * 3
    return jax.shard_map(
        body,
        mesh=mesh,
        in_specs=placed + (P(),) * 12,
        out_specs=results + (last,) * 3 + (first,) * 3 + (P(),) * 14,
        check_vma=False,
    )
```
